32 devices in a mesh: page: 8 (over z, y), seq: 4 (over x, core).
Axes of the slice: x: 2, y: 2, z: 4, core: 2. Of those that a mesh axis runs over, the one named last changes fastest.
Arguments:
- tokens: bfloat16 [8, 512, 1024], P('page', 'seq'), may hold values from -6 to 6
- memory: bfloat16 [8, 512, 1024], P('page', 'seq'), may hold values from -6 to 6
- cotangent: bfloat16 [8, 512, 1024], P('page', 'seq'), may hold values from -6 to 6
- self_qkv: bfloat16 [3, 1024, 1024], P(None, 'page', 'seq'), may hold values from -0.1875 to 0.1875
- self_out: bfloat16 [1024, 1024], P('page', 'seq'), may hold values from -1.5 to 1.5
- cross_qkv: bfloat16 [3, 1024, 1024], P(None, 'page', 'seq'), may hold values from -0.1875 to 0.1875
- cross_out: bfloat16 [1024, 1024], P('page', 'seq'), may hold values from -1.5 to 1.5
- up_weight: bfloat16 [1024, 4096], P('page', 'seq'), may hold values from -0.1875 to 0.1875
- down_weight: bfloat16 [4096, 1024], P('page', 'seq'), may hold values from -0.09375 to 0.09375
- norm_gains: bfloat16 [3, 1024], P(None, ('page', 'seq')), may hold values from 0.099609375 to 1.8984375
- norm_biases: bfloat16 [3, 1024], P(None, ('page', 'seq')), may hold values from -1.796875 to 1.796875
- token_counts: int32 [8], P('page'), may hold values from 256 to 512, as said below
- patch_counts: int32 [8], P('page'), may hold values from 128 to 512, as said below
Outputs:
- mixed: bfloat16 [8, 512, 1024], P('page', 'seq')
- input_grad: float32 [8, 512, 1024], P('page', 'seq')
- memory_grad: float32 [8, 512, 1024], P('page', 'seq')
- self_qkv_grad: float32 [3, 1024, 1024], P(None, 'page', 'seq')
- self_out_grad: float32 [1024, 1024], P('page', 'seq')
- cross_qkv_grad: float32 [3, 1024, 1024], P(None, 'page', 'seq')
- cross_out_grad: float32 [1024, 1024], P('page', 'seq')
- up_grad: float32 [1024, 4096], P('page', 'seq')
- down_grad: float32 [4096, 1024], P('page', 'seq')
- norm_gains_grad: float32 [3, 1024], P(None, ('page', 'seq'))
- norm_biases_grad: float32 [3, 1024], P(None, ('page', 'seq'))
The draws below stay inside these ranges and needn't reach their ends.
Inputs may be any that keep to these rules, and one draw needn't show every extreme that they name: `token_counts`: some page has exactly 512 live tokens; a page with 512 live tokens has 512 live patches. Live tokens and patches are the first ones of a page. `patch_counts`: some page has exactly 512 live patches.
All inputs are finite; a program needn't handle non-finite values.
Results may differ from the reference program's by a relative error of at most 0.03.
Values may be sent and summed in bfloat16 or wider, within the bound.
A program may use at most 256 MiB of HBM per device.

```python
import jax
import jax.numpy as jnp
from jax import lax

HEADS = 16
HEAD_DIM = 64
D = 1024
FF = 4096
PAGES = 8
LENGTH = 512
PATCHES = 512


def page_lengths(key):
    long_draw = jax.random.randint(jax.random.fold_in(key, 1), (PAGES,), 0, 4, dtype=jnp.int32)
    chosen = jax.random.randint(jax.random.fold_in(key, 2), (), 0, PAGES, dtype=jnp.int32)
    is_long = (long_draw == 0) | (jnp.arange(PAGES, dtype=jnp.int32) == chosen)
    short_tokens = jax.random.randint(jax.random.fold_in(key, 3), (PAGES,), LENGTH // 2, 3 * LENGTH // 4 + 1, dtype=jnp.int32)
    short_patches = jax.random.randint(jax.random.fold_in(key, 4), (PAGES,), PATCHES // 4, PATCHES // 2 + 1, dtype=jnp.int32)
    token_live = jnp.where(is_long, LENGTH, short_tokens).astype(jnp.int32)
    patch_live = jnp.where(is_long, PATCHES, short_patches).astype(jnp.int32)
    return (token_live, patch_live)


def draw_token_counts(key, part):
    shared = page_lengths(key)
    return shared[0]


def draw_patch_counts(key, part):
    shared = page_lengths(key)
    return shared[1]


def steps_of(rng, shape, pieces, low, top_value):
    loudness = 1.0
    for dim, parts in pieces:
        steps = jax.random.uniform(jax.random.fold_in(jax.random.fold_in(rng, 6), dim), (parts,), jnp.float32, low / len(pieces), top_value / len(pieces))
        loudness = loudness * jnp.repeat(jnp.exp(steps), shape[dim] // parts).reshape((-1,) + (1,) * (len(shape) - 1 - dim))
    return loudness


def bell_draw(rng, extent, width, reach, shards=(), kind=jnp.bfloat16):
    factor_of = steps_of(rng, extent, shards, -0.22, 0.18) if shards else 1.0
    entries = jax.random.normal(rng, extent, jnp.float32) * width * factor_of
    return jnp.minimum(jnp.maximum(entries, -reach), reach).astype(kind)


def setup_inputs(seed: int = 0) -> dict:
    arg_keys = jax.random.split(jax.random.key(seed), 14)
    return {
        "tokens": bell_draw(arg_keys[0], (PAGES, LENGTH, D), 1.0, 6.0, ((0, 8), (1, 4))),
        "memory": bell_draw(arg_keys[1], (PAGES, PATCHES, D), 1.0, 6.0, ((0, 8), (1, 4))),
        "cotangent": bell_draw(arg_keys[2], (PAGES, LENGTH, D), 1.0, 6.0, ((0, 8), (1, 4))),
        "self_qkv": bell_draw(arg_keys[3], (3, D, D), D ** -0.5, 0.1875, ((1, 8), (2, 4))),
        "self_out": bell_draw(arg_keys[4], (D, D), (max(1, D * 8 // LENGTH)) ** -0.5, 1.5, ((0, 8), (1, 4))),
        "cross_qkv": bell_draw(arg_keys[5], (3, D, D), D ** -0.5, 0.1875, ((1, 8), (2, 4))),
        "cross_out": bell_draw(arg_keys[6], (D, D), (max(1, D * 8 // PATCHES)) ** -0.5, 1.5, ((0, 8), (1, 4))),
        "up_weight": bell_draw(arg_keys[7], (D, FF), D ** -0.5, 0.1875, ((0, 8), (1, 4))),
        "down_weight": bell_draw(arg_keys[8], (FF, D), FF ** -0.5, 0.09375, ((0, 8), (1, 4))),
        "norm_gains": jnp.clip(1.0 + 0.18 * jax.random.normal(arg_keys[9], (3, D), jnp.float32), 0.099609375, 1.8984375).astype(jnp.bfloat16),
        "norm_biases": bell_draw(arg_keys[10], (3, D), 0.3, 1.796875, ((1, 32),)),
        "token_counts": draw_token_counts(jax.random.fold_in(arg_keys[13], 71), 0),
        "patch_counts": draw_patch_counts(jax.random.fold_in(arg_keys[13], 71), 0),
    }


@jax.custom_vjp
def low(v):
    return lax.optimization_barrier(v.astype(jnp.bfloat16)).astype(jnp.float32)

@jax.custom_vjp
def low_back(v):
    return v

def low_keep(v):
    return (low(v), None)

def low_pass(kept, grad):
    return (grad,)

def back_keep(v):
    return (v, None)

def back_low(kept, grad):
    return (low(grad),)
low.defvjp(low_keep, low_pass)
low_back.defvjp(back_keep, back_low)

def round_both(values):
    return low(low_back(values))

def project(left, right):
    return jnp.dot(left, right, precision=lax.Precision.HIGHEST, preferred_element_type=jnp.float32)

def layer_norm(values, gain_row, bias_row):
    center = values - lax.optimization_barrier(jnp.mean(values, axis=-1, keepdims=True))
    spread = lax.optimization_barrier(jnp.mean(center * center, axis=-1, keepdims=True))
    return center * lax.rsqrt(spread + 1e-05) * gain_row + bias_row

def attend(query_rows, key_rows, value_rows, live_count, causal):
    total_rows = query_rows.shape[0]
    block_rows = min(512, total_rows)
    block_count = total_rows // block_rows
    key_heads = key_rows.reshape(key_rows.shape[0], HEADS, HEAD_DIM)
    value_heads = value_rows.reshape(value_rows.shape[0], HEADS, HEAD_DIM)
    key_positions = jnp.arange(key_rows.shape[0], dtype=jnp.int32)

    def one_block(entry):
        query_block, block_start = entry
        query_heads = query_block.reshape(block_rows, HEADS, HEAD_DIM)
        scores = jnp.einsum('qhd,khd->hqk', query_heads, key_heads, precision=lax.Precision.HIGHEST)
        scores = low_back(scores * HEAD_DIM ** (-0.5))
        allowed = key_positions[None, :] < live_count
        if causal:
            row_positions = block_start + jnp.arange(block_rows, dtype=jnp.int32)
            allowed = allowed & (key_positions[None, :] <= row_positions[:, None])
        scores = jnp.where(allowed[None], scores, -1e+30)
        highest = lax.optimization_barrier(jnp.max(scores, axis=-1, keepdims=True))
        expon = jnp.exp(scores - highest)
        probabilities = low(expon / lax.optimization_barrier(jnp.sum(expon, axis=-1, keepdims=True)))
        output = jnp.einsum('hqk,khd->qhd', probabilities, value_heads, precision=lax.Precision.HIGHEST)
        return output.reshape(block_rows, HEADS * HEAD_DIM)
    starts = jnp.arange(block_count, dtype=jnp.int32) * block_rows
    blocks = query_rows.reshape(block_count, block_rows, query_rows.shape[1])
    outputs = lax.map(jax.checkpoint(one_block), (blocks, starts))
    return outputs.reshape(total_rows, query_rows.shape[1])

def layer(inputs, memory_rows, self_qkv, self_out, cross_qkv, cross_out, up_weight, down_weight, gains, biases, token_live, patch_live):
    first_low = low(layer_norm(inputs, gains[0], biases[0]))
    queries = round_both(project(first_low, self_qkv[0]))
    key_rows = round_both(project(first_low, self_qkv[1]))
    value_rows = round_both(project(first_low, self_qkv[2]))
    self_attn = round_both(attend(queries, key_rows, value_rows, token_live, True))
    after_self = inputs + low_back(project(self_attn, self_out))
    second_low = low(layer_norm(after_self, gains[1], biases[1]))
    cross_queries = round_both(project(second_low, cross_qkv[0]))
    patch_keys = round_both(project(memory_rows, cross_qkv[1]))
    patch_values = round_both(project(memory_rows, cross_qkv[2]))
    cross_attn = round_both(attend(cross_queries, patch_keys, patch_values, patch_live, False))
    after_cross = after_self + low_back(project(cross_attn, cross_out))
    third_low = low(layer_norm(after_cross, gains[2], biases[2]))
    hidden_pre = low_back(project(third_low, up_weight))
    hidden_low = low(jax.nn.gelu(hidden_pre, approximate=False))
    result = after_cross + low_back(project(hidden_low, down_weight))
    positions = jnp.arange(inputs.shape[0], dtype=jnp.int32)
    return jnp.where((positions < token_live)[:, None], result, 0.0)

def reference(tokens, memory, cotangent, self_qkv, self_out, cross_qkv, cross_out, up_weight, down_weight, norm_gains, norm_biases, token_counts, patch_counts):
    weight_set = tuple((array.astype(jnp.float32) for array in (self_qkv, self_out, cross_qkv, cross_out, up_weight, down_weight, norm_gains, norm_biases)))

    def page_step(totals, page_entry):
        page_tokens, page_memory, page_cot, token_live, patch_live = page_entry

        def forward(inputs, memory_rows, *weights):
            return layer(inputs, memory_rows, *weights, token_live, patch_live)
        output, pull = jax.vjp(forward, page_tokens.astype(jnp.float32), page_memory.astype(jnp.float32), *weight_set)
        gradients = pull(page_cot.astype(jnp.float32))
        totals = tuple((total + grad for total, grad in zip(totals, gradients[2:])))
        return (totals, (output.astype(jnp.bfloat16), gradients[0], gradients[1]))
    zeros = tuple((jnp.zeros_like(weight) for weight in weight_set))
    totals, outputs = lax.scan(page_step, zeros, (tokens, memory, cotangent, token_counts, patch_counts))
    return (outputs[0], outputs[1], outputs[2], totals[0], totals[1], totals[2], totals[3], totals[4], totals[5], totals[6], totals[7])
```

```python
import jax
import jax.numpy as jnp
from jax import lax
from jax.sharding import PartitionSpec as P

HEADS = 16
HEAD_DIM = 64
F32 = jnp.float32
BF16 = jnp.bfloat16


def layer_norm(values, gain_row, bias_row):
    center = values - jnp.mean(values, axis=-1, keepdims=True)
    spread = jnp.mean(center * center, axis=-1, keepdims=True)
    return center * lax.rsqrt(spread + 1e-05) * gain_row + bias_row


def exact_gelu(values):
    return jax.nn.gelu(values, approximate=False)


def dot(left, right, spec):
    return jnp.einsum(spec, left, right, preferred_element_type=F32)


def heads_of(rows):
    return rows.reshape(rows.shape[0], rows.shape[1] // HEAD_DIM, HEAD_DIM)


def probabilities_of(queries, keys, live, causal):
    scores = dot(heads_of(queries), heads_of(keys), "qhd,khd->hqk") * HEAD_DIM ** (-0.5)
    key_at = lax.broadcasted_iota(jnp.int32, scores.shape[1:], 1)
    allowed = key_at < live
    if causal:
        allowed = allowed & (key_at <= lax.broadcasted_iota(jnp.int32, scores.shape[1:], 0))
    scores = jnp.where(allowed[None], scores, -1e30)
    top = jnp.max(scores, axis=-1, keepdims=True)
    raised = jnp.exp(scores - top)
    return raised / jnp.sum(raised, axis=-1, keepdims=True)


def attend(queries, keys, values, live, causal):
    probs = probabilities_of(queries, keys, live, causal)
    out = dot(probs.astype(BF16), heads_of(values), "hqk,khd->qhd")
    return probs, out.reshape(queries.shape).astype(BF16)


def attend_back(probs, queries, keys, values, grad):
    shape = queries.shape
    scale = HEAD_DIM ** (-0.5)
    q, k, v, g = (heads_of(rows) for rows in (queries, keys, values, grad))
    dp = dot(g, v, "qhd,khd->hqk")
    ds = (probs * (dp - jnp.sum(probs * dp, axis=-1, keepdims=True))).astype(BF16)
    dq = (dot(ds, k, "hqk,khd->qhd") * scale).astype(BF16)
    dk = (dot(ds, q, "hqk,qhd->khd") * scale).astype(BF16)
    dv = dot(probs.astype(BF16), g, "hqk,qhd->khd").astype(BF16)
    return dq.reshape(shape), dk.reshape(keys.shape), dv.reshape(keys.shape)


def per_device(
    tokens,
    memory,
    cotangent,
    self_qkv,
    self_out,
    cross_qkv,
    cross_out,
    up_weight,
    down_weight,
    norm_gains,
    norm_biases,
    token_counts,
    patch_counts,
):
    pages = lax.axis_size("page")
    parts = lax.axis_size("seq")
    here = lax.axis_index("seq")
    ratio = pages // parts
    there = [
        (page * parts + part, ((page % ratio) * parts + part) * parts + page // ratio)
        for page in range(pages)
        for part in range(parts)
    ]
    back = [(b, a) for a, b in there]

    def gather_seq(rows):
        return lax.all_gather(rows, "seq", axis=0, tiled=True)

    def scatter_seq(rows):
        return lax.psum_scatter(
            rows.astype(BF16), "seq", scatter_dimension=0, tiled=True
        ).astype(F32)

    norms = lax.all_gather(
        jnp.concatenate([norm_gains, norm_biases]), ("page", "seq"), axis=1, tiled=True
    ).astype(F32)
    gains, biases = norms[:3], norms[3:]
    moved = lax.ppermute(
        jnp.concatenate([self_out, cross_out, down_weight]), ("page", "seq"), there
    )
    small = self_out.shape[0]
    w_self = lax.all_gather(self_qkv, "page", axis=1, tiled=True)
    tokens_all = gather_seq(tokens[0]).astype(F32)
    memory_all = gather_seq(memory[0])

    def rows_of(piece):
        blocks = lax.all_gather(piece, "page", axis=0, tiled=False)
        rows, cols = piece.shape
        blocks = blocks.reshape(ratio, parts, rows, cols).transpose(0, 2, 1, 3)
        return blocks.reshape(ratio * rows, parts * cols)

    def blocks_of(grad):
        rows, cols = grad.shape[0] // ratio, grad.shape[1] // parts
        blocks = grad.reshape(ratio, rows, parts, cols).transpose(0, 2, 1, 3)
        return blocks.reshape(pages, rows, cols).astype(BF16)

    w_self_out = rows_of(moved[:small])
    w_cross = lax.all_gather(cross_qkv, "page", axis=1, tiled=True)
    w_cross_out = rows_of(moved[small : 2 * small])
    w_up = lax.all_gather(up_weight, "page", axis=0, tiled=True)
    w_down = rows_of(moved[2 * small :])
    cotangent_all = gather_seq(cotangent[0])

    token_rows = tokens.shape[1]
    token_live = token_counts[0]
    patch_live = patch_counts[0]
    every = jnp.arange(tokens_all.shape[0], dtype=jnp.int32)
    dyr = jnp.where((every < token_live)[:, None], cotangent_all, jnp.zeros((), BF16))
    mine = here * token_rows + jnp.arange(token_rows, dtype=jnp.int32)
    live_rows = (mine < token_live)[:, None]
    inputs = tokens[0].astype(F32)
    dy = jnp.where(live_rows, cotangent[0].astype(F32), 0.0)

    a1 = layer_norm(tokens_all, gains[0], biases[0]).astype(BF16)
    q, k, v = (dot(a1, w_self[n], "td,de->te").astype(BF16) for n in range(3))
    p, o = attend(q, k, v, token_live, True)
    x1 = inputs + scatter_seq(dot(o, w_self_out, "td,de->te"))
    a2 = gather_seq(layer_norm(x1, gains[1], biases[1]).astype(BF16))
    kc, vc = (dot(memory_all, w_cross[n], "td,de->te").astype(BF16) for n in (1, 2))
    qc = dot(a2, w_cross[0], "td,de->te").astype(BF16)
    pc, oc = attend(qc, kc, vc, patch_live, False)
    x2 = x1 + scatter_seq(dot(oc, w_cross_out, "td,de->te"))
    a3 = gather_seq(layer_norm(x2, gains[2], biases[2]).astype(BF16))
    u = dot(a3, w_up, "td,df->tf")
    g = exact_gelu(u).astype(BF16)
    result = x2 + scatter_seq(dot(g, w_down, "tf,fd->td"))
    mixed = jnp.where(live_rows, result, 0.0).astype(BF16)[None]

    down_grad = dot(g, dyr, "tf,td->fd")
    dg = dot(dyr, w_down, "td,fd->tf")
    du = jax.vjp(exact_gelu, u)[1](dg)[0].astype(BF16)
    up_grad = dot(a3, du, "td,tf->df")
    da3 = scatter_seq(dot(du, w_up, "tf,df->td"))
    dx2, gain_third, bias_third = jax.vjp(layer_norm, x2, gains[2], biases[2])[1](da3)
    dx2 = dy + dx2
    dz2 = gather_seq(dx2.astype(BF16))
    cross_out_grad = dot(oc, dz2, "td,te->de")
    doc = dot(dz2, w_cross_out, "te,de->td").astype(BF16)
    dqc, dkc, dvc = attend_back(pc, qc, kc, vc, doc)
    da2 = scatter_seq(dot(dqc, w_cross[0], "te,de->td"))
    dx1, gain_second, bias_second = jax.vjp(layer_norm, x1, gains[1], biases[1])[1](da2)
    dx1 = dx2 + dx1
    dz1 = gather_seq(dx1.astype(BF16))
    memory_grad = scatter_seq(
        dot(dkc, w_cross[1], "te,de->td") + dot(dvc, w_cross[2], "te,de->td")
    )
    cross_qkv_grad = jnp.stack(
        [
            dot(a2, dqc, "td,te->de"),
            dot(memory_all, dkc, "td,te->de"),
            dot(memory_all, dvc, "td,te->de"),
        ]
    )
    self_out_grad = dot(o, dz1, "td,te->de")
    dor = dot(dz1, w_self_out, "te,de->td").astype(BF16)
    dq, dk, dv = attend_back(p, q, k, v, dor)
    da1 = scatter_seq(
        dot(dq, w_self[0], "te,de->td")
        + dot(dk, w_self[1], "te,de->td")
        + dot(dv, w_self[2], "te,de->td")
    )
    self_qkv_grad = jnp.stack(
        [dot(a1, dq, "td,te->de"), dot(a1, dk, "td,te->de"), dot(a1, dv, "td,te->de")]
    )
    dx, gain_first, bias_first = jax.vjp(layer_norm, inputs, gains[0], biases[0])[1](da1)
    input_grad = (dx1 + dx)[None]

    def sum_pages(grad, axis):
        return lax.psum_scatter(grad.astype(BF16), "page", scatter_dimension=axis, tiled=True)

    def sum_blocks(grad):
        return lax.psum_scatter(blocks_of(grad), "page", scatter_dimension=0, tiled=False)

    up_out = sum_pages(up_grad, 0).astype(F32)
    down_part = sum_blocks(down_grad)
    cross_out_part = sum_blocks(cross_out_grad)
    cross_out_qkv = sum_pages(cross_qkv_grad, 1).astype(F32)
    self_out_part = sum_blocks(self_out_grad)
    self_out_qkv = sum_pages(self_qkv_grad, 1).astype(F32)
    returned = lax.ppermute(
        jnp.concatenate([self_out_part, cross_out_part, down_part]), ("page", "seq"), back
    ).astype(F32)
    norm_sums = lax.psum_scatter(
        jnp.stack([gain_first, gain_second, gain_third, bias_first, bias_second, bias_third]),
        ("page", "seq"),
        scatter_dimension=1,
        tiled=True,
    )
    return (
        mixed,
        input_grad,
        memory_grad[None],
        self_out_qkv,
        returned[:small],
        cross_out_qkv,
        returned[small : 2 * small],
        up_out,
        returned[2 * small :],
        norm_sums[:3],
        norm_sums[3:],
    )


def solution(mesh):
    rows = P("page", "seq", None)
    stack = P(None, "page", "seq")
    flat = P("page", "seq")
    norm = P(None, ("page", "seq"))
    counts = P("page")
    return jax.shard_map(
        per_device,
        mesh=mesh,
        in_specs=(rows, rows, rows, stack, flat, stack, flat, flat, flat, norm, norm, counts, counts),
        out_specs=(rows, rows, rows, stack, flat, stack, flat, flat, flat, norm, norm),
        check_vma=False,
    )
```

```python
import functools

import jax
import jax.numpy as jnp
from jax import lax
from jax.experimental import pallas as pl
from jax.experimental.pallas import tpu as pltpu
from jax.sharding import PartitionSpec as P

HEADS = 16
HEAD_DIM = 64
F32 = jnp.float32
BF16 = jnp.bfloat16
MESH = pl.DeviceIdType.MESH
NG = 6


def ag_kernel(A, B, S, spaces, *refs):
    ng = 6
    ins, outs = refs[:ng], refs[ng:2*ng]
    stage = refs[2*ng:2*ng+3]
    local_sem, perm_send, perm_recv, recv, send = refs[2*ng+3:]
    page = lax.axis_index("page"); seq = lax.axis_index("seq")
    a = lax.div(page, B); b = lax.rem(page, B)
    Pn = A*B
    R = Pn // S
    tp, ts = lax.rem(page, R)*S + seq, lax.div(page, R)
    fixed = (tp == page) & (ts == seq)
    sp, ss = ts_src = (seq*R + lax.div(page, S), lax.rem(page, S))
    barrier = pltpu.get_barrier_semaphore()
    def sig(dev):
        pl.semaphore_signal(barrier, inc=1, device_id=dev, device_id_type=MESH)
    @pl.when(a > 0)
    def _(): sig((page - B, seq))
    @pl.when(a < A-1)
    def _(): sig((page + B, seq))
    @pl.when(b > 0)
    def _(): sig((page - 1, seq))
    @pl.when(b < B-1)
    def _(): sig((page + 1, seq))
    @pl.when(jnp.logical_not(fixed))
    def _():
        sig((tp, ts)); sig((sp, ss))
    n = (a > 0).astype(jnp.int32) + (a < A-1).astype(jnp.int32) + (b > 0).astype(jnp.int32) + (b < B-1).astype(jnp.int32) + 2*jnp.logical_not(fixed).astype(jnp.int32)
    pl.semaphore_wait(barrier, n)

    def window(g, j):
        ref = outs[g]
        if g in (0, 2):
            r = ins[g].shape[1]
            return ref.at[:, pl.ds(pl.multiple_of(j*r, r), r), :]
        if g == 4:
            r = ins[g].shape[0]
            return ref.at[pl.ds(pl.multiple_of(j*r, r), r), :]
        r, c = ins[g].shape
        return ref.at[pl.ds(pl.multiple_of(lax.div(j, S)*r, r), r), pl.ds(pl.multiple_of(lax.rem(j, S)*c, c), c)]

    def remote(g, j, way):
        dev = {0: (page - B, seq), 1: (page + B, seq), 2: (page - 1, seq), 3: (page + 1, seq)}[way]
        return pltpu.make_async_remote_copy(src_ref=window(g, j), dst_ref=window(g, j), send_sem=send.at[g, j, way], recv_sem=recv.at[g, j], device_id=dev, device_id_type=MESH)
    def landed(g, j):
        pltpu.make_async_remote_copy(src_ref=window(g, j), dst_ref=window(g, j), send_sem=send.at[g, j, 0], recv_sem=recv.at[g, j], device_id=(page, seq), device_id_type=MESH).wait_recv()

    for i, g in enumerate((1, 3, 5)):
        cp = pltpu.make_async_remote_copy(src_ref=ins[g], dst_ref=stage[i], send_sem=perm_send.at[i], recv_sem=perm_recv.at[i], device_id=(tp, ts), device_id_type=MESH)
        @pl.when(jnp.logical_not(fixed))
        def _(): cp.start()
    own = {}
    for i, g in enumerate((0, 2, 4)):
        own[g] = pltpu.make_async_copy(ins[g], window(g, page), local_sem.at[g])
        own[g].start()
    order = [0, 1, 2, 3, 4, 5]
    def first(g):
        if g in own:
            own[g].wait()
        else:
            i = g//2
            cp = pltpu.make_async_remote_copy(src_ref=ins[g], dst_ref=stage[i], send_sem=perm_send.at[i], recv_sem=perm_recv.at[i], device_id=(tp, ts), device_id_type=MESH)
            @pl.when(jnp.logical_not(fixed))
            def _(): cp.wait()
            @pl.when(fixed)
            def _():
                c2 = pltpu.make_async_copy(ins[g], window(g, page), local_sem.at[g]); c2.start(); c2.wait()
            @pl.when(jnp.logical_not(fixed))
            def _():
                c2 = pltpu.make_async_copy(stage[i], window(g, page), local_sem.at[g]); c2.start(); c2.wait()
        @pl.when(a > 0)
        def _(): remote(g, page, 0).start()
        @pl.when(a < A-1)
        def _(): remote(g, page, 1).start()
        @pl.when(b > 0)
        def _(): remote(g, page, 2).start()
        @pl.when(b < B-1)
        def _(): remote(g, page, 3).start()
    def step_a(g, d):
        @pl.when(a - d >= 0)
        def _():
            j = page - d*B
            landed(g, j)
            @pl.when(a < A-1)
            def _(): remote(g, j, 1).start()
            @pl.when(b > 0)
            def _(): remote(g, j, 2).start()
            @pl.when(b < B-1)
            def _(): remote(g, j, 3).start()
        @pl.when(a + d < A)
        def _():
            j = page + d*B
            landed(g, j)
            @pl.when(a > 0)
            def _(): remote(g, j, 0).start()
            @pl.when(b > 0)
            def _(): remote(g, j, 2).start()
            @pl.when(b < B-1)
            def _(): remote(g, j, 3).start()
    def step_b(g, e):
        for a2 in range(A):
            @pl.when(b - e >= 0)
            def _():
                j = a2*B + b - e
                landed(g, j)
                @pl.when(b < B-1)
                def _(): remote(g, j, 3).start()
            @pl.when(b + e < B)
            def _():
                j = a2*B + b + e
                landed(g, j)
                @pl.when(b > 0)
                def _(): remote(g, j, 2).start()
    first(order[0])
    for i, g in enumerate(order):
        if i + 1 < len(order):
            first(order[i+1])
        for d in range(1, A):
            step_a(g, d)
    for g in order:
        for e in range(1, B):
            step_b(g, e)
    for g in order:
        for a2 in range(A):
            for b2 in range(B):
                j = a2*B + b2
                same = b == b2
                @pl.when(same & (a2 >= a) & (a > 0))
                def _(): remote(g, j, 0).wait_send()
                @pl.when(same & (a2 <= a) & (a < A-1))
                def _(): remote(g, j, 1).wait_send()
                @pl.when((b2 >= b) & (b > 0))
                def _(): remote(g, j, 2).wait_send()
                @pl.when((b2 <= b) & (b < B-1))
                def _(): remote(g, j, 3).wait_send()

def ag(ins, A, B, S, space):
    Pn = A*B; R = Pn//S
    shapes = []
    for g, x in enumerate(ins):
        if g in (0, 2): s = (x.shape[0], x.shape[1]*Pn, x.shape[2])
        elif g == 4: s = (x.shape[0]*Pn, x.shape[1])
        else: s = (x.shape[0]*R, x.shape[1]*S)
        shapes.append(jax.ShapeDtypeStruct(s, x.dtype))
    return pl.pallas_call(
        functools.partial(ag_kernel, A, B, S, space),
        out_shape=shapes,
        in_specs=[pl.BlockSpec(memory_space=space)]*6,
        out_specs=[pl.BlockSpec(memory_space=space)]*6,
        scratch_shapes=[pltpu.VMEM(ins[g].shape, BF16) for g in (1, 3, 5)] + [
            pltpu.SemaphoreType.DMA((6,)), pltpu.SemaphoreType.DMA((3,)), pltpu.SemaphoreType.DMA((3,)),
            pltpu.SemaphoreType.DMA((6, Pn)), pltpu.SemaphoreType.DMA((6, Pn, 4))],
        compiler_params=pltpu.CompilerParams(collective_id=0, has_side_effects=True, vmem_limit_bytes=48*2**20),
    )(*ins)


def window(ref, g, j, S, shard):
    if g in (0, 2):
        r = shard[1]
        return ref.at[:, pl.ds(pl.multiple_of(j*r, r), r), :]
    if g == 4:
        r = shard[0]
        return ref.at[pl.ds(pl.multiple_of(j*r, r), r), :]
    r, c = shard
    return ref.at[pl.ds(pl.multiple_of(lax.div(j, S)*r, r), r), pl.ds(pl.multiple_of(lax.rem(j, S)*c, c), c)]

def rs_kernel(A, B, S, shards, *refs):
    grads, outs = refs[:NG], refs[NG:2*NG]
    rb, zz = refs[2*NG:3*NG], refs[3*NG:4*NG]
    stage = refs[4*NG:4*NG+3]
    ysend, yrecv, zsend, zrecv, psend, precv = refs[4*NG+3:]
    page = lax.axis_index("page"); seq = lax.axis_index("seq")
    a = lax.div(page, B); b = lax.rem(page, B)
    Pn = A*B; R = Pn // S
    op, os_ = seq*R + lax.div(page, S), lax.rem(page, S)
    hp, hs = lax.rem(page, R)*S + seq, lax.div(page, R)
    fixed = (op == page) & (os_ == seq)
    barrier = pltpu.get_barrier_semaphore()
    def sig(dev):
        pl.semaphore_signal(barrier, inc=1, device_id=dev, device_id_type=MESH)
    @pl.when(a > 0)
    def _(): sig((page - B, seq))
    @pl.when(a < A-1)
    def _(): sig((page + B, seq))
    for k in range(1, B):
        sig((a*B + lax.rem(b + k, B), seq))
    @pl.when(jnp.logical_not(fixed))
    def _():
        sig((op, os_)); sig((hp, hs))
    n = (a > 0).astype(jnp.int32) + (a < A-1).astype(jnp.int32) + (B-1) + 2*jnp.logical_not(fixed).astype(jnp.int32)
    pl.semaphore_wait(barrier, n)

    def win(g, j): return window(grads[g], g, j, S, shards[g])
    def ycopy(g, k, t):
        b2 = lax.rem(b + k, B)
        return pltpu.make_async_remote_copy(src_ref=win(g, t*B + b2), dst_ref=rb[g].at[B-1-k, t], send_sem=ysend.at[g, k-1, t], recv_sem=yrecv.at[g, B-1-k, t], device_id=(a*B + b2, seq), device_id_type=MESH)
    def ylanded(g, slot, t):
        pltpu.make_async_remote_copy(src_ref=rb[g].at[slot, t], dst_ref=rb[g].at[slot, t], send_sem=ysend.at[g, 0, t], recv_sem=yrecv.at[g, slot, t], device_id=(page, seq), device_id_type=MESH).wait_recv()
    def zcopy(g, t, sg):
        way = lax.div(sg + 1, 2)
        return pltpu.make_async_remote_copy(src_ref=rb[g].at[0, t], dst_ref=zz[g].at[way, t], send_sem=zsend.at[g, t], recv_sem=zrecv.at[g, way, t], device_id=(page + sg*B, seq), device_id_type=MESH)
    def zlanded(g, t, way):
        pltpu.make_async_remote_copy(src_ref=zz[g].at[way, t], dst_ref=zz[g].at[way, t], send_sem=zsend.at[g, t], recv_sem=zrecv.at[g, way, t], device_id=(page, seq), device_id_type=MESH).wait_recv()
    def ys(g):
        for k in range(1, B):
            for t in range(A):
                ycopy(g, k, t).start()
    def acc(g):
        for t in range(A):
            total = win(g, t*B + b)[...].astype(F32)
            for slot in range(B-1):
                ylanded(g, slot, t)
                total = total + rb[g][slot, t].astype(F32)
            rb[g][0, t] = total.astype(BF16)
    def phase(g, sg):
        up = a - sg
        has = (up >= 0) & (up < A)
        way = lax.div(sg + 1, 2)
        for k in range(A-1, 0, -1):
            t = a + sg*k
            @pl.when((t >= 0) & (t < A))
            def _():
                @pl.when(has)
                def _():
                    zlanded(g, t, way)
                    rb[g][0, t] = (rb[g][0, t].astype(F32) + zz[g][way, t].astype(F32)).astype(BF16)
                zcopy(g, t, sg).start()
    first = jnp.where(2*a < A, 1, -1)
    def final(g):
        for way, has in ((1, a > 0), (0, a < A-1)):
            @pl.when(has)
            def _():
                zlanded(g, a, way)
        total = rb[g][0, a].astype(F32)
        zu = jnp.where(a > 0, zz[g][1, a].astype(F32), 0.0)
        zd = jnp.where(a < A-1, zz[g][0, a].astype(F32), 0.0)
        total = total + zu + zd
        if g in (0, 2, 4):
            outs[g][...] = total
        else:
            i = g//2
            stage[i][0] = total.astype(BF16)
            @pl.when(jnp.logical_not(fixed))
            def _():
                pcopy(i).start()
    def pcopy(i):
        return pltpu.make_async_remote_copy(src_ref=stage[i].at[0], dst_ref=stage[i].at[1], send_sem=psend.at[i], recv_sem=precv.at[i], device_id=(op, os_), device_id_type=MESH)
    order = [5, 4, 3, 2, 1, 0]
    AHEAD = 2
    for i in range(AHEAD): ys(order[i])
    for i in range(NG + 2):
        if i + AHEAD < NG: ys(order[i+AHEAD])
        if i < NG:
            acc(order[i]); phase(order[i], first)
        if 0 <= i-1 < NG:
            phase(order[i-1], -first)
        if 0 <= i-2 < NG:
            final(order[i-2])
    for i, g in enumerate((1, 3, 5)):
        @pl.when(jnp.logical_not(fixed))
        def _():
            pcopy(i).wait()
            outs[g][...] = stage[i][1].astype(F32)
        @pl.when(fixed)
        def _():
            outs[g][...] = stage[i][0].astype(F32)
    for g in range(NG):
        for t in range(A):
            for k in range(1, B):
                ycopy(g, k, t).wait_send()
            @pl.when(t != a)
            def _(): zcopy(g, t, jnp.where(t > a, 1, -1)).wait_send()

def rs(grads, shards, A, B, S):
    V = pltpu.VMEM
    return pl.pallas_call(
        functools.partial(rs_kernel, A, B, S, shards),
        out_shape=[jax.ShapeDtypeStruct(s, F32) for s in shards],
        in_specs=[pl.BlockSpec(memory_space=V)]*NG,
        out_specs=[pl.BlockSpec(memory_space=V)]*NG,
        scratch_shapes=[V((B-1, A, *s), BF16) for s in shards] + [V((2, A, *s), BF16) for s in shards] + [V((2, *shards[g]), BF16) for g in (1, 3, 5)] + [
            pltpu.SemaphoreType.DMA((NG, B-1, A)), pltpu.SemaphoreType.DMA((NG, B-1, A)),
            pltpu.SemaphoreType.DMA((NG, A)), pltpu.SemaphoreType.DMA((NG, 2, A)), pltpu.SemaphoreType.DMA((3,)), pltpu.SemaphoreType.DMA((3,))],
        compiler_params=pltpu.CompilerParams(collective_id=1, has_side_effects=True, vmem_limit_bytes=60*2**20), name="rs",
    )(*grads)


def layer_norm(values, gain_row, bias_row):
    center = values - jnp.mean(values, axis=-1, keepdims=True)
    spread = jnp.mean(center * center, axis=-1, keepdims=True)
    return center * lax.rsqrt(spread + 1e-05) * gain_row + bias_row


def exact_gelu(values):
    return jax.nn.gelu(values, approximate=False)


def dot(left, right, spec):
    return jnp.einsum(spec, left, right, preferred_element_type=F32)


def heads_of(rows):
    return rows.reshape(rows.shape[0], rows.shape[1] // HEAD_DIM, HEAD_DIM)


def probabilities_of(queries, keys, live, causal):
    scores = dot(heads_of(queries), heads_of(keys), "qhd,khd->hqk") * HEAD_DIM ** (-0.5)
    key_at = lax.broadcasted_iota(jnp.int32, scores.shape[1:], 1)
    allowed = key_at < live
    if causal:
        allowed = allowed & (key_at <= lax.broadcasted_iota(jnp.int32, scores.shape[1:], 0))
    scores = jnp.where(allowed[None], scores, -1e30)
    top = jnp.max(scores, axis=-1, keepdims=True)
    raised = jnp.exp(scores - top)
    return raised / jnp.sum(raised, axis=-1, keepdims=True)


def attend(queries, keys, values, live, causal):
    probs = probabilities_of(queries, keys, live, causal)
    out = dot(probs.astype(BF16), heads_of(values), "hqk,khd->qhd")
    return probs, out.reshape(queries.shape).astype(BF16)


def attend_back(probs, queries, keys, values, grad):
    shape = queries.shape
    scale = HEAD_DIM ** (-0.5)
    q, k, v, g = (heads_of(rows) for rows in (queries, keys, values, grad))
    dp = dot(g, v, "qhd,khd->hqk")
    ds = (probs * (dp - jnp.sum(probs * dp, axis=-1, keepdims=True))).astype(BF16)
    dq = (dot(ds, k, "hqk,khd->qhd") * scale).astype(BF16)
    dk = (dot(ds, q, "hqk,qhd->khd") * scale).astype(BF16)
    dv = dot(probs.astype(BF16), g, "hqk,qhd->khd").astype(BF16)
    return dq.reshape(shape), dk.reshape(keys.shape), dv.reshape(keys.shape)


def per_device(
    tokens,
    memory,
    cotangent,
    self_qkv,
    self_out,
    cross_qkv,
    cross_out,
    up_weight,
    down_weight,
    norm_gains,
    norm_biases,
    token_counts,
    patch_counts,
):
    pages = lax.axis_size("page")
    parts = lax.axis_size("seq")
    here = lax.axis_index("seq")
    wide = 2 if pages == 8 else 8
    def gather_seq(rows):
        return lax.all_gather(rows, "seq", axis=0, tiled=True)

    def scatter_seq(rows):
        return lax.psum_scatter(
            rows.astype(BF16), "seq", scatter_dimension=0, tiled=True
        ).astype(F32)

    norms = lax.all_gather(
        jnp.concatenate([norm_gains, norm_biases]), ("page", "seq"), axis=1, tiled=True
    ).astype(F32)
    gains, biases = norms[:3], norms[3:]
    pieces = (self_qkv, self_out, cross_qkv, cross_out, up_weight, down_weight)
    w_self, w_self_out, w_cross, w_cross_out, w_up, w_down = ag(
        pieces, pages // wide, wide, parts, pl.ANY
    )
    tokens_all = gather_seq(tokens[0]).astype(F32)
    memory_all = gather_seq(memory[0])

    cotangent_all = gather_seq(cotangent[0])

    token_rows = tokens.shape[1]
    token_live = token_counts[0]
    patch_live = patch_counts[0]
    every = jnp.arange(tokens_all.shape[0], dtype=jnp.int32)
    dyr = jnp.where((every < token_live)[:, None], cotangent_all, jnp.zeros((), BF16))
    mine = here * token_rows + jnp.arange(token_rows, dtype=jnp.int32)
    live_rows = (mine < token_live)[:, None]
    inputs = tokens[0].astype(F32)
    dy = jnp.where(live_rows, cotangent[0].astype(F32), 0.0)

    a1 = layer_norm(tokens_all, gains[0], biases[0]).astype(BF16)
    q, k, v = (dot(a1, w_self[n], "td,de->te").astype(BF16) for n in range(3))
    p, o = attend(q, k, v, token_live, True)
    x1 = inputs + scatter_seq(dot(o, w_self_out, "td,de->te"))
    a2 = gather_seq(layer_norm(x1, gains[1], biases[1]).astype(BF16))
    kc, vc = (dot(memory_all, w_cross[n], "td,de->te").astype(BF16) for n in (1, 2))
    qc = dot(a2, w_cross[0], "td,de->te").astype(BF16)
    pc, oc = attend(qc, kc, vc, patch_live, False)
    x2 = x1 + scatter_seq(dot(oc, w_cross_out, "td,de->te"))
    a3 = gather_seq(layer_norm(x2, gains[2], biases[2]).astype(BF16))
    u = dot(a3, w_up, "td,df->tf")
    g = exact_gelu(u).astype(BF16)
    result = x2 + scatter_seq(dot(g, w_down, "tf,fd->td"))
    mixed = jnp.where(live_rows, result, 0.0).astype(BF16)[None]

    down_grad = dot(g, dyr, "tf,td->fd")
    dg = dot(dyr, w_down, "td,fd->tf")
    du = jax.vjp(exact_gelu, u)[1](dg)[0].astype(BF16)
    up_grad = dot(a3, du, "td,tf->df")
    da3 = scatter_seq(dot(du, w_up, "tf,df->td"))
    dx2, gain_third, bias_third = jax.vjp(layer_norm, x2, gains[2], biases[2])[1](da3)
    dx2 = dy + dx2
    dz2 = gather_seq(dx2.astype(BF16))
    cross_out_grad = dot(oc, dz2, "td,te->de")
    doc = dot(dz2, w_cross_out, "te,de->td").astype(BF16)
    dqc, dkc, dvc = attend_back(pc, qc, kc, vc, doc)
    da2 = scatter_seq(dot(dqc, w_cross[0], "te,de->td"))
    dx1, gain_second, bias_second = jax.vjp(layer_norm, x1, gains[1], biases[1])[1](da2)
    dx1 = dx2 + dx1
    dz1 = gather_seq(dx1.astype(BF16))
    memory_grad = scatter_seq(
        dot(dkc, w_cross[1], "te,de->td") + dot(dvc, w_cross[2], "te,de->td")
    )
    cross_qkv_grad = jnp.stack(
        [
            dot(a2, dqc, "td,te->de"),
            dot(memory_all, dkc, "td,te->de"),
            dot(memory_all, dvc, "td,te->de"),
        ]
    )
    self_out_grad = dot(o, dz1, "td,te->de")
    dor = dot(dz1, w_self_out, "te,de->td").astype(BF16)
    dq, dk, dv = attend_back(p, q, k, v, dor)
    da1 = scatter_seq(
        dot(dq, w_self[0], "te,de->td")
        + dot(dk, w_self[1], "te,de->td")
        + dot(dv, w_self[2], "te,de->td")
    )
    self_qkv_grad = jnp.stack(
        [dot(a1, dq, "td,te->de"), dot(a1, dk, "td,te->de"), dot(a1, dv, "td,te->de")]
    )
    dx, gain_first, bias_first = jax.vjp(layer_norm, inputs, gains[0], biases[0])[1](da1)
    input_grad = (dx1 + dx)[None]

    grads = (
        self_qkv_grad, self_out_grad, cross_qkv_grad, cross_out_grad, up_grad, down_grad
    )
    sums = rs(
        [grad.astype(BF16) for grad in grads],
        [piece.shape for piece in pieces],
        pages // wide,
        wide,
        parts,
    )
    norm_sums = lax.psum_scatter(
        jnp.stack([gain_first, gain_second, gain_third, bias_first, bias_second, bias_third]),
        ("page", "seq"),
        scatter_dimension=1,
        tiled=True,
    )
    return (
        mixed,
        input_grad,
        memory_grad[None],
        *sums,
        norm_sums[:3],
        norm_sums[3:],
    )


def solution(mesh):
    rows = P("page", "seq", None)
    stack = P(None, "page", "seq")
    flat = P("page", "seq")
    norm = P(None, ("page", "seq"))
    counts = P("page")
    return jax.shard_map(
        per_device,
        mesh=mesh,
        in_specs=(rows, rows, rows, stack, flat, stack, flat, flat, flat, norm, norm, counts, counts),
        out_specs=(rows, rows, rows, stack, flat, stack, flat, flat, flat, norm, norm),
        check_vma=False,
    )
```

```python
import types

import jax
import jax.numpy as jnp
from jax import lax
from jax.experimental import pallas as pl
from jax.experimental.pallas import tpu as pltpu
from jax.sharding import PartitionSpec as P

HEAD_DIM = 64
F32 = jnp.float32
BF16 = jnp.bfloat16
MESH = pl.DeviceIdType.MESH
SELF, SELF_OUT, CROSS, CROSS_OUT, UP, DOWN = range(6)
MOVED = (SELF_OUT, CROSS_OUT, DOWN)
G_TOKENS, G_MEMORY, G_COT, G_A2, G_A3, G_DZ2, G_DZ1 = range(7)
R_CHAIN, R_MIXED, R_MEMORY = range(3)
LANES = 128


def nn(left, right):
    return lax.dot_general(left, right, (((1,), (0,)), ((), ())), preferred_element_type=F32)


def nt(left, right):
    return lax.dot_general(left, right, (((1,), (1,)), ((), ())), preferred_element_type=F32)


def tn(left, right):
    return lax.dot_general(left, right, (((0,), (0,)), ((), ())), preferred_element_type=F32)


def rows_at(start, size):
    return pl.ds(pl.multiple_of(start, size), size)


def normed(values):
    center = values - jnp.mean(values, axis=-1, keepdims=True)
    rate = lax.rsqrt(jnp.mean(center * center, axis=-1, keepdims=True) + 1e-05)
    return center * rate, rate


def gelu_pair(values):
    chance = 0.5 + 0.5 * lax.erf(values * 0.7071067811865476)
    density = jnp.exp(-0.5 * values * values) * 0.3989422804014327
    return values * chance, chance + values * density


def layer_kernel(A, B, S, r):
    r.dz1 = r.a3
    ins, w, grad, rb, zz, outs = r.ins, r.w, r.grad, r.rb, r.zz, r.outs
    stage, back = dict(zip(MOVED, r.stage)), dict(zip(MOVED, r.back))
    page, seq = lax.axis_index("page"), lax.axis_index("seq")
    a, b = lax.div(page, B), lax.rem(page, B)
    R = A * B // S
    Tl, D = r.tokens.shape
    T = Tl * S
    Dl = ins[SELF].shape[2]
    Fl = ins[UP].shape[1]
    own = rows_at(seq * Tl, Tl)
    to_page, to_seq = lax.rem(page, R) * S + seq, lax.div(page, R)
    from_page, from_seq = seq * R + lax.div(page, S), lax.rem(page, S)
    fixed = (to_page == page) & (to_seq == seq)
    moves = jnp.logical_not(fixed)

    def remote(src, dst, send, recv, device):
        return pltpu.make_async_remote_copy(
            src_ref=src, dst_ref=dst, send_sem=send, recv_sem=recv, device_id=device, device_id_type=MESH
        )

    def landed(dst, recv):
        remote(dst, dst, recv, recv, (page, seq)).wait_recv()

    barrier = pltpu.get_barrier_semaphore()

    def greet(device):
        pl.semaphore_signal(barrier, inc=1, device_id=device, device_id_type=MESH)

    for k in range(1, S):
        greet((page, lax.rem(seq + k, S)))
    for k in range(1, B):
        greet((a * B + lax.rem(b + k, B), seq))
    for k in range(1, A):
        greet((lax.rem(a + k, A) * B + b, seq))

    @pl.when(moves)
    def _():
        greet((to_page, to_seq))
        greet((from_page, from_seq))

    pl.semaphore_wait(barrier, S + A + B - 3 + 2 * moves.astype(jnp.int32))

    def ag_copy(i, src, dst, k):
        return remote(
            src, dst.at[own], r.ag_send.at[i, k - 1], r.ag_recv.at[i, seq], (page, lax.rem(seq + k, S))
        )

    def ag_start(i, src, dst):
        for k in range(S - 1, 0, -1):
            ag_copy(i, src, dst, k).start()

    def ag_wait(i, dst):
        for k in range(1, S):
            source = lax.rem(seq + k, S)
            landed(dst.at[rows_at(source * Tl, Tl)], r.ag_recv.at[i, source])

    def ag_sent(i, src, dst):
        for k in range(1, S):
            ag_copy(i, src, dst, k).wait_send()

    def rs_copy(i, k):
        peer = lax.rem(seq + k, S)
        return remote(
            r.part[i].at[rows_at(peer * Tl, Tl)],
            r.got[i].at[k - 1],
            r.rs_send.at[i, k - 1],
            r.rs_recv.at[i, k - 1],
            (page, peer),
        )

    def rs_start(i, term):
        part = r.part[i]
        for k in range(S - 1, -1, -1):
            at = rows_at(lax.rem(seq + k, S) * Tl, Tl)
            part[at, :] = term(at).astype(BF16)
            if k:
                rs_copy(i, k).start()

    def rs_wait(i):
        total = r.part[i][own, :].astype(F32)
        for k in range(1, S):
            rs_copy(i, k).wait_recv()
            total = total + r.got[i][k - 1].astype(F32)
        return total

    def rs_sent(i):
        for k in range(1, S):
            rs_copy(i, k).wait_send()

    def sum_all(i, value):
        buf, sent, come = r.small.at[i], r.sm_send.at[i], r.sm_recv.at[i]
        slots = r.small_got.at[i]
        buf[...] = value
        base = 0
        for count, device in (
            (S, lambda k: (page, lax.rem(seq + k, S))),
            (B, lambda k: (a * B + lax.rem(b + k, B), seq)),
            (A, lambda k: (lax.rem(a + k, A) * B + b, seq)),
        ):
            copies = [
                remote(buf, slots.at[base + k - 1], sent.at[base + k - 1], come.at[base + k - 1], device(k))
                for k in range(1, count)
            ]
            for copy in copies:
                copy.start()
            for copy in copies:
                copy.wait()
            total = buf[...]
            for k in range(1, count):
                total = total + slots[base + k - 1]
            buf[...] = total
            base += count - 1

    def window(array, g, j):
        shard = ins[g].shape
        if g in (SELF, CROSS):
            return array.at[:, rows_at(j * shard[1], shard[1]), :]
        if g == UP:
            return array.at[rows_at(j * shard[0], shard[0]), :]
        return array.at[rows_at(lax.div(j, S) * shard[0], shard[0]), rows_at(lax.rem(j, S) * shard[1], shard[1])]

    def w_copy(g, j, way, src=None):
        place = window(w[g], g, j)
        device = (page + (-B, B, -1, 1)[way], seq)
        return remote(place if src is None else src, place, r.w_send.at[g, j, way], r.w_recv.at[g, j], device)

    ways = (a > 0, a < A - 1, b > 0, b < B - 1)

    def w_forward(g, j, along, src=None):
        for way in along:
            @pl.when(ways[way])
            def _():
                w_copy(g, j, way, src).start()

    def w_local(g):
        return pltpu.make_async_copy(
            stage[g] if g in MOVED else ins[g], window(w[g], g, page), r.w_local.at[g]
        )

    def move_copy(g):
        return remote(ins[g], stage[g], r.mv_send.at[g], r.mv_recv.at[g], (to_page, to_seq))

    def move_start(g):
        @pl.when(moves)
        def _():
            move_copy(g).start()

        @pl.when(fixed)
        def _():
            pltpu.make_async_copy(ins[g], stage[g], r.mv_recv.at[g]).start()

    def w_first(g):
        src = ins[g]
        if g in MOVED:
            src = stage[g]

            @pl.when(moves)
            def _():
                move_copy(g).wait_recv()

            @pl.when(fixed)
            def _():
                pltpu.make_async_copy(ins[g], stage[g], r.mv_recv.at[g]).wait()

        w_forward(g, page, (0, 1, 2, 3), src)
        w_local(g).start()

    def w_step(g, d):
        @pl.when(a - d >= 0)
        def _():
            j = page - d * B
            landed(window(w[g], g, j), r.w_recv.at[g, j])
            w_forward(g, j, (1, 2, 3))

        @pl.when(a + d < A)
        def _():
            j = page + d * B
            landed(window(w[g], g, j), r.w_recv.at[g, j])
            w_forward(g, j, (0, 2, 3))

    def w_wait(g):
        w_local(g).wait()
        for e in range(1, B):
            for t in range(A):
                @pl.when(b - e >= 0)
                def _():
                    j = t * B + b - e
                    landed(window(w[g], g, j), r.w_recv.at[g, j])
                    w_forward(g, j, (3,))

                @pl.when(b + e < B)
                def _():
                    j = t * B + b + e
                    landed(window(w[g], g, j), r.w_recv.at[g, j])
                    w_forward(g, j, (2,))

    def w_sent(g):
        if g in MOVED:
            @pl.when(moves)
            def _():
                move_copy(g).wait_send()

        for t in range(A):
            for e in range(B):
                j = t * B + e
                for way, when in enumerate(
                    ((b == e) & (t >= a), (b == e) & (t <= a), e >= b, e <= b)
                ):
                    @pl.when(when & ways[way])
                    def _():
                        w_copy(g, j, way).wait_send()

    def y_copy(g, k, t):
        other = lax.rem(b + k, B)
        return remote(
            window(grad[g], g, t * B + other),
            rb[g].at[B - 1 - k, t],
            r.y_send.at[g, k - 1, t],
            r.y_recv.at[g, B - 1 - k, t],
            (a * B + other, seq),
        )

    def y_start(g):
        for k in range(1, B):
            for t in range(A):
                y_copy(g, k, t).start()

    def y_sum(g):
        for t in range(A):
            total = window(grad[g], g, t * B + b)[...].astype(F32)
            for slot in range(B - 1):
                landed(rb[g].at[slot, t], r.y_recv.at[g, slot, t])
                total = total + rb[g][slot, t].astype(F32)
            rb[g][0, t] = total.astype(BF16)

    def z_slot(t, at, sign):
        return jnp.where((t == at) & (sign < 0), A, t)

    def z_copy(g, t, sign):
        slot = z_slot(t, a + sign, sign)
        return remote(
            rb[g].at[0, t],
            zz[g].at[slot],
            r.z_send.at[g, t],
            r.z_recv.at[g, slot],
            (page + sign * B, seq),
        )

    def z_pass(g, sign):
        before = a - sign
        has = (before >= 0) & (before < A)
        for k in range(A - 1, 0, -1):
            t = a + sign * k

            @pl.when((t >= 0) & (t < A))
            def _():
                @pl.when(has)
                def _():
                    landed(zz[g].at[t], r.z_recv.at[g, t])
                    rb[g][0, t] = (rb[g][0, t].astype(F32) + zz[g][t].astype(F32)).astype(BF16)

                z_copy(g, t, sign).start()

    first_sign = jnp.where(2 * a < A, 1, -1)

    def back_copy(g):
        return remote(
            back[g].at[0], back[g].at[1], r.bk_send.at[g], r.bk_recv.at[g], (from_page, from_seq)
        )

    def z_total(g):
        @pl.when(a > 0)
        def _():
            landed(zz[g].at[a], r.z_recv.at[g, a])

        @pl.when(a < A - 1)
        def _():
            landed(zz[g].at[A], r.z_recv.at[g, A])

        total = rb[g][0, a].astype(F32)
        total = total + jnp.where(a > 0, zz[g][a].astype(F32), 0.0)
        total = total + jnp.where(a < A - 1, zz[g][A].astype(F32), 0.0)
        if g in MOVED:
            back[g][0] = total.astype(BF16)

            @pl.when(moves)
            def _():
                back_copy(g).start()
        else:
            outs[g][...] = total

    def z_finish(g):
        if g in MOVED:
            @pl.when(moves)
            def _():
                back_copy(g).wait()
                outs[g][...] = back[g][1].astype(F32)

            @pl.when(fixed)
            def _():
                outs[g][...] = back[g][0].astype(F32)

        for t in range(A):
            for k in range(1, B):
                y_copy(g, k, t).wait_send()

            @pl.when(t != a)
            def _():
                z_copy(g, t, jnp.where(t > a, 1, -1)).wait_send()

    token_live = r.token_counts[0]
    patch_live = r.patch_counts[0]
    gains = lambda k: r.small[0, k : k + 1, :]
    biases = lambda k: r.small[0, 3 + k : 4 + k, :]
    QB = min(256, T)
    lane = lax.broadcasted_iota(jnp.int32, (1, LANES), 1)
    halves = [(lane // HEAD_DIM == h) for h in range(2)]
    half_of = [half.astype(F32).astype(BF16) for half in halves]
    scale = HEAD_DIM ** (-0.5)

    def project(dst, left, weight):
        for n, (out, index) in enumerate(dst):
            out[...] = nn(left[...], weight[index]).astype(BF16)

    def attend(q, k, v, o, probs, live, causal):
        @pl.loop(0, Dl // LANES)
        def _(pair):
            cols = rows_at(pair * LANES, LANES)
            for block in range(T // QB):
                extent = (block + 1) * QB if causal else T
                rows = slice(block * QB, (block + 1) * QB)
                q2 = q[rows, cols]
                k2, v2 = k[:extent, cols], v[:extent, cols]
                at = lax.broadcasted_iota(jnp.int32, (QB, extent), 1)
                allowed = at < live
                if causal:
                    row = block * QB + lax.broadcasted_iota(jnp.int32, (QB, extent), 0)
                    allowed = allowed & (at <= row)
                found = []
                for h in range(2):
                    scores = nt(q2 * half_of[h], k2) * scale
                    scores = jnp.where(allowed, scores, -1e30)
                    raised = jnp.exp(scores - jnp.max(scores, axis=-1, keepdims=True))
                    share = (raised / jnp.sum(raised, axis=-1, keepdims=True)).astype(BF16)
                    probs[2 * pair + h, rows, :extent] = share
                    found.append(nn(share, v2))
                o[rows, cols] = jnp.where(halves[0], found[0], found[1]).astype(BF16)

    def attend_back(q, k, v, do, probs, dq, dk, dv, causal):
        @pl.loop(0, Dl // LANES)
        def _(pair):
            cols = rows_at(pair * LANES, LANES)
            r.dk_sum[...] = jnp.zeros_like(r.dk_sum)
            r.dv_sum[...] = jnp.zeros_like(r.dv_sum)
            for block in range(T // QB):
                extent = (block + 1) * QB if causal else T
                rows = slice(block * QB, (block + 1) * QB)
                q2, do2 = q[rows, cols], do[rows, cols]
                k2, v2 = k[:extent, cols], v[:extent, cols]
                dqs, dks, dvs = [], [], []
                for h in range(2):
                    share = probs[2 * pair + h, rows, :extent]
                    wide = share.astype(F32)
                    dp = nt(do2 * half_of[h], v2)
                    delta = jnp.sum(wide * dp, axis=-1, keepdims=True)
                    ds = (wide * (dp - delta)).astype(BF16)
                    dqs.append(nn(ds, k2))
                    dks.append(tn(ds, q2))
                    dvs.append(tn(share, do2))
                dq[rows, cols] = (jnp.where(halves[0], dqs[0], dqs[1]) * scale).astype(BF16)
                r.dk_sum[:extent, :] += jnp.where(halves[0], dks[0], dks[1])
                r.dv_sum[:extent, :] += jnp.where(halves[0], dvs[0], dvs[1])
            dk[:, cols] = (r.dk_sum[...] * scale).astype(BF16)
            dv[:, cols] = r.dv_sum[...].astype(BF16)

    def norm_back(k, values, incoming):
        unit, rate = normed(values)
        r.norm_terms[k : k + 1, :] = jnp.sum(incoming * unit, axis=0, keepdims=True)
        r.norm_terms[3 + k : 4 + k, :] = jnp.sum(incoming, axis=0, keepdims=True)
        dn = incoming * gains(k)
        return rate * (
            dn - jnp.mean(dn, axis=-1, keepdims=True) - unit * jnp.mean(dn * unit, axis=-1, keepdims=True)
        )

    def norm_own(k, values, dst):
        dst[own, :] = (normed(values)[0] * gains(k) + biases(k)).astype(BF16)

    tile = min(256, Fl)
    tiles = Fl // tile

    for g in MOVED:
        move_start(g)
    loads = []
    given = (
        (G_TOKENS, r.tokens, r.all_tokens), (G_MEMORY, r.memory, r.all_memory), (G_COT, r.cotangent, r.dyr)
    )
    for i, mine, everyone in given:
        ag_start(i, mine, everyone)
        load = pltpu.make_async_copy(mine, everyone.at[own], r.ld_sem.at[i])
        load.start()
        loads.append(load)
    w_first(SELF)
    sum_all(0, r.norms[...])
    w_first(SELF_OUT)
    w_first(CROSS)
    for load in loads:
        load.wait()
    ag_wait(G_TOKENS, r.all_tokens)

    @pl.loop(0, S)
    def _(n):
        at = rows_at(n * Tl, Tl)
        values = r.all_tokens[at, :].astype(F32)
        r.a1[at, :] = (normed(values)[0] * gains(0) + biases(0)).astype(BF16)

    w_step(SELF, 1)
    w_step(SELF_OUT, 1)
    w_step(SELF, 2)
    w_step(SELF_OUT, 2)
    w_step(SELF, 3) if A > 3 else None
    w_step(SELF_OUT, 3) if A > 3 else None
    w_step(CROSS, 1)
    w_first(CROSS_OUT)
    w_first(UP)
    w_wait(SELF)
    project(((r.q, 0), (r.k, 1), (r.v, 2)), r.a1, w[SELF])
    w_step(CROSS, 2)
    w_step(CROSS_OUT, 1)
    attend(r.q, r.k, r.v, r.o, r.p, token_live, True)
    w_step(CROSS, 3)
    w_step(CROSS_OUT, 2)
    w_wait(SELF_OUT)
    rs_start(R_CHAIN, lambda at: nn(r.o[at, :], w[SELF_OUT][...]))
    w_step(CROSS_OUT, 3)
    w_step(UP, 1)
    w_first(DOWN)
    w_wait(CROSS)
    ag_wait(G_MEMORY, r.all_memory)
    project(((r.kc, 1), (r.vc, 2)), r.all_memory, w[CROSS])
    r.x1[...] = r.all_tokens[own, :].astype(F32) + rs_wait(R_CHAIN)
    norm_own(1, r.x1[...], r.a2)
    ag_start(G_A2, r.a2.at[own], r.a2)
    rs_sent(R_CHAIN)
    w_step(UP, 2)
    w_step(DOWN, 1)
    ag_wait(G_A2, r.a2)
    project(((r.qc, 0),), r.a2, w[CROSS])
    attend(r.qc, r.kc, r.vc, r.oc, r.pc, patch_live, False)
    w_step(UP, 3)
    w_step(DOWN, 2)
    w_wait(CROSS_OUT)
    rs_start(R_CHAIN, lambda at: nn(r.oc[at, :], w[CROSS_OUT][...]))
    w_step(DOWN, 3)
    ag_wait(G_COT, r.dyr)

    @pl.loop(0, S)
    def _(n):
        at = rows_at(n * Tl, Tl)
        row = n * Tl + lax.broadcasted_iota(jnp.int32, (Tl, 1), 0)
        values = r.dyr[at, :].astype(F32)
        r.dyr[at, :] = jnp.where(row < token_live, values, 0.0).astype(BF16)

    r.x2[...] = r.x1[...] + rs_wait(R_CHAIN)
    norm_own(2, r.x2[...], r.a3)
    ag_start(G_A3, r.a3.at[own], r.a3)
    rs_sent(R_CHAIN)
    w_wait(UP)
    ag_wait(G_A3, r.a3)

    @pl.loop(0, tiles)
    def _(n):
        cols = rows_at(n * tile, tile)
        out, slope = gelu_pair(nn(r.a3[...], w[UP][:, cols]))
        r.g[:, cols] = out.astype(BF16)
        r.slope[:, cols] = slope

    w_wait(DOWN)

    @pl.loop(0, tiles)
    def _(n):
        cols = rows_at(n * tile, tile)
        r.du[:, cols] = (nt(r.dyr[...], w[DOWN][cols, :]) * r.slope[:, cols]).astype(BF16)

    rs_start(R_CHAIN, lambda at: nt(r.du[at, :], w[UP][...]))

    @pl.loop(0, tiles)
    def _(n):
        cols = rows_at(n * tile, tile)
        grad[DOWN][cols, :] = tn(r.g[:, cols], r.dyr[...]).astype(BF16)

    y_start(DOWN)

    @pl.loop(0, D // 256)
    def _(n):
        cols = rows_at(n * 256, 256)
        grad[UP][cols, :] = tn(r.a3[:, cols], r.du[...]).astype(BF16)

    y_start(UP)
    r.dx2[...] = r.dyr[own, :].astype(F32) + norm_back(2, r.x2[...], rs_wait(R_CHAIN))
    r.dz2[own, :] = r.dx2[...].astype(BF16)
    ag_start(G_DZ2, r.dz2.at[own], r.dz2)
    rs_sent(R_CHAIN)
    rs_start(R_MIXED, lambda at: nn(r.g[at, :], w[DOWN][...]))
    ag_wait(G_DZ2, r.dz2)
    r.do[...] = nt(r.dz2[...], w[CROSS_OUT][...]).astype(BF16)
    attend_back(
        r.qc, r.kc, r.vc, r.do, r.pc, r.dq, r.dk, r.dv, False
    )
    rs_start(R_CHAIN, lambda at: nt(r.dq[at, :], w[CROSS][0]))
    y_sum(DOWN)
    z_pass(DOWN, first_sign)
    grad[CROSS_OUT][...] = tn(r.oc[...], r.dz2[...]).astype(BF16)
    for n, (left, right) in enumerate(((r.a2, r.dq), (r.all_memory, r.dk), (r.all_memory, r.dv))):
        grad[CROSS][n] = tn(left[...], right[...]).astype(BF16)
    y_start(CROSS_OUT)
    y_start(CROSS)
    r.dx1[...] = r.dx2[...] + norm_back(1, r.x1[...], rs_wait(R_CHAIN))
    ag_sent(G_A3, r.a3.at[own], r.a3)
    r.dz1[own, :] = r.dx1[...].astype(BF16)
    ag_start(G_DZ1, r.dz1.at[own], r.dz1)
    rs_sent(R_CHAIN)
    rs_start(
        R_MEMORY, lambda at: nt(r.dk[at, :], w[CROSS][1]) + nt(r.dv[at, :], w[CROSS][2])
    )
    z_pass(DOWN, -first_sign)
    ag_wait(G_DZ1, r.dz1)
    r.do[...] = nt(r.dz1[...], w[SELF_OUT][...]).astype(BF16)
    attend_back(r.q, r.k, r.v, r.do, r.p, r.dq, r.dk, r.dv, True)
    rs_start(
        R_CHAIN,
        lambda at: nt(r.dq[at, :], w[SELF][0])
        + nt(r.dk[at, :], w[SELF][1])
        + nt(r.dv[at, :], w[SELF][2]),
    )
    y_sum(UP)
    z_pass(UP, first_sign)
    grad[SELF_OUT][...] = tn(r.o[...], r.dz1[...]).astype(BF16)
    for n, right in enumerate((r.dq, r.dk, r.dv)):
        grad[SELF][n] = tn(r.a1[...], right[...]).astype(BF16)
    y_start(SELF_OUT)
    y_start(SELF)
    z_total(DOWN)
    z_pass(UP, -first_sign)
    live_row = (seq * Tl + lax.broadcasted_iota(jnp.int32, (Tl, 1), 0)) < token_live
    r.mixed[...] = jnp.where(live_row, r.x2[...] + rs_wait(R_MIXED), 0.0).astype(BF16)
    r.memory_grad[...] = rs_wait(R_MEMORY)
    r.input_grad[...] = r.dx1[...] + norm_back(
        0, r.all_tokens[own, :].astype(F32), rs_wait(R_CHAIN)
    )
    y_sum(CROSS_OUT)
    z_pass(CROSS_OUT, first_sign)
    y_sum(CROSS)
    z_pass(CROSS, first_sign)
    z_total(UP)
    z_pass(CROSS_OUT, -first_sign)
    z_pass(CROSS, -first_sign)
    y_sum(SELF_OUT)
    z_pass(SELF_OUT, first_sign)
    y_sum(SELF)
    z_pass(SELF, first_sign)
    z_pass(SELF_OUT, -first_sign)
    z_total(CROSS_OUT)
    z_total(CROSS)
    r.norm_terms[6:8, :] = jnp.zeros((2, D), F32)
    sum_all(1, r.norm_terms[...])
    r.norm_sums[...] = r.small[1]
    z_pass(SELF, -first_sign)
    z_total(SELF_OUT)
    z_total(SELF)

    for i in (R_CHAIN, R_MIXED, R_MEMORY):
        rs_sent(i)
    for i, mine, everyone in given:
        ag_sent(i, mine, everyone)
    for i, everyone in ((G_A2, r.a2), (G_DZ2, r.dz2), (G_DZ1, r.dz1)):
        ag_sent(i, everyone.at[own], everyone)
    for g in range(6):
        w_sent(g)
        z_finish(g)


def layer_call(A, B, S, rows, weights, norms, counts):
    V = pltpu.VMEM
    Tl, D = rows[0].shape
    T = Tl * S
    Dl = weights[SELF].shape[2]
    Fl = weights[UP].shape[1]
    pages = A * B
    R = pages // S
    heads = Dl // HEAD_DIM
    shards = [x.shape for x in weights]
    full = []
    for g, s in enumerate(shards):
        if g in (SELF, CROSS):
            full.append((s[0], s[1] * pages, s[2]))
        elif g == UP:
            full.append((s[0] * pages, s[1]))
        else:
            full.append((s[0] * R, s[1] * S))
    hbm, vmem, smem = (pl.BlockSpec(memory_space=m) for m in (pl.ANY, V, pltpu.SMEM))
    shape = jax.ShapeDtypeStruct
    dma = pltpu.SemaphoreType.DMA
    small_slots = S + A + B - 3
    row_ref, wide_ref = V((T, D), BF16), V((T, Dl), BF16)
    own_ref, hidden_ref = V((Tl, D), F32), V((T, Fl), BF16)
    operands = dict(
        tokens=rows[0],
        memory=rows[1],
        cotangent=rows[2],
        ins=list(weights),
        norms=norms,
        token_counts=counts[0],
        patch_counts=counts[1],
    )
    specs = dict(
        tokens=hbm, memory=hbm, cotangent=hbm, ins=[hbm] * 6, norms=vmem, token_counts=smem, patch_counts=smem
    )
    results = dict(
        mixed=shape((Tl, D), BF16),
        input_grad=shape((Tl, D), F32),
        memory_grad=shape((Tl, D), F32),
        outs=[shape(s, F32) for s in shards],
        norm_sums=shape((8, D), F32),
    )
    scratch = dict(
        w=[V(s, BF16) for s in full],
        grad=[V(s, BF16) for s in full],
        rb=[V((B - 1, A, *s), BF16) for s in shards],
        zz=[V((A + 1, *s), BF16) for s in shards],
        stage=[V(shards[g], BF16) for g in MOVED],
        back=[V((2, *shards[g]), BF16) for g in MOVED],
        all_tokens=row_ref,
        all_memory=row_ref,
        dyr=row_ref,
        a1=row_ref,
        a2=row_ref,
        a3=row_ref,
        dz2=row_ref,
        q=wide_ref,
        k=wide_ref,
        v=wide_ref,
        o=wide_ref,
        qc=wide_ref,
        kc=wide_ref,
        vc=wide_ref,
        oc=wide_ref,
        do=wide_ref,
        dq=wide_ref,
        dk=wide_ref,
        dv=wide_ref,
        p=V((heads, T, T), BF16),
        pc=V((heads, T, T), BF16),
        g=hidden_ref,
        du=hidden_ref,
        slope=V((T, Fl), F32),
        x1=own_ref,
        x2=own_ref,
        dx1=own_ref,
        dx2=own_ref,
        dk_sum=V((T, LANES), F32),
        dv_sum=V((T, LANES), F32),
        part=[row_ref] * 3,
        got=[V((S - 1, Tl, D), BF16)] * 3,
        small=V((2, 8, D), F32),
        small_got=V((2, small_slots, 8, D), F32),
        norm_terms=V((8, D), F32),
        ag_send=dma((7, S - 1)),
        ag_recv=dma((7, S)),
        rs_send=dma((3, S - 1)),
        rs_recv=dma((3, S - 1)),
        sm_send=dma((2, small_slots)),
        sm_recv=dma((2, small_slots)),
        ld_sem=dma((3,)),
        w_send=dma((6, pages, 4)),
        w_recv=dma((6, pages)),
        w_local=dma((6,)),
        mv_send=dma((6,)),
        mv_recv=dma((6,)),
        y_send=dma((6, B - 1, A)),
        y_recv=dma((6, B - 1, A)),
        z_send=dma((6, A)),
        z_recv=dma((6, A + 1)),
        bk_send=dma((6,)),
        bk_recv=dma((6,)),
    )
    parts = [jax.tree.flatten(part) for part in (operands, specs, results, scratch)]
    values, in_specs, out_shape, scratch_shapes = (leaves for leaves, _ in parts)
    ends = [len(values), len(values) + len(out_shape)]

    def kernel(*refs):
        held = (refs[: ends[0]], refs[ends[0] : ends[1]], refs[ends[1] :])
        r = types.SimpleNamespace()
        for (_, tree), some in zip((parts[0], parts[2], parts[3]), held):
            vars(r).update(jax.tree.unflatten(tree, some))
        layer_kernel(A, B, S, r)

    found = pl.pallas_call(
        kernel,
        out_shape=out_shape,
        in_specs=in_specs,
        out_specs=[vmem] * len(out_shape),
        scratch_shapes=scratch_shapes,
        compiler_params=pltpu.CompilerParams(
            collective_id=0, has_side_effects=True, vmem_limit_bytes=62 * 2**20
        ),
        name="layer",
    )(*values)
    return jax.tree.unflatten(parts[2][1], found)


def per_device(
    tokens,
    memory,
    cotangent,
    self_qkv,
    self_out,
    cross_qkv,
    cross_out,
    up_weight,
    down_weight,
    norm_gains,
    norm_biases,
    token_counts,
    patch_counts,
):
    pages = lax.axis_size("page")
    parts = lax.axis_size("seq")
    wide = 2 if pages == 8 else 8
    features = tokens.shape[2]
    few = norm_gains.shape[1]
    place = (lax.axis_index("page") * parts + lax.axis_index("seq")) * few
    norms = lax.dynamic_update_slice(
        jnp.zeros((8, features), F32),
        jnp.concatenate([norm_gains, norm_biases]).astype(F32),
        (0, place),
    )
    found = layer_call(
        pages // wide,
        wide,
        parts,
        (tokens[0], memory[0], cotangent[0]),
        (self_qkv, self_out, cross_qkv, cross_out, up_weight, down_weight),
        norms,
        (token_counts, patch_counts),
    )
    norm_own = lax.dynamic_slice(found["norm_sums"], (0, place), (8, few))
    return (
        found["mixed"][None],
        found["input_grad"][None],
        found["memory_grad"][None],
        *found["outs"],
        norm_own[:3],
        norm_own[3:6],
    )


def solution(mesh):
    rows = P("page", "seq", None)
    stack = P(None, "page", "seq")
    flat = P("page", "seq")
    norm = P(None, ("page", "seq"))
    counts = P("page")
    return jax.shard_map(
        per_device,
        mesh=mesh,
        in_specs=(rows, rows, rows, stack, flat, stack, flat, flat, flat, norm, norm, counts, counts),
        out_specs=(rows, rows, rows, stack, flat, stack, flat, flat, flat, norm, norm),
        check_vma=False,
    )
```

```python
import types

import jax
import jax.numpy as jnp
from jax import lax
from jax.experimental import pallas as pl
from jax.experimental.pallas import tpu as pltpu
from jax.sharding import PartitionSpec as P

HEAD_DIM = 64
F32 = jnp.float32
BF16 = jnp.bfloat16
MESH = pl.DeviceIdType.MESH
SELF, SELF_OUT, CROSS, CROSS_OUT, UP, DOWN = range(6)
MOVED = (SELF_OUT, CROSS_OUT, DOWN)
UNITS = ((SELF, 0), (SELF, 1), (SELF, 2), (CROSS, 0), (CROSS, 1), (CROSS, 2), (UP, None))
SELF_UNITS, CROSS_UNITS, UP_UNIT = (0, 1, 2), (3, 4, 5), 6
G_TOKENS, G_MEMORY, G_COT, G_A2, G_A3, G_DZ2, G_DZ1 = range(7)
R_CHAIN, R_MIXED, R_MEMORY = range(3)
LANES = 128


def nn(left, right):
    return lax.dot_general(left, right, (((1,), (0,)), ((), ())), preferred_element_type=F32)


def nt(left, right):
    return lax.dot_general(left, right, (((1,), (1,)), ((), ())), preferred_element_type=F32)


def tn(left, right):
    return lax.dot_general(left, right, (((0,), (0,)), ((), ())), preferred_element_type=F32)


def rows_at(start, size):
    return pl.ds(pl.multiple_of(start, size), size)


def normed(values):
    center = values - jnp.mean(values, axis=-1, keepdims=True)
    rate = lax.rsqrt(jnp.mean(center * center, axis=-1, keepdims=True) + 1e-05)
    return center * rate, rate


def gelu_pair(values):
    chance = 0.5 + 0.5 * lax.erf(values * 0.7071067811865476)
    density = jnp.exp(-0.5 * values * values) * 0.3989422804014327
    return values * chance, chance + values * density


def layer_kernel(A, B, S, r):
    r.dz1 = r.a3
    r.part = [r.chain_part, r.dz2, r.a2]
    ins, w, grad, outs = r.ins, r.w, r.grad, r.outs
    page, seq = lax.axis_index("page"), lax.axis_index("seq")
    a, b = lax.div(page, B), lax.rem(page, B)
    R = A * B // S
    Tl, D = r.tokens.shape
    T = Tl * S
    Dl = ins[SELF].shape[2]
    Fl = ins[UP].shape[1]
    own = rows_at(seq * Tl, Tl)
    shelf, collector = lax.rem(page, R), lax.div(page, R)
    collects = seq == collector
    a0, b0 = lax.div(seq * R, B), lax.rem(seq * R, B)
    mine = b - b0
    holds = (mine >= 0) & (mine < R)

    def remote(src, dst, send, recv, device):
        return pltpu.make_async_remote_copy(
            src_ref=src, dst_ref=dst, send_sem=send, recv_sem=recv, device_id=device, device_id_type=MESH
        )

    def landed(dst, recv):
        remote(dst, dst, recv, recv, (page, seq)).wait_recv()

    barrier = pltpu.get_barrier_semaphore()

    def greet(device):
        pl.semaphore_signal(barrier, inc=1, device_id=device, device_id_type=MESH)

    for k in range(1, S):
        greet((page, lax.rem(seq + k, S)))
    for k in range(1, B):
        greet((a * B + lax.rem(b + k, B), seq))
    for k in range(1, A):
        greet((lax.rem(a + k, A) * B + b, seq))

    pl.semaphore_wait(barrier, S + A + B - 3)

    X = S // 2
    chip, core = lax.div(seq, 2), lax.rem(seq, 2)
    sibling = chip * 2 + 1 - core
    half = Tl // 2

    def part_of(source, ch):
        return rows_at(source * Tl + ch * half, half)

    def chip_at(dx):
        return lax.rem(chip + dx, X)

    def ag_copy(i, src, dst, ch, n):
        source = chip_at(2 * X - 1 - n) * 2 + core if n >= X else seq
        mine = dst.at[part_of(source, ch)] if n >= X else src.at[rows_at(ch * half, half)]
        to = chip_at(n) * 2 + core if 0 < n < X else sibling
        return remote(
            mine, dst.at[part_of(source, ch)], r.ag_send.at[i, ch, n], r.ag_recv.at[i, ch, source], (page, to)
        )

    def ag_start(i, src, dst, ch):
        for n in (*range(1, X), 0):
            ag_copy(i, src, dst, ch, n).start()

    def ag_begin(i, src, dst):
        for ch in range(2):
            ag_start(i, src, dst, ch)

    def ag_forward(i, dst):
        for ch in range(2):
            for n in range(X, 2 * X - 1):
                source = chip_at(2 * X - 1 - n) * 2 + core
                landed(dst.at[part_of(source, ch)], r.ag_recv.at[i, ch, source])
                ag_copy(i, None, dst, ch, n).start()

    def ag_wait(i, dst):
        for ch in range(2):
            for x in range(X):
                source = 2 * x + 1 - core
                landed(dst.at[part_of(source, ch)], r.ag_recv.at[i, ch, source])

    def ag_sent(i, src, dst):
        for ch in range(2):
            for n in range(2 * X - 1):
                ag_copy(i, src, dst, ch, n).wait_send()

    def rs_copy(i, x, ch):
        return remote(
            r.part[i].at[part_of(x * 2 + 1 - core, ch)],
            r.got[i].at[x, rows_at(ch * half, half)],
            r.rs_send.at[i, ch, x],
            r.rs_recv.at[i, ch, x],
            (page, sibling),
        )

    def rs_far(i, dx, ch):
        to = chip_at(dx) * 2 + core
        slot = X + dx - 1
        return remote(
            r.part[i].at[part_of(to, ch)],
            r.got[i].at[slot, rows_at(ch * half, half)],
            r.rs_send.at[i, ch, slot],
            r.rs_recv.at[i, ch, slot],
            (page, to),
        )

    def rs_start(i, term):
        part, got = r.part[i], r.got[i]
        for n in range(1, X + 1):
            x = chip_at(n)
            at = rows_at((x * 2 + 1 - core) * Tl, Tl)
            part[at, :] = term(at).astype(BF16)
            for ch in range(2):
                rs_copy(i, x, ch).start()
        for dx in range(1, X):
            x = chip_at(dx)
            at = rows_at((x * 2 + core) * Tl, Tl)
            mine = term(at)
            for ch in range(2):
                rs_copy(i, x, ch).wait_recv()
                other = got[x, ch * half : (ch + 1) * half, :].astype(F32)
                part[part_of(x * 2 + core, ch), :] = (mine[ch * half : (ch + 1) * half] + other).astype(BF16)
                rs_far(i, dx, ch).start()
        part[own, :] = term(own).astype(BF16)

    def rs_wait(i, ch):
        rows = slice(ch * half, (ch + 1) * half)
        rs_copy(i, chip, ch).wait_recv()
        total = r.part[i][part_of(seq, ch), :].astype(F32) + r.got[i][chip, rows, :].astype(F32)
        for dx in range(1, X):
            rs_far(i, dx, ch).wait_recv()
            total = total + r.got[i][X + dx - 1, rows, :].astype(F32)
        return total

    def rs_sent(i):
        for ch in range(2):
            for x in range(X):
                rs_copy(i, x, ch).wait_send()
            for dx in range(1, X):
                rs_far(i, dx, ch).wait_send()

    def small_copies(i, level):
        count, base, device = (
            (B, 0, lambda k: (a * B + lax.rem(b + k, B), seq)),
            (A, B - 1, lambda k: (lax.rem(a + k, A) * B + b, seq)),
            (S, A + B - 2, lambda k: (page, lax.rem(seq + k, S))),
        )[level]
        return [
            remote(
                r.small.at[i],
                r.small_got.at[i, base + k - 1],
                r.sm_send.at[i, base + k - 1],
                r.sm_recv.at[i, base + k - 1],
                device(k),
            )
            for k in range(1, count)
        ], base

    def small_start(i, level):
        for copy in small_copies(i, level)[0]:
            copy.start()

    def small_wait(i, level):
        copies, base = small_copies(i, level)
        for copy in copies:
            copy.wait()
        total = r.small[i]
        for k in range(len(copies)):
            total = total + r.small_got[i, base + k]
        r.small[i] = total

    def rows_of(arrays, u, j):
        g, n = UNITS[u]
        size = ins[g].shape[-2]
        at = rows_at(j * size, size)
        return arrays[g].at[at, :] if n is None else arrays[g].at[n, at, :]

    def whole_of(arrays, u):
        g, n = UNITS[u]
        return arrays[g] if n is None else arrays[g].at[n]

    def w_copy(u, j, way, src=None):
        place = rows_of(w, u, j)
        device = (page + (-B, B, -1, 1)[way], seq)
        return remote(place if src is None else src, place, r.w_send.at[u, j, way], r.w_recv.at[u, j], device)

    ways = (a > 0, a < A - 1, b > 0, b < B - 1)

    def w_forward(u, j, along, src=None):
        for way in along:
            @pl.when(ways[way])
            def _():
                w_copy(u, j, way, src).start()

    def w_local(u):
        return pltpu.make_async_copy(whole_of(ins, u), rows_of(w, u, page), r.w_local.at[u])

    def w_first(*units):
        for u in units:
            w_forward(u, page, (0, 1, 2, 3), whole_of(ins, u))
            w_local(u).start()

    def w_step(d, *units):
        for u in units:
            @pl.when(a - d >= 0)
            def _():
                j = page - d * B
                landed(rows_of(w, u, j), r.w_recv.at[u, j])
                w_forward(u, j, (1, 2, 3))

            @pl.when(a + d < A)
            def _():
                j = page + d * B
                landed(rows_of(w, u, j), r.w_recv.at[u, j])
                w_forward(u, j, (0, 2, 3))

    def w_wait(*units):
        for u in units:
            w_local(u).wait()
            for e in range(1, B):
                for t in range(A):
                    @pl.when(b - e >= 0)
                    def _():
                        j = t * B + b - e
                        landed(rows_of(w, u, j), r.w_recv.at[u, j])
                        w_forward(u, j, (3,))

                    @pl.when(b + e < B)
                    def _():
                        j = t * B + b + e
                        landed(rows_of(w, u, j), r.w_recv.at[u, j])
                        w_forward(u, j, (2,))

    def w_sent(u):
        for t in range(A):
            for e in range(B):
                j = t * B + e
                for way, when in enumerate(
                    ((b == e) & (t >= a), (b == e) & (t <= a), e >= b, e <= b)
                ):
                    @pl.when(when & ways[way])
                    def _():
                        w_copy(u, j, way).wait_send()

    def block(array, g, e, n):
        rows, cols = ins[g].shape
        return array.at[rows_at(e * rows, rows), rows_at(n * cols, cols)]

    def m_local(g):
        return pltpu.make_async_copy(ins[g], block(w[g], g, shelf, seq), r.m_got.at[MOVED.index(g), seq])

    def m_collect_copy(g):
        i = MOVED.index(g)
        return remote(
            ins[g], block(w[g], g, shelf, seq), r.m_gave.at[i], r.m_got.at[i, seq], (page, collector)
        )

    def m_collect(g):
        @pl.when(collects)
        def _():
            m_local(g).start()

        @pl.when(jnp.logical_not(collects))
        def _():
            m_collect_copy(g).start()

    def m_copy(g, n, way):
        i = MOVED.index(g)
        place = block(w[g], g, mine, n)
        device = (page + B, page - B)[way] if way < 2 else a * B + lax.rem(b + way - 1, B)
        return remote(place, place, r.m_send.at[i, n, way], r.m_recv.at[i, mine, n], (device, seq))

    m_ways = [holds & (a >= a0) & (a < A - 1), holds & (a <= a0) & (a > 0)] + [holds] * (B - 1)

    def m_forward(g, n):
        for way in range(B + 1):
            @pl.when(m_ways[way])
            def _():
                m_copy(g, n, way).start()

    def m_first(g, n):
        @pl.when(collects)
        def _():
            @pl.when(seq == n)
            def _():
                m_local(g).wait()

            @pl.when(seq != n)
            def _():
                landed(block(w[g], g, shelf, n), r.m_got.at[MOVED.index(g), n])

            m_forward(g, n)

    def m_pass(g, n):
        @pl.when(holds & (a != a0))
        def _():
            landed(block(w[g], g, mine, n), r.m_recv.at[MOVED.index(g), mine, n])
            m_forward(g, n)

    def m_wait(g):
        for e in range(R):
            @pl.when(jnp.logical_not(holds) | (mine != e))
            def _():
                for n in range(S):
                    landed(block(w[g], g, e, n), r.m_recv.at[MOVED.index(g), e, n])

    def m_sent(g):
        @pl.when(jnp.logical_not(collects))
        def _():
            m_collect_copy(g).wait_send()

        for n in range(S):
            for way in range(B + 1):
                @pl.when(m_ways[way])
                def _():
                    m_copy(g, n, way).wait_send()

    low = 2 * a < A
    near = jnp.where(low, a, A - 1 - a)

    def order(m):
        if m == A - 1:
            return a
        t = jnp.where(m < A - 1 - near, A - 1 - m, m - (A - 1 - near))
        return jnp.where(low, t, A - 1 - t)

    def y_copy(u, k, t):
        other = lax.rem(b + k, B)
        return remote(
            rows_of(grad, u, t * B + other),
            r.rb[u].at[B - 1 - k, t],
            r.y_send.at[u, k - 1, t],
            r.y_recv.at[u, B - 1 - k, t],
            (a * B + other, seq),
        )

    def y_start(*units):
        for u in units:
            for m in range(A):
                for k in range(1, B):
                    y_copy(u, k, order(m)).start()

    def z_copy(u, t, sign):
        slot = jnp.where((t == a + sign) & (sign < 0), A, t)
        return remote(
            r.rb[u].at[0, t],
            r.zz[u].at[slot],
            r.z_send.at[u, t],
            r.z_recv.at[u, slot],
            (page + sign * B, seq),
        )

    def z_way(t):
        sign = jnp.where(t > a, 1, -1)
        before = a - sign
        return sign, (before >= 0) & (before < A)

    def y_sum(m, u):
        t = order(m)
        total = rows_of(grad, u, t * B + b)[...].astype(F32)
        for slot in range(B - 1):
            landed(r.rb[u].at[slot, t], r.y_recv.at[u, slot, t])
            total = total + r.rb[u][slot, t].astype(F32)
        r.rb[u][0, t] = total.astype(BF16)
        if m < A - 1:
            sign, has = z_way(t)

            @pl.when(jnp.logical_not(has))
            def _():
                z_copy(u, t, sign).start()

    def z_sum(m, u):
        t = order(m)
        sign, has = z_way(t)

        @pl.when(has)
        def _():
            landed(r.zz[u].at[t], r.z_recv.at[u, t])
            r.rb[u][0, t] = (r.rb[u][0, t].astype(F32) + r.zz[u][t].astype(F32)).astype(BF16)
            z_copy(u, t, sign).start()

    def z_total(u):
        @pl.when(a > 0)
        def _():
            landed(r.zz[u].at[a], r.z_recv.at[u, a])

        @pl.when(a < A - 1)
        def _():
            landed(r.zz[u].at[A], r.z_recv.at[u, A])

        total = r.rb[u][0, a].astype(F32)
        total = total + jnp.where(a > 0, r.zz[u][a].astype(F32), 0.0)
        total = total + jnp.where(a < A - 1, r.zz[u][A].astype(F32), 0.0)
        g, n = UNITS[u]
        if n is None:
            outs[g][...] = total
        else:
            outs[g][n] = total

    def z_sent(u):
        for t in range(A):
            for k in range(1, B):
                y_copy(u, k, t).wait_send()

            @pl.when(t != a)
            def _():
                z_copy(u, t, jnp.where(t > a, 1, -1)).wait_send()

    def unit_steps(*units):
        steps = [lambda: [y_sum(0, u) for u in units]]
        for m in range(1, A - 1):
            steps.append(lambda m=m: [(y_sum(m, u), z_sum(m - 1, u)) for u in units])
        steps.append(lambda: [(z_sum(A - 2, u), y_sum(A - 1, u)) for u in units])
        steps.append(lambda: [z_total(u) for u in units])
        return steps

    def f_copy(g, k, n):
        i = MOVED.index(g)
        other = lax.rem(b + k, B)
        return remote(
            block(grad[g], g, other - b0, n),
            r.fb[i].at[B - 1 - k, n],
            r.f_send.at[i, k - 1, n],
            r.f_recv.at[i, B - 1 - k, n],
            (a * B + other, seq),
        )

    def wanted(k):
        shelf_of = lax.rem(b + k, B) - b0
        return (shelf_of >= 0) & (shelf_of < R)

    def f_start(g):
        for n in range(S):
            for k in range(1, B):
                @pl.when(wanted(k))
                def _():
                    f_copy(g, k, n).start()

    inward = jnp.where(a > a0, -1, 1)
    from_out = holds & (a != a0) & (a > 0) & (a < A - 1)
    starts_line = holds & (a != a0) & ((a == 0) | (a == A - 1))

    def v_copy(g, n):
        i = MOVED.index(g)
        slot = jnp.where((a + 1 == a0), 1, 0)
        return remote(
            r.fb[i].at[0, n], r.vv[i].at[slot, n], r.v_send.at[i, n], r.v_recv.at[i, slot, n], (page + inward * B, seq)
        )

    def s_copy(g, n):
        i = MOVED.index(g)
        return remote(r.fb[i].at[0, n], r.back[i], r.s_send.at[i, n], r.s_recv.at[i], (page, n))

    def f_sum(g, n):
        i = MOVED.index(g)

        @pl.when(holds)
        def _():
            total = block(grad[g], g, mine, n)[...].astype(F32)
            for slot in range(B - 1):
                landed(r.fb[i].at[slot, n], r.f_recv.at[i, slot, n])
                total = total + r.fb[i][slot, n].astype(F32)
            r.fb[i][0, n] = total.astype(BF16)

            @pl.when(starts_line)
            def _():
                v_copy(g, n).start()

    def v_sum(g, n):
        i = MOVED.index(g)

        @pl.when(from_out)
        def _():
            landed(r.vv[i].at[0, n], r.v_recv.at[i, 0, n])
            r.fb[i][0, n] = (r.fb[i][0, n].astype(F32) + r.vv[i][0, n].astype(F32)).astype(BF16)
            v_copy(g, n).start()

    def v_total(g, n):
        i = MOVED.index(g)

        @pl.when(collects)
        def _():
            @pl.when(a < A - 1)
            def _():
                landed(r.vv[i].at[0, n], r.v_recv.at[i, 0, n])

            @pl.when(a > 0)
            def _():
                landed(r.vv[i].at[1, n], r.v_recv.at[i, 1, n])

            total = r.fb[i][0, n].astype(F32)
            total = total + jnp.where(a < A - 1, r.vv[i][0, n].astype(F32), 0.0)
            total = total + jnp.where(a > 0, r.vv[i][1, n].astype(F32), 0.0)

            @pl.when(seq == n)
            def _():
                outs[g][...] = total

            @pl.when(seq != n)
            def _():
                r.fb[i][0, n] = total.astype(BF16)
                s_copy(g, n).start()

    def s_wait(g):
        i = MOVED.index(g)

        @pl.when(jnp.logical_not(collects))
        def _():
            landed(r.back[i], r.s_recv.at[i])
            outs[g][...] = r.back[i][...].astype(F32)

    def v_sent(g):
        for n in range(S):
            for k in range(1, B):
                @pl.when(wanted(k))
                def _():
                    f_copy(g, k, n).wait_send()

            @pl.when(starts_line | from_out)
            def _():
                v_copy(g, n).wait_send()

            @pl.when(collects & (seq != n))
            def _():
                s_copy(g, n).wait_send()

    def moved_steps(g):
        steps = [lambda: f_sum(g, 0)]
        for n in range(1, S):
            steps.append(lambda n=n: (f_sum(g, n), v_sum(g, n - 1)))
        steps.append(lambda: (v_sum(g, S - 1), v_total(g, 0)))
        steps.append(lambda: [v_total(g, n) for n in range(1, S)])
        return steps

    token_live = r.token_counts[0]
    patch_live = r.patch_counts[0]
    r.norm_terms[6:8, :] = jnp.zeros((2, D), F32)
    gains = lambda k: r.small[0, k : k + 1, :]
    biases = lambda k: r.small[0, 3 + k : 4 + k, :]
    QB = min(256, T)
    lane = lax.broadcasted_iota(jnp.int32, (1, LANES), 1)
    halves = [(lane // HEAD_DIM == h) for h in range(2)]
    half_of = [half.astype(F32).astype(BF16) for half in halves]
    scale = HEAD_DIM ** (-0.5)

    def project(dst, left, weight):
        for n, (out, index) in enumerate(dst):
            out[...] = nn(left[...], weight[index]).astype(BF16)

    def attend(q, k, v, o, probs, live, causal):
        @pl.loop(0, Dl // LANES)
        def _(pair):
            cols = rows_at(pair * LANES, LANES)
            for block in range(T // QB):
                extent = (block + 1) * QB if causal else T
                rows = slice(block * QB, (block + 1) * QB)
                q2 = q[rows, cols]
                k2, v2 = k[:extent, cols], v[:extent, cols]
                at = lax.broadcasted_iota(jnp.int32, (QB, extent), 1)
                allowed = at < live
                if causal:
                    row = block * QB + lax.broadcasted_iota(jnp.int32, (QB, extent), 0)
                    allowed = allowed & (at <= row)
                found = []
                for h in range(2):
                    scores = nt(q2 * half_of[h], k2) * scale
                    scores = jnp.where(allowed, scores, -1e30)
                    raised = jnp.exp(scores - jnp.max(scores, axis=-1, keepdims=True))
                    share = (raised / jnp.sum(raised, axis=-1, keepdims=True)).astype(BF16)
                    probs[2 * pair + h, rows, :extent] = share
                    found.append(nn(share, v2))
                o[rows, cols] = jnp.where(halves[0], found[0], found[1]).astype(BF16)

    def attend_back(q, k, v, do, probs, dq, dk, dv, causal):
        @pl.loop(0, Dl // LANES)
        def _(pair):
            cols = rows_at(pair * LANES, LANES)
            r.dk_sum[...] = jnp.zeros_like(r.dk_sum)
            r.dv_sum[...] = jnp.zeros_like(r.dv_sum)
            for block in range(T // QB):
                extent = (block + 1) * QB if causal else T
                rows = slice(block * QB, (block + 1) * QB)
                q2, do2 = q[rows, cols], do[rows, cols]
                k2, v2 = k[:extent, cols], v[:extent, cols]
                dqs, dks, dvs = [], [], []
                for h in range(2):
                    share = probs[2 * pair + h, rows, :extent]
                    wide = share.astype(F32)
                    dp = nt(do2 * half_of[h], v2)
                    delta = jnp.sum(wide * dp, axis=-1, keepdims=True)
                    ds = (wide * (dp - delta)).astype(BF16)
                    dqs.append(nn(ds, k2))
                    dks.append(tn(ds, q2))
                    dvs.append(tn(share, do2))
                dq[rows, cols] = (jnp.where(halves[0], dqs[0], dqs[1]) * scale).astype(BF16)
                r.dk_sum[:extent, :] += jnp.where(halves[0], dks[0], dks[1])
                r.dv_sum[:extent, :] += jnp.where(halves[0], dvs[0], dvs[1])
            dk[:, cols] = (r.dk_sum[...] * scale).astype(BF16)
            dv[:, cols] = r.dv_sum[...].astype(BF16)

    def norm_back(k, values, incoming, ch):
        unit, rate = normed(values)
        for row, term in ((k, incoming * unit), (3 + k, incoming)):
            so_far = jnp.sum(term, axis=0, keepdims=True)
            r.norm_terms[row : row + 1, :] = so_far if ch == 0 else r.norm_terms[row : row + 1, :] + so_far
        dn = incoming * gains(k)
        return rate * (
            dn - jnp.mean(dn, axis=-1, keepdims=True) - unit * jnp.mean(dn * unit, axis=-1, keepdims=True)
        )

    def norm_own(k, values, dst, ch):
        dst[part_of(seq, ch), :] = (normed(values)[0] * gains(k) + biases(k)).astype(BF16)

    tile = min(256, Fl)
    tiles = Fl // tile

    few = r.norm_gains.shape[1]
    at_feature = lax.broadcasted_iota(jnp.int32, (few, D), 1)
    placed = at_feature == lax.broadcasted_iota(jnp.int32, (few, D), 0) + (page * S + seq) * few
    r.small[0] = jnp.zeros((8, D), F32)
    r.small[0, 0:3, :] = nn(r.norm_gains[...], placed.astype(F32).astype(BF16))
    r.small[0, 3:6, :] = nn(r.norm_biases[...], placed.astype(F32).astype(BF16))
    small_start(0, 0)
    w_first(*SELF_UNITS)
    m_collect(SELF_OUT)
    given = (
        (G_TOKENS, r.tokens, r.all_tokens), (G_MEMORY, r.memory, r.all_memory), (G_COT, r.cotangent, r.dyr)
    )
    loads = [pltpu.make_async_copy(piece, everyone.at[own], r.ld_sem.at[i]) for i, piece, everyone in given]
    ag_begin(*given[0])
    for load in loads:
        load.start()
    w_step(1, *SELF_UNITS)
    small_wait(0, 0)
    small_start(0, 1)
    m_collect(CROSS_OUT)
    ag_begin(*given[1])
    m_collect(DOWN)
    w_step(2, *SELF_UNITS)
    for n in range(S):
        m_first(SELF_OUT, n)
    small_wait(0, 1)
    small_start(0, 2)
    ag_forward(G_TOKENS, r.all_tokens)
    w_first(*CROSS_UNITS)
    ag_begin(*given[2])
    w_step(3, *SELF_UNITS)
    for n in range(S):
        m_pass(SELF_OUT, n)
    w_step(1, *CROSS_UNITS)
    small_wait(0, 2)
    ag_wait(G_TOKENS, r.all_tokens)
    for load in loads:
        load.wait()

    @pl.loop(0, S)
    def _(n):
        at = rows_at(n * Tl, Tl)
        values = r.all_tokens[at, :].astype(F32)
        r.a1[at, :] = (normed(values)[0] * gains(0) + biases(0)).astype(BF16)

    w_wait(*SELF_UNITS)
    project(((r.q, 0), (r.k, 1), (r.v, 2)), r.a1, w[SELF])
    w_step(2, *CROSS_UNITS)
    w_first(UP_UNIT)
    ag_forward(G_MEMORY, r.all_memory)
    attend(r.q, r.k, r.v, r.o, r.p, token_live, True)
    w_step(3, *CROSS_UNITS)
    m_wait(SELF_OUT)
    rs_start(R_CHAIN, lambda at: nn(r.o[at, :], w[SELF_OUT][...]))
    for n in range(S):
        m_first(CROSS_OUT, n)
    w_step(1, UP_UNIT)
    m_first(DOWN, 0)
    ag_forward(G_COT, r.dyr)
    for ch in range(2):
        rows = slice(ch * half, (ch + 1) * half)
        r.x1[rows, :] = r.all_tokens[part_of(seq, ch), :].astype(F32) + rs_wait(R_CHAIN, ch)
        norm_own(1, r.x1[rows, :], r.a2, ch)
        ag_start(G_A2, r.a2.at[own], r.a2, ch)
    rs_sent(R_CHAIN)
    for n in range(S):
        m_pass(CROSS_OUT, n)
    w_wait(*CROSS_UNITS)
    ag_wait(G_MEMORY, r.all_memory)
    project(((r.kc, 1), (r.vc, 2)), r.all_memory, w[CROSS])
    ag_forward(G_A2, r.a2)
    ag_wait(G_A2, r.a2)
    w_step(2, UP_UNIT)
    m_first(DOWN, 1)
    m_pass(DOWN, 0)
    project(((r.qc, 0),), r.a2, w[CROSS])
    attend(r.qc, r.kc, r.vc, r.oc, r.pc, patch_live, False)
    m_wait(CROSS_OUT)
    rs_start(R_CHAIN, lambda at: nn(r.oc[at, :], w[CROSS_OUT][...]))
    w_step(3, UP_UNIT)
    m_first(DOWN, 2)
    m_pass(DOWN, 1)
    m_first(DOWN, 3)
    ag_wait(G_COT, r.dyr)
    ag_sent(*given[2])

    @pl.loop(0, S)
    def _(n):
        at = rows_at(n * Tl, Tl)
        row = n * Tl + lax.broadcasted_iota(jnp.int32, (Tl, 1), 0)
        values = r.dyr[at, :].astype(F32)
        r.dyr[at, :] = jnp.where(row < token_live, values, 0.0).astype(BF16)

    for ch in range(2):
        rows = slice(ch * half, (ch + 1) * half)
        r.x2[rows, :] = r.x1[rows, :] + rs_wait(R_CHAIN, ch)
        norm_own(2, r.x2[rows, :], r.a3, ch)
        ag_start(G_A3, r.a3.at[own], r.a3, ch)
    rs_sent(R_CHAIN)
    m_pass(DOWN, 2)
    ag_forward(G_A3, r.a3)
    ag_wait(G_A3, r.a3)
    for n in range(3, S):
        m_pass(DOWN, n)
    w_wait(UP_UNIT)

    @pl.loop(0, tiles)
    def _(n):
        cols = rows_at(n * tile, tile)
        out, slope = gelu_pair(nn(r.a3[...], w[UP][:, cols]))
        r.g[:, cols] = out.astype(BF16)
        r.slope[:, cols] = slope

    @pl.loop(0, tiles)
    def _(n):
        cols = rows_at(n * tile, tile)
        grad[DOWN][cols, :] = tn(r.g[:, cols], r.dyr[...]).astype(BF16)

    f_start(DOWN)
    m_wait(DOWN)

    @pl.loop(0, tiles)
    def _(n):
        cols = rows_at(n * tile, tile)
        r.du[:, cols] = (nt(r.dyr[...], w[DOWN][cols, :]) * r.slope[:, cols]).astype(BF16)

    ag_sent(G_A3, r.a3.at[own], r.a3)
    rs_start(R_CHAIN, lambda at: nt(r.du[at, :], w[UP][...]))

    @pl.loop(0, D // 256)
    def _(n):
        cols = rows_at(n * 256, 256)
        grad[UP][cols, :] = tn(r.a3[:, cols], r.du[...]).astype(BF16)

    y_start(UP_UNIT)
    down, up = moved_steps(DOWN), unit_steps(UP_UNIT)
    down.pop(0)()
    for ch in range(2):
        rows = slice(ch * half, (ch + 1) * half)
        back_term = norm_back(2, r.x2[rows, :], rs_wait(R_CHAIN, ch), ch)
        r.dx2[rows, :] = r.dyr[part_of(seq, ch), :].astype(F32) + back_term
        r.dz2[part_of(seq, ch), :] = r.dx2[rows, :].astype(BF16)
        ag_start(G_DZ2, r.dz2.at[own], r.dz2, ch)
    rs_sent(R_CHAIN)
    down.pop(0)()
    ag_forward(G_DZ2, r.dz2)
    ag_wait(G_DZ2, r.dz2)
    r.do[...] = nt(r.dz2[...], w[CROSS_OUT][...]).astype(BF16)
    attend_back(r.qc, r.kc, r.vc, r.do, r.pc, r.dq, r.dk, r.dv, False)
    rs_start(R_CHAIN, lambda at: nt(r.dq[at, :], w[CROSS][0]))
    grad[CROSS_OUT][...] = tn(r.oc[...], r.dz2[...]).astype(BF16)
    f_start(CROSS_OUT)
    for n, (left, right) in enumerate(((r.a2, r.dq), (r.all_memory, r.dk), (r.all_memory, r.dv))):
        grad[CROSS][n] = tn(left[...], right[...]).astype(BF16)
    y_start(*CROSS_UNITS)
    down.pop(0)()
    down.pop(0)()
    for ch in range(2):
        rows = slice(ch * half, (ch + 1) * half)
        r.dx1[rows, :] = r.dx2[rows, :] + norm_back(1, r.x1[rows, :], rs_wait(R_CHAIN, ch), ch)
        r.dz1[part_of(seq, ch), :] = r.dx1[rows, :].astype(BF16)
        ag_start(G_DZ1, r.dz1.at[own], r.dz1, ch)
    rs_sent(R_CHAIN)
    up.pop(0)()
    down.pop(0)()
    ag_forward(G_DZ1, r.dz1)
    ag_wait(G_DZ1, r.dz1)
    r.do[...] = nt(r.dz1[...], w[SELF_OUT][...]).astype(BF16)
    grad[SELF_OUT][...] = tn(r.o[...], r.dz1[...]).astype(BF16)
    f_start(SELF_OUT)
    ag_sent(G_A2, r.a2.at[own], r.a2)
    rs_start(R_MEMORY, lambda at: nt(r.dk[at, :], w[CROSS][1]) + nt(r.dv[at, :], w[CROSS][2]))
    attend_back(r.q, r.k, r.v, r.do, r.p, r.dq, r.dk, r.dv, True)
    for n, right in enumerate((r.dq, r.dk, r.dv)):
        grad[SELF][n] = tn(r.a1[...], right[...]).astype(BF16)
    y_start(*SELF_UNITS)
    up.pop(0)()
    rs_start(
        R_CHAIN, lambda at: nt(r.dq[at, :], w[SELF][0]) + nt(r.dk[at, :], w[SELF][1]) + nt(r.dv[at, :], w[SELF][2])
    )
    down.pop(0)()
    up.pop(0)()
    cross_out, cross = moved_steps(CROSS_OUT), unit_steps(*CROSS_UNITS)
    self_out, selves = moved_steps(SELF_OUT), unit_steps(*SELF_UNITS)
    up.pop(0)()
    for ch in range(2):
        rows = slice(ch * half, (ch + 1) * half)
        back_term = norm_back(0, r.all_tokens[part_of(seq, ch), :].astype(F32), rs_wait(R_CHAIN, ch), ch)
        r.input_grad[rows, :] = r.dx1[rows, :] + back_term
    r.small[1] = r.norm_terms[...]
    small_start(1, 2)
    ag_sent(G_DZ2, r.dz2.at[own], r.dz2)
    rs_start(R_MIXED, lambda at: nn(r.g[at, :], w[DOWN][...]))
    for step in cross_out[:-2]:
        step()
    for ch in range(2):
        r.memory_grad[ch * half : (ch + 1) * half, :] = rs_wait(R_MEMORY, ch)
    small_wait(1, 2)
    small_start(1, 0)
    cross.pop(0)()
    up.pop(0)()
    cross.pop(0)()
    for step in cross_out[-2:]:
        step()
    cross.pop(0)()
    small_wait(1, 0)
    small_start(1, 1)
    cross.pop(0)()
    for step in self_out[:-2]:
        step()
    cross.pop(0)()
    selves.pop(0)()
    for step in self_out[-2:]:
        step()
    for ch in range(2):
        rows = slice(ch * half, (ch + 1) * half)
        live_row = (seq * Tl + ch * half + lax.broadcasted_iota(jnp.int32, (half, 1), 0)) < token_live
        r.mixed[rows, :] = jnp.where(live_row, r.x2[rows, :] + rs_wait(R_MIXED, ch), 0.0).astype(BF16)
    selves.pop(0)()
    selves.pop(0)()
    small_wait(1, 1)
    picked = lax.dot_general(
        r.small[1],
        placed.astype(F32),
        (((1,), (1,)), ((), ())),
        precision=lax.Precision.HIGHEST,
        preferred_element_type=F32,
    )
    r.gains_grad[...] = picked[0:3]
    r.biases_grad[...] = picked[3:6]
    for g in MOVED:
        s_wait(g)
    for step in (*down, *up, *cross, *selves):
        step()

    for i in (R_CHAIN, R_MIXED, R_MEMORY):
        rs_sent(i)
    for i, piece, everyone in given[:2]:
        ag_sent(i, piece, everyone)
    ag_sent(G_DZ1, r.dz1.at[own], r.dz1)
    for u in range(len(UNITS)):
        w_sent(u)
        z_sent(u)
    for g in MOVED:
        m_sent(g)
        v_sent(g)


def layer_call(A, B, S, rows, weights, norms, counts):
    V = pltpu.VMEM
    Tl, D = rows[0].shape
    T = Tl * S
    Dl = weights[SELF].shape[2]
    Fl = weights[UP].shape[1]
    pages = A * B
    R = pages // S
    heads = Dl // HEAD_DIM
    shards = [x.shape for x in weights]
    full = []
    for g, s in enumerate(shards):
        if g in (SELF, CROSS):
            full.append((s[0], s[1] * pages, s[2]))
        elif g == UP:
            full.append((s[0] * pages, s[1]))
        else:
            full.append((s[0] * R, s[1] * S))
    hbm, vmem, smem = (pl.BlockSpec(memory_space=m) for m in (pl.ANY, V, pltpu.SMEM))
    shape = jax.ShapeDtypeStruct
    dma = pltpu.SemaphoreType.DMA
    small_slots = S + A + B - 3
    units = len(UNITS)
    row_ref, wide_ref = V((T, D), BF16), V((T, Dl), BF16)
    own_ref, hidden_ref = V((Tl, D), F32), V((T, Fl), BF16)
    operands = dict(
        tokens=rows[0],
        memory=rows[1],
        cotangent=rows[2],
        ins=list(weights),
        norm_gains=norms[0],
        norm_biases=norms[1],
        token_counts=counts[0],
        patch_counts=counts[1],
    )
    specs = dict(
        tokens=hbm, memory=hbm, cotangent=hbm, ins=[hbm] * 6, norm_gains=vmem, norm_biases=vmem, token_counts=smem, patch_counts=smem
    )
    results = dict(
        mixed=shape((Tl, D), BF16),
        input_grad=shape((Tl, D), F32),
        memory_grad=shape((Tl, D), F32),
        outs=[shape(s, F32) for s in shards],
        gains_grad=shape(norms[0].shape, F32),
        biases_grad=shape(norms[1].shape, F32),
    )
    scratch = dict(
        w=[V(s, BF16) for s in full],
        grad=[V(s, BF16) for s in full],
        rb=[V((B - 1, A, *shards[g][-2:]), BF16) for g, _ in UNITS],
        zz=[V((A + 1, *shards[g][-2:]), BF16) for g, _ in UNITS],
        fb=[V((B - 1, S, *shards[g]), BF16) for g in MOVED],
        vv=[V((2, S, *shards[g]), BF16) for g in MOVED],
        back=[V(shards[g], BF16) for g in MOVED],
        all_tokens=row_ref,
        all_memory=row_ref,
        dyr=row_ref,
        a1=row_ref,
        a2=row_ref,
        a3=row_ref,
        dz2=row_ref,
        q=wide_ref,
        k=wide_ref,
        v=wide_ref,
        o=wide_ref,
        qc=wide_ref,
        kc=wide_ref,
        vc=wide_ref,
        oc=wide_ref,
        do=wide_ref,
        dq=wide_ref,
        dk=wide_ref,
        dv=wide_ref,
        p=V((heads, T, T), BF16),
        pc=V((heads, T, T), BF16),
        g=hidden_ref,
        du=hidden_ref,
        slope=V((T, Fl), F32),
        x1=own_ref,
        x2=own_ref,
        dx1=own_ref,
        dx2=own_ref,
        dk_sum=V((T, LANES), F32),
        dv_sum=V((T, LANES), F32),
        chain_part=row_ref,
        got=[V((S - 1, Tl, D), BF16)] * 3,
        small=V((2, 8, D), F32),
        small_got=V((2, small_slots, 8, D), F32),
        norm_terms=V((8, D), F32),
        ag_send=dma((7, 2, S - 1)),
        ag_recv=dma((7, 2, S)),
        rs_send=dma((3, 2, S - 1)),
        rs_recv=dma((3, 2, S - 1)),
        sm_send=dma((2, small_slots)),
        sm_recv=dma((2, small_slots)),
        ld_sem=dma((3,)),
        w_send=dma((units, pages, 4)),
        w_recv=dma((units, pages)),
        w_local=dma((units,)),
        y_send=dma((units, B - 1, A)),
        y_recv=dma((units, B - 1, A)),
        z_send=dma((units, A)),
        z_recv=dma((units, A + 1)),
        m_gave=dma((3,)),
        m_got=dma((3, S)),
        m_send=dma((3, S, B + 1)),
        m_recv=dma((3, R, S)),
        f_send=dma((3, B - 1, S)),
        f_recv=dma((3, B - 1, S)),
        v_send=dma((3, S)),
        v_recv=dma((3, 2, S)),
        s_send=dma((3, S)),
        s_recv=dma((3,)),
    )
    parts = [jax.tree.flatten(part) for part in (operands, specs, results, scratch)]
    values, in_specs, out_shape, scratch_shapes = (leaves for leaves, _ in parts)
    ends = [len(values), len(values) + len(out_shape)]

    def kernel(*refs):
        held = (refs[: ends[0]], refs[ends[0] : ends[1]], refs[ends[1] :])
        r = types.SimpleNamespace()
        for (_, tree), some in zip((parts[0], parts[2], parts[3]), held):
            vars(r).update(jax.tree.unflatten(tree, some))
        layer_kernel(A, B, S, r)

    found = pl.pallas_call(
        kernel,
        out_shape=out_shape,
        in_specs=in_specs,
        out_specs=[vmem] * len(out_shape),
        scratch_shapes=scratch_shapes,
        compiler_params=pltpu.CompilerParams(
            collective_id=0, has_side_effects=True, vmem_limit_bytes=62 * 2**20
        ),
        name="layer",
    )(*values)
    return jax.tree.unflatten(parts[2][1], found)


def keep_kernel(*refs):
    *arrays, sems = refs
    count = len(arrays) // 3
    given, kept, held = (arrays[n * count : (n + 1) * count] for n in range(3))
    loads = [pltpu.make_async_copy(given[n], held[n], sems.at[0, n]) for n in range(count)]
    stores = [pltpu.make_async_copy(held[n], kept[n], sems.at[1, n]) for n in range(count)]
    for load in loads:
        load.start()
    for load, store in zip(loads, stores):
        load.wait()
        store.start()
    for store in stores:
        store.wait()


def keep(*arrays):
    hbm = pl.BlockSpec(memory_space=pl.ANY)
    return pl.pallas_call(
        keep_kernel,
        out_shape=[jax.ShapeDtypeStruct(x.shape, x.dtype) for x in arrays],
        in_specs=[hbm] * len(arrays),
        out_specs=[hbm] * len(arrays),
        scratch_shapes=[pltpu.VMEM(x.shape, x.dtype) for x in arrays]
        + [pltpu.SemaphoreType.DMA((2, len(arrays)))],
        name="keep",
    )(*arrays)


def per_device(
    tokens,
    memory,
    cotangent,
    self_qkv,
    self_out,
    cross_qkv,
    cross_out,
    up_weight,
    down_weight,
    norm_gains,
    norm_biases,
    token_counts,
    patch_counts,
):
    pages = lax.axis_size("page")
    parts = lax.axis_size("seq")
    wide = 2 if pages == 8 else 8
    found = layer_call(
        pages // wide,
        wide,
        parts,
        (tokens[0], memory[0], cotangent[0]),
        (self_qkv, self_out, cross_qkv, cross_out, up_weight, down_weight),
        (norm_gains, norm_biases),
        (token_counts, patch_counts),
    )
    return keep(
        found["mixed"][None],
        found["input_grad"][None],
        found["memory_grad"][None],
        *found["outs"],
        found["gains_grad"],
        found["biases_grad"],
    )


def solution(mesh):
    rows = P("page", "seq", None)
    stack = P(None, "page", "seq")
    flat = P("page", "seq")
    norm = P(None, ("page", "seq"))
    counts = P("page")
    return jax.shard_map(
        per_device,
        mesh=mesh,
        in_specs=(rows, rows, rows, stack, flat, stack, flat, flat, flat, norm, norm, counts, counts),
        out_specs=(rows, rows, rows, stack, flat, stack, flat, flat, flat, norm, norm),
        check_vma=False,
    )
```

```python
import types

import jax
import jax.numpy as jnp
from jax import lax
from jax.experimental import pallas as pl
from jax.experimental.pallas import tpu as pltpu
from jax.sharding import PartitionSpec as P

HEAD_DIM = 64
F32 = jnp.float32
BF16 = jnp.bfloat16
MESH = pl.DeviceIdType.MESH
SELF, SELF_OUT, CROSS, CROSS_OUT, UP, DOWN = range(6)
MOVED = (SELF_OUT, CROSS_OUT, DOWN)
QUARTERS = 4
UNITS = tuple((g, n) for g, count in ((SELF, 3), (CROSS, 3), (UP, QUARTERS)) for n in range(count))
SELF_UNITS, CROSS_UNITS, UP_UNITS = (0, 1, 2), (3, 4, 5), (6, 7, 8, 9)
G_TOKENS, G_MEMORY, G_COT, G_A2, G_A3, G_DZ2, G_DZ1 = range(7)
R_CHAIN, R_MIXED, R_MEMORY = range(3)
LANES = 128


def nn(left, right):
    return lax.dot_general(left, right, (((1,), (0,)), ((), ())), preferred_element_type=F32)


def nt(left, right):
    return lax.dot_general(left, right, (((1,), (1,)), ((), ())), preferred_element_type=F32)


def tn(left, right):
    return lax.dot_general(left, right, (((0,), (0,)), ((), ())), preferred_element_type=F32)


def rows_at(start, size):
    return pl.ds(pl.multiple_of(start, size), size)


def normed(values):
    center = values - jnp.mean(values, axis=-1, keepdims=True)
    rate = lax.rsqrt(jnp.mean(center * center, axis=-1, keepdims=True) + 1e-05)
    return center * rate, rate


def gelu_pair(values):
    chance = 0.5 + 0.5 * lax.erf(values * 0.7071067811865476)
    density = jnp.exp(-0.5 * values * values) * 0.3989422804014327
    return values * chance, chance + values * density


def layer_kernel(A, B, S, r):
    r.dz1 = r.a3
    r.part = [r.chain_part, r.dz2, r.a2]
    ins, w, grad, outs = r.ins, r.w, r.grad, r.outs
    page, seq = lax.axis_index("page"), lax.axis_index("seq")
    a, b = lax.div(page, B), lax.rem(page, B)
    R = A * B // S
    Tl, D = r.tokens.shape
    T = Tl * S
    Dl = ins[SELF].shape[2]
    Fl = ins[UP].shape[1]
    Fq = Fl // QUARTERS
    own = rows_at(seq * Tl, Tl)
    shelf, collector = lax.rem(page, R), lax.div(page, R)
    collects = seq == collector
    a0, b0 = lax.div(seq * R, B), lax.rem(seq * R, B)
    mine = b - b0
    holds = (mine >= 0) & (mine < R)

    def remote(src, dst, send, recv, device):
        return pltpu.make_async_remote_copy(
            src_ref=src, dst_ref=dst, send_sem=send, recv_sem=recv, device_id=device, device_id_type=MESH
        )

    def landed(dst, recv):
        remote(dst, dst, recv, recv, (page, seq)).wait_recv()

    barrier = pltpu.get_barrier_semaphore()

    def greet(device):
        pl.semaphore_signal(barrier, inc=1, device_id=device, device_id_type=MESH)

    for k in range(1, S):
        greet((page, lax.rem(seq + k, S)))
    for k in range(1, B):
        greet((a * B + lax.rem(b + k, B), seq))
    for k in range(1, A):
        greet((lax.rem(a + k, A) * B + b, seq))

    pl.semaphore_wait(barrier, S + A + B - 3)

    X = S // 2
    chip, core = lax.div(seq, 2), lax.rem(seq, 2)
    sibling = chip * 2 + 1 - core
    half = Tl // 2

    def part_of(source, ch):
        return rows_at(source * Tl + ch * half, half)

    def chip_at(dx):
        return lax.rem(chip + dx, X)

    def ag_copy(i, src, dst, ch, n):
        source = chip_at(2 * X - 1 - n) * 2 + core if n >= X else seq
        mine = dst.at[part_of(source, ch)] if n >= X else src.at[rows_at(ch * half, half)]
        to = chip_at(n) * 2 + core if 0 < n < X else sibling
        return remote(
            mine, dst.at[part_of(source, ch)], r.ag_send.at[i, ch, n], r.ag_recv.at[i, ch, source], (page, to)
        )

    def ag_start(i, src, dst, ch):
        for n in (*range(1, X), 0):
            ag_copy(i, src, dst, ch, n).start()

    def ag_begin(i, src, dst):
        for ch in range(2):
            ag_start(i, src, dst, ch)

    def ag_forward(i, dst):
        for ch in range(2):
            for n in range(X, 2 * X - 1):
                source = chip_at(2 * X - 1 - n) * 2 + core
                landed(dst.at[part_of(source, ch)], r.ag_recv.at[i, ch, source])
                ag_copy(i, None, dst, ch, n).start()

    def ag_wait(i, dst):
        for ch in range(2):
            for x in range(X):
                source = 2 * x + 1 - core
                landed(dst.at[part_of(source, ch)], r.ag_recv.at[i, ch, source])

    def ag_sent(i, src, dst):
        for ch in range(2):
            for n in range(2 * X - 1):
                ag_copy(i, src, dst, ch, n).wait_send()

    def rs_copy(i, x, ch):
        return remote(
            r.part[i].at[part_of(x * 2 + 1 - core, ch)],
            r.got[i].at[x, rows_at(ch * half, half)],
            r.rs_send.at[i, ch, x],
            r.rs_recv.at[i, ch, x],
            (page, sibling),
        )

    def rs_far(i, dx, ch):
        to = chip_at(dx) * 2 + core
        slot = X + dx - 1
        return remote(
            r.part[i].at[part_of(to, ch)],
            r.got[i].at[slot, rows_at(ch * half, half)],
            r.rs_send.at[i, ch, slot],
            r.rs_recv.at[i, ch, slot],
            (page, to),
        )

    def rs_start(i, term):
        part, got = r.part[i], r.got[i]
        for n in range(1, X + 1):
            x = chip_at(n)
            at = rows_at((x * 2 + 1 - core) * Tl, Tl)
            part[at, :] = term(at).astype(BF16)
            for ch in range(2):
                rs_copy(i, x, ch).start()
        for dx in range(1, X):
            x = chip_at(dx)
            at = rows_at((x * 2 + core) * Tl, Tl)
            mine = term(at)
            for ch in range(2):
                rs_copy(i, x, ch).wait_recv()
                other = got[x, ch * half : (ch + 1) * half, :].astype(F32)
                part[part_of(x * 2 + core, ch), :] = (mine[ch * half : (ch + 1) * half] + other).astype(BF16)
                rs_far(i, dx, ch).start()
        part[own, :] = term(own).astype(BF16)

    def rs_wait(i, ch):
        rows = slice(ch * half, (ch + 1) * half)
        rs_copy(i, chip, ch).wait_recv()
        total = r.part[i][part_of(seq, ch), :].astype(F32) + r.got[i][chip, rows, :].astype(F32)
        for dx in range(1, X):
            rs_far(i, dx, ch).wait_recv()
            total = total + r.got[i][X + dx - 1, rows, :].astype(F32)
        return total

    def rs_sent(i):
        for ch in range(2):
            for x in range(X):
                rs_copy(i, x, ch).wait_send()
            for dx in range(1, X):
                rs_far(i, dx, ch).wait_send()

    def small_copies(i, level):
        count, base, device = (
            (B, 0, lambda k: (a * B + lax.rem(b + k, B), seq)),
            (A, B - 1, lambda k: (lax.rem(a + k, A) * B + b, seq)),
            (S, A + B - 2, lambda k: (page, lax.rem(seq + k, S))),
        )[level]
        return [
            remote(
                r.small.at[i],
                r.small_got.at[i, base + k - 1],
                r.sm_send.at[i, base + k - 1],
                r.sm_recv.at[i, base + k - 1],
                device(k),
            )
            for k in range(1, count)
        ], base

    def small_start(i, level):
        for copy in small_copies(i, level)[0]:
            copy.start()

    def small_wait(i, level):
        copies, base = small_copies(i, level)
        for copy in copies:
            copy.wait()
        total = r.small[i]
        for k in range(len(copies)):
            total = total + r.small_got[i, base + k]
        r.small[i] = total

    def rows_of(arrays, u, j):
        g, n = UNITS[u]
        size = ins[g].shape[-2]
        at = rows_at(j * size, size)
        return arrays[g].at[at, n * Fq : (n + 1) * Fq] if g == UP else arrays[g].at[n, at, :]

    def whole_of(arrays, u):
        g, n = UNITS[u]
        return arrays[g].at[:, n * Fq : (n + 1) * Fq] if g == UP else arrays[g].at[n]

    turned = UP_UNITS[2:] if B == 2 else ()
    turned_back = UP_UNITS[3:] if B == 2 else ()
    beside = a * B + 1 - b

    def w_copy(u, j, way, src=None):
        place = rows_of(w, u, j)
        device = (page + (-B, B, -1, 1)[way], seq)
        return remote(place if src is None else src, place, r.w_send.at[u, j, way], r.w_recv.at[u, j], device)

    ways = (a > 0, a < A - 1, b > 0, b < B - 1)

    def w_forward(u, j, along, src=None):
        for way in along:
            @pl.when(ways[way])
            def _():
                w_copy(u, j, way, src).start()

    def w_local(u):
        return pltpu.make_async_copy(whole_of(ins, u), rows_of(w, u, page), r.w_local.at[u])

    def w_first(*units, along=(0, 1, 2, 3)):
        for u in units:
            w_forward(u, page, along, whole_of(ins, u))
            if 2 in along:
                w_local(u).start()

    def w_turn(*units):
        for u in units:
            landed(rows_of(w, u, beside), r.w_recv.at[u, beside])
            w_forward(u, beside, (0, 1))

    def w_step(d, *units):
        for u in units:
            for sign, way in ((-1, 1), (1, 0)):
                @pl.when((a + sign * d >= 0) & (a + sign * d < A))
                def _():
                    for column in (page, beside) if u in turned else (page,):
                        j = column + sign * d * B
                        landed(rows_of(w, u, j), r.w_recv.at[u, j])
                        w_forward(u, j, (way,) if u in turned else (way, 2, 3))

    def w_wait(*units):
        for u in units:
            w_local(u).wait()
            for e in range(1, 1 if u in turned else B):
                for t in range(A):
                    @pl.when(b - e >= 0)
                    def _():
                        j = t * B + b - e
                        landed(rows_of(w, u, j), r.w_recv.at[u, j])
                        w_forward(u, j, (3,))

                    @pl.when(b + e < B)
                    def _():
                        j = t * B + b + e
                        landed(rows_of(w, u, j), r.w_recv.at[u, j])
                        w_forward(u, j, (2,))

    def w_sent(u):
        for t in range(A):
            for e in range(B):
                j = t * B + e
                along = ((b == e) & (t >= a), (b == e) & (t <= a), e >= b, e <= b)
                if u in turned:
                    along = (t >= a, t <= a, (b == e) & (t == a), (b == e) & (t == a))
                for way, when in enumerate(along):
                    @pl.when(when & ways[way])
                    def _():
                        w_copy(u, j, way).wait_send()

    def block(array, g, e, n):
        rows, cols = ins[g].shape
        return array.at[rows_at(e * rows, rows), rows_at(n * cols, cols)]

    def m_local(g):
        return pltpu.make_async_copy(ins[g], block(w[g], g, shelf, seq), r.m_got.at[MOVED.index(g), seq])

    def m_collect_copy(g):
        i = MOVED.index(g)
        return remote(
            ins[g], block(w[g], g, shelf, seq), r.m_gave.at[i], r.m_got.at[i, seq], (page, collector)
        )

    def m_collect(g):
        @pl.when(collects)
        def _():
            m_local(g).start()

        @pl.when(jnp.logical_not(collects))
        def _():
            m_collect_copy(g).start()

    def m_copy(g, n, way):
        i = MOVED.index(g)
        place = block(w[g], g, mine, n)
        device = (page + B, page - B)[way] if way < 2 else a * B + lax.rem(b + way - 1, B)
        return remote(place, place, r.m_send.at[i, n, way], r.m_recv.at[i, mine, n], (device, seq))

    m_ways = [holds & (a >= a0) & (a < A - 1), holds & (a <= a0) & (a > 0)] + [holds] * (B - 1)

    def m_forward(g, n):
        for way in range(B + 1):
            @pl.when(m_ways[way])
            def _():
                m_copy(g, n, way).start()

    def m_first(g, n):
        @pl.when(collects)
        def _():
            @pl.when(seq == n)
            def _():
                m_local(g).wait()

            @pl.when(seq != n)
            def _():
                landed(block(w[g], g, shelf, n), r.m_got.at[MOVED.index(g), n])

            m_forward(g, n)

    inside = (a > 0) & (a < A - 1)
    hops = jnp.abs(a - a0)

    def m_pass(g, n, hop):
        @pl.when(holds & (hops == hop))
        def _():
            landed(block(w[g], g, mine, n), r.m_recv.at[MOVED.index(g), mine, n])
            m_forward(g, n)

    def m_wait(g):
        for e in range(R):
            @pl.when(jnp.logical_not(holds) | (mine != e))
            def _():
                for n in range(S):
                    landed(block(w[g], g, e, n), r.m_recv.at[MOVED.index(g), e, n])

    def m_sent(g):
        @pl.when(jnp.logical_not(collects))
        def _():
            m_collect_copy(g).wait_send()

        for n in range(S):
            for way in range(B + 1):
                @pl.when(m_ways[way])
                def _():
                    m_copy(g, n, way).wait_send()

    low = 2 * a < A
    near = jnp.where(low, a, A - 1 - a)

    def order(m):
        if m == A - 1:
            return a
        t = jnp.where(m < A - 1 - near, A - 1 - m, m - (A - 1 - near))
        return jnp.where(low, t, A - 1 - t)

    def y_copy(u, k, t):
        other = lax.rem(b + k, B)
        return remote(
            rows_of(grad, u, t * B + other),
            r.rb[u].at[B - 1 - k, t],
            r.y_send.at[u, k - 1, t],
            r.y_recv.at[u, B - 1 - k, t],
            (a * B + other, seq),
        )

    def y_start(*units):
        for m in range(A):
            for u in units:
                for k in range(1, B):
                    y_copy(u, k, order(m)).start()

    def z_copy(u, t, sign):
        slot = jnp.where((t == a + sign) & (sign < 0), A, t)
        return remote(
            r.rb[u].at[0, t],
            r.zz[u].at[slot],
            r.z_send.at[u, t],
            r.z_recv.at[u, slot],
            (page + sign * B, seq),
        )

    def z_way(t):
        sign = jnp.where(t > a, 1, -1)
        before = a - sign
        return sign, (before >= 0) & (before < A)

    def y_sum(m, u):
        t = order(m)
        total = rows_of(grad, u, t * B + b)[...].astype(F32)
        for slot in range(B - 1):
            landed(r.rb[u].at[slot, t], r.y_recv.at[u, slot, t])
            total = total + r.rb[u][slot, t].astype(F32)
        r.rb[u][0, t] = total.astype(BF16)
        if m < A - 1:
            sign, has = z_way(t)

            @pl.when(jnp.logical_not(has))
            def _():
                z_copy(u, t, sign).start()

    def z_sum(m, u):
        t = order(m)
        sign, has = z_way(t)

        @pl.when(has)
        def _():
            landed(r.zz[u].at[t], r.z_recv.at[u, t])
            r.rb[u][0, t] = (r.rb[u][0, t].astype(F32) + r.zz[u][t].astype(F32)).astype(BF16)
            z_copy(u, t, sign).start()

    def z_total(u):
        @pl.when(a > 0)
        def _():
            landed(r.zz[u].at[a], r.z_recv.at[u, a])

        @pl.when(a < A - 1)
        def _():
            landed(r.zz[u].at[A], r.z_recv.at[u, A])

        total = r.rb[u][0, a].astype(F32)
        total = total + jnp.where(a > 0, r.zz[u][a].astype(F32), 0.0)
        total = total + jnp.where(a < A - 1, r.zz[u][A].astype(F32), 0.0)
        whole_of(outs, u)[...] = total

    def c_copy(u, t, sign, side, src):
        slot = jnp.where((t == a + sign) & (sign < 0), A, t)
        return remote(
            src,
            r.tz.at[side, slot],
            r.tz_send.at[side, t],
            r.tz_recv.at[side, slot],
            (page + sign * B, seq),
        )

    def c_own(u, t, side):
        return rows_of(grad, u, t * B + (b, 1 - b)[side])

    def c_first(u):
        for m in range(A - 1):
            t = order(m)
            sign, has = z_way(t)
            for side in range(2):
                @pl.when(jnp.logical_not(has))
                def _():
                    c_copy(u, t, sign, side, c_own(u, t, side)).start()

    def c_sum(m, u):
        t = order(m)
        sign, has = z_way(t)

        @pl.when(has)
        def _():
            for side in range(2):
                landed(r.tz.at[side, t], r.tz_recv.at[side, t])
                total = c_own(u, t, side)[...].astype(F32) + r.tz[side, t].astype(F32)
                r.ta[side, t] = total.astype(BF16)
                c_copy(u, t, sign, side, r.ta.at[side, t]).start()

    def c_turn(u):
        return remote(r.ta.at[1, a], r.tb, r.y_send.at[u, 0, 0], r.y_recv.at[u, 0, 0], (beside, seq))

    def c_total(u):
        for side in (1, 0):
            total = c_own(u, a, side)[...].astype(F32)
            for has, slot in ((a > 0, a), (a < A - 1, A)):
                @pl.when(has)
                def _():
                    landed(r.tz.at[side, slot], r.tz_recv.at[side, slot])

                total = total + jnp.where(has, r.tz[side, slot].astype(F32), 0.0)
            if side:
                r.ta[1, a] = total.astype(BF16)
                c_turn(u).start()
            else:
                whole_of(outs, u)[...] = total

    def c_end(u):
        landed(r.tb, r.y_recv.at[u, 0, 0])
        whole_of(outs, u)[...] = whole_of(outs, u)[...] + r.tb[...].astype(F32)

    def z_sent(u):
        if u in turned_back:
            c_turn(u).wait_send()
            for m in range(A - 1):
                t = order(m)
                for side in range(2):
                    c_copy(u, t, z_way(t)[0], side, c_own(u, t, side)).wait_send()
            return
        for t in range(A):
            for k in range(1, B):
                y_copy(u, k, t).wait_send()

            @pl.when(t != a)
            def _():
                z_copy(u, t, jnp.where(t > a, 1, -1)).wait_send()

    def f_copy(g, k, n):
        i = MOVED.index(g)
        other = lax.rem(b + k, B)
        return remote(
            block(grad[g], g, other - b0, n),
            r.fb[i].at[B - 1 - k, n],
            r.f_send.at[i, k - 1, n],
            r.f_recv.at[i, B - 1 - k, n],
            (a * B + other, seq),
        )

    def wanted(k):
        shelf_of = lax.rem(b + k, B) - b0
        return (shelf_of >= 0) & (shelf_of < R)

    def f_start(g):
        for n in range(S):
            for k in range(1, B):
                @pl.when(wanted(k))
                def _():
                    f_copy(g, k, n).start()

    inward = jnp.where(a > a0, -1, 1)
    from_out = holds & (a != a0) & inside
    starts_line = holds & (a != a0) & jnp.logical_not(inside)

    def v_copy(g, n):
        i = MOVED.index(g)
        slot = jnp.where((a + 1 == a0), 1, 0)
        return remote(
            r.fb[i].at[0, n], r.vv[i].at[slot, n], r.v_send.at[i, n], r.v_recv.at[i, slot, n], (page + inward * B, seq)
        )

    def s_copy(g, n):
        i = MOVED.index(g)
        return remote(r.fb[i].at[0, n], r.back[i], r.s_send.at[i, n], r.s_recv.at[i], (page, n))

    def f_sum(g, n):
        i = MOVED.index(g)

        @pl.when(holds)
        def _():
            total = block(grad[g], g, mine, n)[...].astype(F32)
            for slot in range(B - 1):
                landed(r.fb[i].at[slot, n], r.f_recv.at[i, slot, n])
                total = total + r.fb[i][slot, n].astype(F32)
            r.fb[i][0, n] = total.astype(BF16)

            @pl.when(starts_line)
            def _():
                v_copy(g, n).start()

    passed = jnp.where(a > a0, A - 1 - a, a)

    def v_sum(g, n, hop):
        i = MOVED.index(g)

        @pl.when(from_out & (passed == hop))
        def _():
            landed(r.vv[i].at[0, n], r.v_recv.at[i, 0, n])
            r.fb[i][0, n] = (r.fb[i][0, n].astype(F32) + r.vv[i][0, n].astype(F32)).astype(BF16)
            v_copy(g, n).start()

    def v_total(g, n):
        i = MOVED.index(g)

        @pl.when(collects)
        def _():
            @pl.when(a < A - 1)
            def _():
                landed(r.vv[i].at[0, n], r.v_recv.at[i, 0, n])

            @pl.when(a > 0)
            def _():
                landed(r.vv[i].at[1, n], r.v_recv.at[i, 1, n])

            total = r.fb[i][0, n].astype(F32)
            total = total + jnp.where(a < A - 1, r.vv[i][0, n].astype(F32), 0.0)
            total = total + jnp.where(a > 0, r.vv[i][1, n].astype(F32), 0.0)

            @pl.when(seq == n)
            def _():
                outs[g][...] = total

            @pl.when(seq != n)
            def _():
                r.fb[i][0, n] = total.astype(BF16)
                s_copy(g, n).start()

    def s_wait(g):
        i = MOVED.index(g)

        @pl.when(jnp.logical_not(collects))
        def _():
            landed(r.back[i], r.s_recv.at[i])
            outs[g][...] = r.back[i][...].astype(F32)

    def v_sent(g):
        for n in range(S):
            for k in range(1, B):
                @pl.when(wanted(k))
                def _():
                    f_copy(g, k, n).wait_send()

            @pl.when(starts_line | from_out)
            def _():
                v_copy(g, n).wait_send()

            @pl.when(collects & (seq != n))
            def _():
                s_copy(g, n).wait_send()

    token_live = r.token_counts[0]
    patch_live = r.patch_counts[0]
    r.norm_terms[6:8, :] = jnp.zeros((2, D), F32)
    gains = lambda k: r.small[0, k : k + 1, :]
    biases = lambda k: r.small[0, 3 + k : 4 + k, :]
    QB = min(256, T)
    lane = lax.broadcasted_iota(jnp.int32, (1, LANES), 1)
    halves = [(lane // HEAD_DIM == h) for h in range(2)]
    half_of = [half.astype(F32).astype(BF16) for half in halves]
    scale = HEAD_DIM ** (-0.5)

    def project(dst, left, weight):
        for n, (out, index) in enumerate(dst):
            out[...] = nn(left[...], weight[index]).astype(BF16)

    def attend(q, k, v, o, probs, live, causal):
        @pl.loop(0, Dl // LANES)
        def _(pair):
            cols = rows_at(pair * LANES, LANES)
            for block in range(T // QB):
                extent = (block + 1) * QB if causal else T
                rows = slice(block * QB, (block + 1) * QB)
                q2 = q[rows, cols]
                k2, v2 = k[:extent, cols], v[:extent, cols]
                at = lax.broadcasted_iota(jnp.int32, (QB, extent), 1)
                allowed = at < live
                if causal:
                    row = block * QB + lax.broadcasted_iota(jnp.int32, (QB, extent), 0)
                    allowed = allowed & (at <= row)
                found = []
                for h in range(2):
                    scores = nt(q2 * half_of[h], k2) * scale
                    scores = jnp.where(allowed, scores, -1e30)
                    raised = jnp.exp(scores - jnp.max(scores, axis=-1, keepdims=True))
                    share = (raised / jnp.sum(raised, axis=-1, keepdims=True)).astype(BF16)
                    probs[2 * pair + h, rows, :extent] = share
                    found.append(nn(share, v2))
                o[rows, cols] = jnp.where(halves[0], found[0], found[1]).astype(BF16)

    def attend_back(q, k, v, do, probs, dq, dk, dv, causal):
        @pl.loop(0, Dl // LANES)
        def _(pair):
            cols = rows_at(pair * LANES, LANES)
            r.dk_sum[...] = jnp.zeros_like(r.dk_sum)
            r.dv_sum[...] = jnp.zeros_like(r.dv_sum)
            for block in range(T // QB):
                extent = (block + 1) * QB if causal else T
                rows = slice(block * QB, (block + 1) * QB)
                q2, do2 = q[rows, cols], do[rows, cols]
                k2, v2 = k[:extent, cols], v[:extent, cols]
                dqs, dks, dvs = [], [], []
                for h in range(2):
                    share = probs[2 * pair + h, rows, :extent]
                    wide = share.astype(F32)
                    dp = nt(do2 * half_of[h], v2)
                    delta = jnp.sum(wide * dp, axis=-1, keepdims=True)
                    ds = (wide * (dp - delta)).astype(BF16)
                    dqs.append(nn(ds, k2))
                    dks.append(tn(ds, q2))
                    dvs.append(tn(share, do2))
                dq[rows, cols] = (jnp.where(halves[0], dqs[0], dqs[1]) * scale).astype(BF16)
                r.dk_sum[:extent, :] += jnp.where(halves[0], dks[0], dks[1])
                r.dv_sum[:extent, :] += jnp.where(halves[0], dvs[0], dvs[1])
            dk[:, cols] = (r.dk_sum[...] * scale).astype(BF16)
            dv[:, cols] = r.dv_sum[...].astype(BF16)

    def norm_back(k, values, incoming, ch):
        unit, rate = normed(values)
        for row, term in ((k, incoming * unit), (3 + k, incoming)):
            so_far = jnp.sum(term, axis=0, keepdims=True)
            r.norm_terms[row : row + 1, :] = so_far if ch == 0 else r.norm_terms[row : row + 1, :] + so_far
        dn = incoming * gains(k)
        return rate * (
            dn - jnp.mean(dn, axis=-1, keepdims=True) - unit * jnp.mean(dn * unit, axis=-1, keepdims=True)
        )

    def norm_own(k, values, dst, ch):
        dst[part_of(seq, ch), :] = (normed(values)[0] * gains(k) + biases(k)).astype(BF16)

    tile = min(256, Fl)
    tiles = Fl // tile

    few = r.norm_gains.shape[1]
    at_feature = lax.broadcasted_iota(jnp.int32, (few, D), 1)
    placed = at_feature == lax.broadcasted_iota(jnp.int32, (few, D), 0) + (page * S + seq) * few
    plan = []

    def when(time, *steps):
        plan.extend((time, step) for step in steps)

    def each_row_part(step):
        def run():
            for ch in range(2):
                step(ch, slice(ch * half, (ch + 1) * half))

        return run

    def w_moved(g, first, hop_time, gap):
        for n in range(S):
            when(first + n * gap, lambda n=n: m_first(g, n))
            for hop in range(1, A):
                when(first + n * gap + hop * hop_time, lambda n=n, hop=hop: m_pass(g, n, hop))

    def g_moved(g, first, hop_time, gap, late):
        for n in range(S):
            time = first + n * gap
            when(time, lambda n=n: f_sum(g, n))
            for hop in range(1, A - 1):
                when(time + late + hop * hop_time, lambda n=n, hop=hop: v_sum(g, n, hop))
            when(time + late + (A - 1) * hop_time, lambda n=n: v_total(g, n))

    def g_units(units, first, hop_time, gap, late):
        for place, u in enumerate(units):
            time = first + gap * place / len(units)
            for m in range(A):
                when(time + gap * m, lambda m=m, u=u: y_sum(m, u))
            for m in range(A - 2):
                when(time + gap * m + late + hop_time, lambda m=m, u=u: z_sum(m, u))
            after = time + late + 2 * hop_time
            when(max(after, time + gap * (A - 2)), lambda u=u: z_sum(A - 2, u))
            when(max(after + gap, time + gap * (A - 1)), lambda u=u: z_total(u))

    given = (
        (G_TOKENS, r.tokens, r.all_tokens), (G_MEMORY, r.memory, r.all_memory), (G_COT, r.cotangent, r.dyr)
    )
    loads = [pltpu.make_async_copy(piece, everyone.at[own], r.ld_sem.at[i]) for i, piece, everyone in given]

    def begin():
        r.small[0] = jnp.zeros((8, D), F32)
        r.small[0, 0:3, :] = nn(r.norm_gains[...], placed.astype(F32).astype(BF16))
        r.small[0, 3:6, :] = nn(r.norm_biases[...], placed.astype(F32).astype(BF16))
        small_start(0, 0)
        w_first(*SELF_UNITS)
        m_collect(SELF_OUT)
        ag_begin(*given[0])
        for load in loads:
            load.start()

    def small_next(i, level):
        small_wait(i, level)
        small_start(i, level + 1 if i == 0 else level - 1)

    def take_tokens():
        small_wait(0, 2)
        ag_wait(G_TOKENS, r.all_tokens)
        for load in loads:
            load.wait()

        @pl.loop(0, S)
        def _(n):
            at = rows_at(n * Tl, Tl)
            values = r.all_tokens[at, :].astype(F32)
            r.a1[at, :] = (normed(values)[0] * gains(0) + biases(0)).astype(BF16)

    def self_project():
        w_wait(*SELF_UNITS)
        project(((r.q, 0), (r.k, 1), (r.v, 2)), r.a1, w[SELF])

    def self_sum():
        m_wait(SELF_OUT)
        rs_start(R_CHAIN, lambda at: nn(r.o[at, :], w[SELF_OUT][...]))

    @each_row_part
    def self_add(ch, rows):
        r.x1[rows, :] = r.all_tokens[part_of(seq, ch), :].astype(F32) + rs_wait(R_CHAIN, ch)
        norm_own(1, r.x1[rows, :], r.a2, ch)
        ag_start(G_A2, r.a2.at[own], r.a2, ch)

    def memory_project():
        w_wait(*CROSS_UNITS)
        ag_wait(G_MEMORY, r.all_memory)
        project(((r.kc, 1), (r.vc, 2)), r.all_memory, w[CROSS])

    def cross_project():
        ag_wait(G_A2, r.a2)
        project(((r.qc, 0),), r.a2, w[CROSS])

    def cross_sum():
        m_wait(CROSS_OUT)
        rs_sent(R_CHAIN)
        rs_start(R_CHAIN, lambda at: nn(r.oc[at, :], w[CROSS_OUT][...]))

    def take_cotangent():
        ag_wait(G_COT, r.dyr)
        ag_sent(*given[2])

        @pl.loop(0, S)
        def _(n):
            at = rows_at(n * Tl, Tl)
            row = n * Tl + lax.broadcasted_iota(jnp.int32, (Tl, 1), 0)
            values = r.dyr[at, :].astype(F32)
            r.dyr[at, :] = jnp.where(row < token_live, values, 0.0).astype(BF16)

    @each_row_part
    def cross_add(ch, rows):
        r.x2[rows, :] = r.x1[rows, :] + rs_wait(R_CHAIN, ch)
        norm_own(2, r.x2[rows, :], r.a3, ch)
        ag_start(G_A3, r.a3.at[own], r.a3, ch)

    def hidden():
        w_wait(*UP_UNITS)
        ag_wait(G_A3, r.a3)

        @pl.loop(0, tiles)
        def _(n):
            cols = rows_at(far_first(n) * tile, tile)
            out, slope = gelu_pair(nn(r.a3[...], w[UP][:, cols]))
            r.g[:, cols] = out.astype(BF16)
            r.slope[:, cols] = slope
            grad[DOWN][cols, :] = tn(r.g[:, cols], r.dyr[...]).astype(BF16)

            @pl.when(n == tiles * (R - 1) // R - 1)
            def _():
                f_start(DOWN)

    def far_first(n):
        shelf_last = jnp.where(holds, mine + 1, 0) * (tiles // R)
        return lax.rem(n + shelf_last, tiles)

    straight = tuple(u for u in UP_UNITS if u not in turned)
    when(0, begin)
    when(6, lambda: w_step(1, *SELF_UNITS))
    when(8, lambda: small_next(0, 0), lambda: m_collect(CROSS_OUT), lambda: ag_begin(*given[1]), lambda: m_collect(DOWN))
    when(12, lambda: w_step(2, *SELF_UNITS))
    w_moved(SELF_OUT, 13, 4, 0.1)
    when(15, lambda: small_next(0, 1), lambda: ag_forward(G_TOKENS, r.all_tokens), lambda: ag_begin(*given[2]))
    when(16.5, lambda: w_step(3, *SELF_UNITS))
    when(17.5, lambda: w_first(*CROSS_UNITS))
    when(21, lambda: w_first(*turned, along=(2, 3)))
    when(22, lambda: w_first(*straight))
    when(23.5, lambda: w_step(1, *CROSS_UNITS))
    when(24.5, take_tokens)
    when(27, self_project)
    when(29, lambda: w_step(2, *CROSS_UNITS))
    w_moved(CROSS_OUT, 30, 5, 0.1)
    when(31, lambda: ag_forward(G_MEMORY, r.all_memory))
    when(32, lambda: attend(r.q, r.k, r.v, r.o, r.p, token_live, True))
    when(34.5, lambda: w_step(3, *CROSS_UNITS))
    when(36, self_sum)
    when(37, lambda: w_step(1, *straight))
    w_moved(DOWN, 37.5, 7.5, 4.5)
    when(42, lambda: ag_forward(G_COT, r.dyr))
    when(43, lambda: w_step(2, *straight))
    when(46, self_add)
    when(47, lambda: w_first(*turned, along=(0, 1)))
    when(48, memory_project)
    when(49, lambda: w_step(3, *straight))
    when(50, lambda: w_turn(*turned))
    when(52, lambda: ag_forward(G_A2, r.a2))
    when(53.2, cross_project)
    when(54, lambda: attend(r.qc, r.kc, r.vc, r.oc, r.pc, patch_live, False))
    when(57, cross_sum)
    when(58, lambda: w_step(1, *turned))
    when(61, take_cotangent)
    when(67, cross_add)
    when(66, lambda: w_step(2, *turned))
    when(73, lambda: w_step(3, *turned))
    when(75, lambda: ag_forward(G_A3, r.a3))
    when(78, hidden)

    def hidden_back():
        m_wait(DOWN)

        @pl.loop(0, tiles)
        def _(n):
            cols = rows_at(n * tile, tile)
            r.du[:, cols] = (nt(r.dyr[...], w[DOWN][cols, :]) * r.slope[:, cols]).astype(BF16)

        straight_columns = (QUARTERS - len(turned_back)) * Fq
        for part in (slice(straight_columns, Fl), slice(0, straight_columns)):
            if part.start == part.stop:
                continue

            @pl.loop(0, D // 256)
            def _(n):
                cols = rows_at(n * 256, 256)
                grad[UP][cols, part] = tn(r.a3[:, cols], r.du[:, part]).astype(BF16)

            if part.start:
                for u in turned_back:
                    c_first(u)
        y_start(*UP_UNITS[: QUARTERS - len(turned_back)])

    def hidden_sum():
        ag_sent(G_A3, r.a3.at[own], r.a3)
        rs_sent(R_CHAIN)
        rs_start(R_CHAIN, lambda at: nt(r.du[at, :], w[UP][...]))

    @each_row_part
    def hidden_add(ch, rows):
        back_term = norm_back(2, r.x2[rows, :], rs_wait(R_CHAIN, ch), ch)
        r.dx2[rows, :] = r.dyr[part_of(seq, ch), :].astype(F32) + back_term
        r.dz2[part_of(seq, ch), :] = r.dx2[rows, :].astype(BF16)
        ag_start(G_DZ2, r.dz2.at[own], r.dz2, ch)

    def cross_back():
        ag_wait(G_DZ2, r.dz2)
        grad[CROSS_OUT][...] = tn(r.oc[...], r.dz2[...]).astype(BF16)
        f_start(CROSS_OUT)
        r.do[...] = nt(r.dz2[...], w[CROSS_OUT][...]).astype(BF16)
        attend_back(r.qc, r.kc, r.vc, r.do, r.pc, r.dq, r.dkc, r.dvc, False)

    def cross_back_sum():
        rs_sent(R_CHAIN)
        rs_start(R_CHAIN, lambda at: nt(r.dq[at, :], w[CROSS][0]))

    def cross_grad():
        for n, (left, right) in enumerate(((r.a2, r.dq), (r.all_memory, r.dkc), (r.all_memory, r.dvc))):
            grad[CROSS][n] = tn(left[...], right[...]).astype(BF16)
        y_start(*CROSS_UNITS)

    @each_row_part
    def cross_back_add(ch, rows):
        r.dx1[rows, :] = r.dx2[rows, :] + norm_back(1, r.x1[rows, :], rs_wait(R_CHAIN, ch), ch)
        r.dz1[part_of(seq, ch), :] = r.dx1[rows, :].astype(BF16)
        ag_start(G_DZ1, r.dz1.at[own], r.dz1, ch)

    def self_back():
        ag_wait(G_DZ1, r.dz1)
        grad[SELF_OUT][...] = tn(r.o[...], r.dz1[...]).astype(BF16)
        f_start(SELF_OUT)
        r.do[...] = nt(r.dz1[...], w[SELF_OUT][...]).astype(BF16)
        attend_back(r.q, r.k, r.v, r.do, r.p, r.dq, r.dk, r.dv, True)
        for n, right in enumerate((r.dq, r.dk, r.dv)):
            grad[SELF][n] = tn(r.a1[...], right[...]).astype(BF16)
        y_start(*SELF_UNITS)

    def self_back_sum():
        rs_sent(R_CHAIN)
        rs_start(
            R_CHAIN,
            lambda at: nt(r.dq[at, :], w[SELF][0]) + nt(r.dk[at, :], w[SELF][1]) + nt(r.dv[at, :], w[SELF][2]),
        )

    def memory_sum():
        ag_sent(G_A2, r.a2.at[own], r.a2)
        rs_start(R_MEMORY, lambda at: nt(r.dkc[at, :], w[CROSS][1]) + nt(r.dvc[at, :], w[CROSS][2]))

    @each_row_part
    def input_add(ch, rows):
        back_term = norm_back(0, r.all_tokens[part_of(seq, ch), :].astype(F32), rs_wait(R_CHAIN, ch), ch)
        r.input_grad[rows, :] = r.dx1[rows, :] + back_term

    def small_last():
        r.small[1] = r.norm_terms[...]
        small_start(1, 2)

    def mixed_sum():
        ag_sent(G_DZ2, r.dz2.at[own], r.dz2)
        rs_start(R_MIXED, lambda at: nn(r.g[at, :], w[DOWN][...]))

    @each_row_part
    def memory_add(ch, rows):
        r.memory_grad[rows, :] = rs_wait(R_MEMORY, ch)

    @each_row_part
    def mixed_add(ch, rows):
        live_row = (seq * Tl + ch * half + lax.broadcasted_iota(jnp.int32, (half, 1), 0)) < token_live
        r.mixed[rows, :] = jnp.where(live_row, r.x2[rows, :] + rs_wait(R_MIXED, ch), 0.0).astype(BF16)

    def norms_out():
        small_wait(1, 0)
        picked = lax.dot_general(
            r.small[1],
            placed.astype(F32),
            (((1,), (1,)), ((), ())),
            precision=lax.Precision.HIGHEST,
            preferred_element_type=F32,
        )
        r.gains_grad[...] = picked[0:3]
        r.biases_grad[...] = picked[3:6]

    when(87, hidden_back)
    when(91, hidden_sum)
    if turned_back:
        when(99, lambda: c_sum(0, UP_UNITS[3]))
        when(102, lambda: c_sum(1, UP_UNITS[3]))
        when(104, lambda: c_sum(2, UP_UNITS[3]))
        when(110, lambda: c_total(UP_UNITS[3]))
        when(138, lambda: c_end(UP_UNITS[3]))
        g_moved(DOWN, 97, 7.2, 5.6, 5)
        g_units(UP_UNITS[:3], 120.5, 4.5, 4.2, 7)
    else:
        g_moved(DOWN, 97, 7.2, 5.6, 0)
        g_units(UP_UNITS, 120.5, 4.5, 5.6, 0)
    when(102, hidden_add)
    when(106.5, lambda: ag_forward(G_DZ2, r.dz2))
    when(108.5, cross_back)
    when(114, cross_back_sum)
    when(116, cross_grad)
    when(124, cross_back_add)
    when(130, lambda: ag_forward(G_DZ1, r.dz1))
    when(132, self_back)
    when(137, self_back_sum)
    g_moved(CROSS_OUT, 134, 3.2, 1.4, 6)
    when(142, memory_sum)
    g_units(CROSS_UNITS, 141.5, 6, 4.2, 4)
    when(146, input_add)
    when(147, small_last)
    when(150, mixed_sum)
    when(152, lambda: small_next(1, 2))
    when(154, memory_add)
    g_moved(SELF_OUT, 157, 3.2, 1.4, 2)
    when(162, lambda: small_next(1, 1))
    when(166, mixed_add)
    g_units(SELF_UNITS, 168, 6, 4.2, 0)
    when(177, lambda: s_wait(DOWN), lambda: s_wait(CROSS_OUT))
    when(181, lambda: s_wait(SELF_OUT), norms_out)

    for _, step in sorted(plan, key=lambda entry: entry[0]):
        step()

    for i in (R_CHAIN, R_MIXED, R_MEMORY):
        rs_sent(i)
    for i, piece, everyone in given[:2]:
        ag_sent(i, piece, everyone)
    ag_sent(G_DZ1, r.dz1.at[own], r.dz1)
    for u in range(len(UNITS)):
        w_sent(u)
        z_sent(u)
    for g in MOVED:
        m_sent(g)
        v_sent(g)


def layer_call(A, B, S, rows, weights, norms, counts):
    V = pltpu.VMEM
    Tl, D = rows[0].shape
    T = Tl * S
    Dl = weights[SELF].shape[2]
    Fl = weights[UP].shape[1]
    pages = A * B
    R = pages // S
    heads = Dl // HEAD_DIM
    shards = [x.shape for x in weights]
    full = []
    for g, s in enumerate(shards):
        if g in (SELF, CROSS):
            full.append((s[0], s[1] * pages, s[2]))
        elif g == UP:
            full.append((s[0] * pages, s[1]))
        else:
            full.append((s[0] * R, s[1] * S))
    hbm, vmem, smem = (pl.BlockSpec(memory_space=m) for m in (pl.ANY, V, pltpu.SMEM))
    shape = jax.ShapeDtypeStruct
    dma = pltpu.SemaphoreType.DMA
    small_slots = S + A + B - 3
    units = len(UNITS)
    pieces = [(shards[g][0], Fl // QUARTERS) if g == UP else shards[g][1:] for g, _ in UNITS]
    turn = pieces[-1]
    if B == 2:
        pieces[-1] = (16, LANES)
    else:
        turn = (16, LANES)
    row_ref, wide_ref = V((T, D), BF16), V((T, Dl), BF16)
    own_ref, hidden_ref = V((Tl, D), F32), V((T, Fl), BF16)
    operands = dict(
        tokens=rows[0],
        memory=rows[1],
        cotangent=rows[2],
        ins=list(weights),
        norm_gains=norms[0],
        norm_biases=norms[1],
        token_counts=counts[0],
        patch_counts=counts[1],
    )
    specs = dict(
        tokens=hbm, memory=hbm, cotangent=hbm, ins=[hbm] * 6, norm_gains=vmem, norm_biases=vmem, token_counts=smem, patch_counts=smem
    )
    results = dict(
        mixed=shape((Tl, D), BF16),
        input_grad=shape((Tl, D), F32),
        memory_grad=shape((Tl, D), F32),
        outs=[shape(s, F32) for s in shards],
        gains_grad=shape(norms[0].shape, F32),
        biases_grad=shape(norms[1].shape, F32),
    )
    scratch = dict(
        w=[V(s, BF16) for s in full],
        grad=[V(s, BF16) for s in full],
        rb=[V((B - 1, A, *piece), BF16) for piece in pieces],
        zz=[V((A + 1, *piece), BF16) for piece in pieces],
        ta=V((2, A, *turn), BF16),
        tz=V((2, A + 1, *turn), BF16),
        tb=V(turn, BF16),
        fb=[V((B - 1, S, *shards[g]), BF16) for g in MOVED],
        vv=[V((2, S, *shards[g]), BF16) for g in MOVED],
        back=[V(shards[g], BF16) for g in MOVED],
        all_tokens=row_ref,
        all_memory=row_ref,
        dyr=row_ref,
        a1=row_ref,
        a2=row_ref,
        a3=row_ref,
        dz2=row_ref,
        q=wide_ref,
        k=wide_ref,
        v=wide_ref,
        o=wide_ref,
        qc=wide_ref,
        kc=wide_ref,
        vc=wide_ref,
        oc=wide_ref,
        do=wide_ref,
        dq=wide_ref,
        dk=wide_ref,
        dv=wide_ref,
        dkc=wide_ref,
        dvc=wide_ref,
        p=V((heads, T, T), BF16),
        pc=V((heads, T, T), BF16),
        g=hidden_ref,
        du=hidden_ref,
        slope=V((T, Fl), F32),
        x1=own_ref,
        x2=own_ref,
        dx1=own_ref,
        dx2=own_ref,
        dk_sum=V((T, LANES), F32),
        dv_sum=V((T, LANES), F32),
        chain_part=row_ref,
        got=[V((S - 1, Tl, D), BF16)] * 3,
        small=V((2, 8, D), F32),
        small_got=V((2, small_slots, 8, D), F32),
        norm_terms=V((8, D), F32),
        ag_send=dma((7, 2, S - 1)),
        ag_recv=dma((7, 2, S)),
        rs_send=dma((3, 2, S - 1)),
        rs_recv=dma((3, 2, S - 1)),
        sm_send=dma((2, small_slots)),
        sm_recv=dma((2, small_slots)),
        ld_sem=dma((3,)),
        w_send=dma((units, pages, 4)),
        w_recv=dma((units, pages)),
        w_local=dma((units,)),
        y_send=dma((units, B - 1, A)),
        y_recv=dma((units, B - 1, A)),
        z_send=dma((units, A)),
        z_recv=dma((units, A + 1)),
        tz_send=dma((2, A)),
        tz_recv=dma((2, A + 1)),
        m_gave=dma((3,)),
        m_got=dma((3, S)),
        m_send=dma((3, S, B + 1)),
        m_recv=dma((3, R, S)),
        f_send=dma((3, B - 1, S)),
        f_recv=dma((3, B - 1, S)),
        v_send=dma((3, S)),
        v_recv=dma((3, 2, S)),
        s_send=dma((3, S)),
        s_recv=dma((3,)),
    )
    parts = [jax.tree.flatten(part) for part in (operands, specs, results, scratch)]
    values, in_specs, out_shape, scratch_shapes = (leaves for leaves, _ in parts)
    ends = [len(values), len(values) + len(out_shape)]

    def kernel(*refs):
        held = (refs[: ends[0]], refs[ends[0] : ends[1]], refs[ends[1] :])
        r = types.SimpleNamespace()
        for (_, tree), some in zip((parts[0], parts[2], parts[3]), held):
            vars(r).update(jax.tree.unflatten(tree, some))
        layer_kernel(A, B, S, r)

    found = pl.pallas_call(
        kernel,
        out_shape=out_shape,
        in_specs=in_specs,
        out_specs=[vmem] * len(out_shape),
        scratch_shapes=scratch_shapes,
        compiler_params=pltpu.CompilerParams(
            collective_id=0, has_side_effects=True, vmem_limit_bytes=62 * 2**20
        ),
        name="layer",
    )(*values)
    return jax.tree.unflatten(parts[2][1], found)


def keep_kernel(*refs):
    *arrays, sems = refs
    count = len(arrays) // 3
    given, kept, held = (arrays[n * count : (n + 1) * count] for n in range(3))
    loads = [pltpu.make_async_copy(given[n], held[n], sems.at[0, n]) for n in range(count)]
    stores = [pltpu.make_async_copy(held[n], kept[n], sems.at[1, n]) for n in range(count)]
    for load in loads:
        load.start()
    for load, store in zip(loads, stores):
        load.wait()
        store.start()
    for store in stores:
        store.wait()


def keep(*arrays):
    hbm = pl.BlockSpec(memory_space=pl.ANY)
    return pl.pallas_call(
        keep_kernel,
        out_shape=[jax.ShapeDtypeStruct(x.shape, x.dtype) for x in arrays],
        in_specs=[hbm] * len(arrays),
        out_specs=[hbm] * len(arrays),
        scratch_shapes=[pltpu.VMEM(x.shape, x.dtype) for x in arrays]
        + [pltpu.SemaphoreType.DMA((2, len(arrays)))],
        name="keep",
    )(*arrays)


def per_device(
    tokens,
    memory,
    cotangent,
    self_qkv,
    self_out,
    cross_qkv,
    cross_out,
    up_weight,
    down_weight,
    norm_gains,
    norm_biases,
    token_counts,
    patch_counts,
):
    pages = lax.axis_size("page")
    parts = lax.axis_size("seq")
    wide = 2 if pages == 8 else 8
    found = layer_call(
        pages // wide,
        wide,
        parts,
        (tokens[0], memory[0], cotangent[0]),
        (self_qkv, self_out, cross_qkv, cross_out, up_weight, down_weight),
        (norm_gains, norm_biases),
        (token_counts, patch_counts),
    )
    return keep(
        found["mixed"][None],
        found["input_grad"][None],
        found["memory_grad"][None],
        *found["outs"],
        found["gains_grad"],
        found["biases_grad"],
    )


def solution(mesh):
    rows = P("page", "seq", None)
    stack = P(None, "page", "seq")
    flat = P("page", "seq")
    norm = P(None, ("page", "seq"))
    counts = P("page")
    return jax.shard_map(
        per_device,
        mesh=mesh,
        in_specs=(rows, rows, rows, stack, flat, stack, flat, flat, flat, norm, norm, counts, counts),
        out_specs=(rows, rows, rows, stack, flat, stack, flat, flat, flat, norm, norm),
        check_vma=False,
    )
```

```python
import types

import jax
import jax.numpy as jnp
from jax import lax
from jax.experimental import pallas as pl
from jax.experimental.pallas import tpu as pltpu
from jax.sharding import PartitionSpec as P

HEAD_DIM = 64
F32 = jnp.float32
BF16 = jnp.bfloat16
MESH = pl.DeviceIdType.MESH
SELF, SELF_OUT, CROSS, CROSS_OUT, UP, DOWN = range(6)
MOVED = (SELF_OUT, CROSS_OUT, DOWN)
QUARTERS = 4
UNITS = ((SELF, 0), (SELF, 1), (SELF, 2), (CROSS, None), *((UP, n) for n in range(QUARTERS)))
SELF_UNITS, CROSS_UNITS, UP_UNITS = (0, 1, 2), (3,), (4, 5, 6, 7)
G_TOKENS, G_MEMORY, G_COT, G_A2, G_A3, G_DZ2, G_DZ1 = range(7)
R_CHAIN, R_MIXED, R_MEMORY = range(3)
LANES = 128


def nn(left, right):
    return lax.dot_general(left, right, (((1,), (0,)), ((), ())), preferred_element_type=F32)


def nt(left, right):
    return lax.dot_general(left, right, (((1,), (1,)), ((), ())), preferred_element_type=F32)


def tn(left, right):
    return lax.dot_general(left, right, (((0,), (0,)), ((), ())), preferred_element_type=F32)


def rows_at(start, size):
    return pl.ds(pl.multiple_of(start, size), size)


def normed(values):
    center = values - jnp.mean(values, axis=-1, keepdims=True)
    rate = lax.rsqrt(jnp.mean(center * center, axis=-1, keepdims=True) + 1e-05)
    return center * rate, rate


def gelu_pair(values):
    chance = 0.5 + 0.5 * lax.erf(values * 0.7071067811865476)
    density = jnp.exp(-0.5 * values * values) * 0.3989422804014327
    return values * chance, chance + values * density


def layer_kernel(A, B, S, r):
    r.dz1 = r.a3
    r.part = [r.chain_part, r.dz2, r.a2]
    ins, w, grad, outs = r.ins, r.w, r.grad, r.sums
    page, seq = lax.axis_index("page"), lax.axis_index("seq")
    a, b = lax.div(page, B), lax.rem(page, B)
    R = A * B // S
    Tl, D = r.tokens.shape
    T = Tl * S
    Dl = ins[SELF].shape[2]
    Fl = ins[UP].shape[1]
    Fq = Fl // QUARTERS
    own = rows_at(seq * Tl, Tl)
    shelf, collector = lax.rem(page, R), lax.div(page, R)
    collects = seq == collector
    a0, b0 = lax.div(seq * R, B), lax.rem(seq * R, B)
    mine = b - b0
    holds = (mine >= 0) & (mine < R)

    def remote(src, dst, send, recv, device):
        return pltpu.make_async_remote_copy(
            src_ref=src, dst_ref=dst, send_sem=send, recv_sem=recv, device_id=device, device_id_type=MESH
        )

    def landed(dst, recv):
        remote(dst, dst, recv, recv, (page, seq)).wait_recv()

    barrier = pltpu.get_barrier_semaphore()

    def greet(device):
        pl.semaphore_signal(barrier, inc=1, device_id=device, device_id_type=MESH)

    for k in range(1, S):
        greet((page, lax.rem(seq + k, S)))
    for k in range(1, B):
        greet((a * B + lax.rem(b + k, B), seq))
    for k in range(1, A):
        greet((lax.rem(a + k, A) * B + b, seq))

    pl.semaphore_wait(barrier, S + A + B - 3)

    X = S // 2
    chip, core = lax.div(seq, 2), lax.rem(seq, 2)
    sibling = chip * 2 + 1 - core
    half = Tl // 2

    def part_of(source, ch):
        return rows_at(source * Tl + ch * half, half)

    def chip_at(dx):
        return lax.rem(chip + dx, X)

    def ag_copy(i, src, dst, ch, n):
        source = chip_at(2 * X - 1 - n) * 2 + core if n >= X else seq
        mine = dst.at[part_of(source, ch)] if n >= X else src.at[rows_at(ch * half, half)]
        to = chip_at(n) * 2 + core if 0 < n < X else sibling
        return remote(
            mine, dst.at[part_of(source, ch)], r.ag_send.at[i, ch, n], r.ag_recv.at[i, ch, source], (page, to)
        )

    def ag_start(i, src, dst, ch):
        for n in (*range(1, X), 0):
            ag_copy(i, src, dst, ch, n).start()

    def ag_begin(i, src, dst):
        for ch in range(2):
            ag_start(i, src, dst, ch)

    def ag_forward(i, dst):
        for ch in range(2):
            for n in range(X, 2 * X - 1):
                source = chip_at(2 * X - 1 - n) * 2 + core
                landed(dst.at[part_of(source, ch)], r.ag_recv.at[i, ch, source])
                ag_copy(i, None, dst, ch, n).start()

    def ag_wait(i, dst):
        for ch in range(2):
            for x in range(X):
                source = 2 * x + 1 - core
                landed(dst.at[part_of(source, ch)], r.ag_recv.at[i, ch, source])

    def ag_sent(i, src, dst):
        for ch in range(2):
            for n in range(2 * X - 1):
                ag_copy(i, src, dst, ch, n).wait_send()

    def rs_copy(i, x, ch):
        return remote(
            r.part[i].at[part_of(x * 2 + 1 - core, ch)],
            r.got[i].at[x, rows_at(ch * half, half)],
            r.rs_send.at[i, ch, x],
            r.rs_recv.at[i, ch, x],
            (page, sibling),
        )

    def rs_far(i, dx, ch):
        to = chip_at(dx) * 2 + core
        slot = X + dx - 1
        return remote(
            r.part[i].at[part_of(to, ch)],
            r.got[i].at[slot, rows_at(ch * half, half)],
            r.rs_send.at[i, ch, slot],
            r.rs_recv.at[i, ch, slot],
            (page, to),
        )

    def rs_start(i, term):
        part, got = r.part[i], r.got[i]
        for n in range(1, X + 1):
            x = chip_at(n)
            at = rows_at((x * 2 + 1 - core) * Tl, Tl)
            part[at, :] = term(at).astype(BF16)
            for ch in range(2):
                rs_copy(i, x, ch).start()
        for dx in range(1, X):
            x = chip_at(dx)
            at = rows_at((x * 2 + core) * Tl, Tl)
            mine = term(at)
            for ch in range(2):
                rs_copy(i, x, ch).wait_recv()
                other = got[x, ch * half : (ch + 1) * half, :].astype(F32)
                part[part_of(x * 2 + core, ch), :] = (mine[ch * half : (ch + 1) * half] + other).astype(BF16)
                rs_far(i, dx, ch).start()
        part[own, :] = term(own).astype(BF16)

    def rs_wait(i, ch):
        rows = slice(ch * half, (ch + 1) * half)
        rs_copy(i, chip, ch).wait_recv()
        total = r.part[i][part_of(seq, ch), :].astype(F32) + r.got[i][chip, rows, :].astype(F32)
        for dx in range(1, X):
            rs_far(i, dx, ch).wait_recv()
            total = total + r.got[i][X + dx - 1, rows, :].astype(F32)
        return total

    def rs_sent(i):
        for ch in range(2):
            for x in range(X):
                rs_copy(i, x, ch).wait_send()
            for dx in range(1, X):
                rs_far(i, dx, ch).wait_send()

    def small_copies(i, level):
        count, base, device = (
            (B, 0, lambda k: (a * B + lax.rem(b + k, B), seq)),
            (A, B - 1, lambda k: (lax.rem(a + k, A) * B + b, seq)),
            (S, A + B - 2, lambda k: (page, lax.rem(seq + k, S))),
        )[level]
        return [
            remote(
                r.small.at[i],
                r.small_got.at[i, base + k - 1],
                r.sm_send.at[base + k - 1],
                r.sm_recv.at[base + k - 1],
                device(k),
            )
            for k in range(1, count)
        ], base

    def small_start(i, level):
        for copy in small_copies(i, level)[0]:
            copy.start()

    def small_wait(i, level):
        copies, base = small_copies(i, level)
        for copy in copies:
            copy.wait()
        total = r.small[i]
        for k in range(len(copies)):
            total = total + r.small_got[i, base + k]
        r.small[i] = total

    def rows_of(arrays, u, j):
        g, n = UNITS[u]
        size = ins[g].shape[-2]
        at = rows_at(j * size, size)
        if g == UP:
            return arrays[g].at[at, n * Fq : (n + 1) * Fq]
        return arrays[g].at[:, at, :] if n is None else arrays[g].at[n, at, :]

    def whole_of(arrays, u):
        g, n = UNITS[u]
        if g == UP:
            return arrays[g].at[:, n * Fq : (n + 1) * Fq]
        return arrays[g] if n is None else arrays[g].at[n]

    turned = UP_UNITS[2:] if B == 2 else ()
    turned_back = UP_UNITS[3:] if B == 2 else ()
    beside = a * B + 1 - b
    inside = (a > 0) & (a < A - 1)

    def w_slot(u, j, way):
        t, e = lax.div(j, B), lax.rem(j, B)
        if way < 2:
            side = jnp.where(e == b, 0, A + 1) if u in turned else 0
            return r.w_send.at[u, side + jnp.where((t == a) & (way == 1), A, t)]
        base = 2 * (A + 1)
        return r.w_send.at[u, base + (t if B == 2 else jnp.where((e == b) & (way == 3), A * B + t, j))]

    def w_copy(u, j, way, src=None):
        place = rows_of(w, u, j)
        device = (page + (-B, B, -1, 1)[way], seq)
        return remote(place if src is None else src, place, w_slot(u, j, way), r.w_recv.at[u, j], device)

    ways = (a > 0, a < A - 1, b > 0, b < B - 1)

    def w_forward(u, j, along, src=None):
        for way in along:
            @pl.when(ways[way])
            def _():
                w_copy(u, j, way, src).start()

    def w_local(u):
        return pltpu.make_async_copy(whole_of(ins, u), rows_of(w, u, page), r.w_local.at[u])

    def w_first(*units, along=(0, 1, 2, 3)):
        for u in units:
            w_forward(u, page, along, whole_of(ins, u))
            if 2 in along:
                w_local(u).start()

    def w_turn(*units):
        for u in units:
            landed(rows_of(w, u, beside), r.w_recv.at[u, beside])
            w_forward(u, beside, (0, 1))

    def w_step(d, *units, on=True):
        for u in units:
            for sign, way in ((-1, 1), (1, 0)):
                @pl.when((a + sign * d >= 0) & (a + sign * d < A) & on)
                def _():
                    for column in (page, beside) if u in turned else (page,):
                        j = column + sign * d * B
                        landed(rows_of(w, u, j), r.w_recv.at[u, j])
                        w_forward(u, j, (way,) if u in turned else (way, 2, 3))

    def w_wait(*units):
        for u in units:
            w_local(u).wait()
            for e in range(1, 1 if u in turned else B):
                for t in range(A):
                    @pl.when(b - e >= 0)
                    def _():
                        j = t * B + b - e
                        landed(rows_of(w, u, j), r.w_recv.at[u, j])
                        w_forward(u, j, (3,))

                    @pl.when(b + e < B)
                    def _():
                        j = t * B + b + e
                        landed(rows_of(w, u, j), r.w_recv.at[u, j])
                        w_forward(u, j, (2,))

    def w_sent(u):
        for t in range(A):
            for e in range(B):
                j = t * B + e
                along = ((b == e) & (t >= a), (b == e) & (t <= a), e >= b, e <= b)
                if u in turned:
                    along = (t >= a, t <= a, (b == e) & (t == a), (b == e) & (t == a))
                for way, when in enumerate(along):
                    @pl.when(when & ways[way])
                    def _():
                        w_copy(u, j, way).wait_send()

    def block(array, g, e, n):
        rows, cols = ins[g].shape
        return array.at[rows_at(e * rows, rows), rows_at(n * cols, cols)]

    def m_local(g):
        return pltpu.make_async_copy(ins[g], block(w[g], g, shelf, seq), r.m_got.at[MOVED.index(g), seq])

    def m_collect_copy(g):
        i = MOVED.index(g)
        return remote(
            ins[g], block(w[g], g, shelf, seq), r.m_gave.at[i], r.m_got.at[i, seq], (page, collector)
        )

    def m_collect(g):
        @pl.when(collects)
        def _():
            m_local(g).start()

        @pl.when(jnp.logical_not(collects))
        def _():
            m_collect_copy(g).start()

    def m_copy(g, n, way):
        i = MOVED.index(g)
        place = block(w[g], g, mine, n)
        device = (page + B, page - B)[way] if way < 2 else a * B + lax.rem(b + way - 1, B)
        return remote(place, place, r.m_send.at[i, n, way], r.m_recv.at[i, mine, n], (device, seq))

    m_ways = [holds & (a >= a0) & (a < A - 1), holds & (a <= a0) & (a > 0)] + [holds] * (B - 1)

    def m_forward(g, n):
        for way in range(B + 1):
            @pl.when(m_ways[way])
            def _():
                m_copy(g, n, way).start()

    def m_first(g, n):
        @pl.when(collects)
        def _():
            @pl.when(seq == n)
            def _():
                m_local(g).wait()

            @pl.when(seq != n)
            def _():
                landed(block(w[g], g, shelf, n), r.m_got.at[MOVED.index(g), n])

            m_forward(g, n)

    hops = jnp.abs(a - a0)

    def m_pass(g, n, hop, where):
        @pl.when(holds & (hops == hop) & where)
        def _():
            landed(block(w[g], g, mine, n), r.m_recv.at[MOVED.index(g), mine, n])
            m_forward(g, n)

    def m_wait(g):
        for e in range(R):
            @pl.when(jnp.logical_not(holds) | (mine != e))
            def _():
                for n in range(S):
                    landed(block(w[g], g, e, n), r.m_recv.at[MOVED.index(g), e, n])

    def m_sent(g):
        @pl.when(jnp.logical_not(collects))
        def _():
            m_collect_copy(g).wait_send()

        for n in range(S):
            for way in range(B + 1):
                @pl.when(m_ways[way])
                def _():
                    m_copy(g, n, way).wait_send()

    low = 2 * a < A
    near = jnp.where(low, a, A - 1 - a)

    def order(m):
        if m == A - 1:
            return a
        t = jnp.where(m < A - 1 - near, A - 1 - m, m - (A - 1 - near))
        return jnp.where(low, t, A - 1 - t)

    def y_copy(u, k, t):
        other = lax.rem(b + k, B)
        return remote(
            rows_of(grad, u, t * B + other),
            r.rb[u].at[B - 1 - k, t],
            r.y_send.at[u, k - 1, t],
            r.y_recv.at[u, B - 1 - k, t],
            (a * B + other, seq),
        )

    def y_start(*units):
        for m in range(A):
            for u in units:
                for k in range(1, B):
                    y_copy(u, k, order(m)).start()

    def z_copy(u, t, sign):
        slot = jnp.where((t == a + sign) & (sign < 0), A, t)
        return remote(
            r.rb[u].at[0, t],
            r.zz[u].at[slot],
            r.z_send.at[u, t],
            r.z_recv.at[u, slot],
            (page + sign * B, seq),
        )

    def z_way(t):
        sign = jnp.where(t > a, 1, -1)
        before = a - sign
        return sign, (before >= 0) & (before < A)

    def y_sum(m, u):
        t = order(m)
        total = rows_of(grad, u, t * B + b)[...].astype(F32)
        for slot in range(B - 1):
            landed(r.rb[u].at[slot, t], r.y_recv.at[u, slot, t])
            total = total + r.rb[u][slot, t].astype(F32)
        r.rb[u][0, t] = total.astype(BF16)
        if m < A - 1:
            sign, has = z_way(t)

            @pl.when(jnp.logical_not(has))
            def _():
                z_copy(u, t, sign).start()

    def z_sum(m, u):
        t = order(m)
        sign, has = z_way(t)

        @pl.when(has)
        def _():
            landed(r.zz[u].at[t], r.z_recv.at[u, t])
            r.rb[u][0, t] = (r.rb[u][0, t].astype(F32) + r.zz[u][t].astype(F32)).astype(BF16)
            z_copy(u, t, sign).start()

    def z_total(u):
        @pl.when(a > 0)
        def _():
            landed(r.zz[u].at[a], r.z_recv.at[u, a])

        @pl.when(a < A - 1)
        def _():
            landed(r.zz[u].at[A], r.z_recv.at[u, A])

        total = r.rb[u][0, a].astype(F32)
        total = total + jnp.where(a > 0, r.zz[u][a].astype(F32), 0.0)
        total = total + jnp.where(a < A - 1, r.zz[u][A].astype(F32), 0.0)
        whole_of(outs, u)[...] = total

    def c_copy(u, t, sign, side, src):
        slot = jnp.where((t == a + sign) & (sign < 0), A, t)
        return remote(
            src,
            r.tz.at[side, slot],
            r.tz_send.at[side, t],
            r.tz_recv.at[side, slot],
            (page + sign * B, seq),
        )

    def c_own(u, t, side):
        return rows_of(grad, u, t * B + (b, 1 - b)[side])

    def c_first(u):
        for m in range(A - 1):
            t = order(m)
            sign, has = z_way(t)
            for side in range(2):
                @pl.when(jnp.logical_not(has))
                def _():
                    c_copy(u, t, sign, side, c_own(u, t, side)).start()

    def c_sum(m, u):
        t = order(m)
        sign, has = z_way(t)

        @pl.when(has)
        def _():
            for side in range(2):
                landed(r.tz.at[side, t], r.tz_recv.at[side, t])
                total = c_own(u, t, side)[...].astype(F32) + r.tz[side, t].astype(F32)
                r.ta[side, t] = total.astype(BF16)
                c_copy(u, t, sign, side, r.ta.at[side, t]).start()

    def c_turn(u):
        return remote(r.ta.at[1, a], r.tb, r.y_send.at[u, 0, 0], r.y_recv.at[u, 0, 0], (beside, seq))

    def c_total(u):
        for side in (1, 0):
            total = c_own(u, a, side)[...].astype(F32)
            for has, slot in ((a > 0, a), (a < A - 1, A)):
                @pl.when(has)
                def _():
                    landed(r.tz.at[side, slot], r.tz_recv.at[side, slot])

                total = total + jnp.where(has, r.tz[side, slot].astype(F32), 0.0)
            if side:
                r.ta[1, a] = total.astype(BF16)
                c_turn(u).start()
            else:
                whole_of(outs, u)[...] = total

    def c_end(u):
        landed(r.tb, r.y_recv.at[u, 0, 0])
        whole_of(outs, u)[...] = whole_of(outs, u)[...] + r.tb[...].astype(F32)

    def z_sent(u):
        if u in turned_back:
            c_turn(u).wait_send()
            for m in range(A - 1):
                t = order(m)
                for side in range(2):
                    c_copy(u, t, z_way(t)[0], side, c_own(u, t, side)).wait_send()
            return
        for t in range(A):
            for k in range(1, B):
                y_copy(u, k, t).wait_send()

            @pl.when(t != a)
            def _():
                z_copy(u, t, jnp.where(t > a, 1, -1)).wait_send()

    def f_parts(g):
        return max(QUARTERS // R, 1) if g == DOWN else 1

    def f_copy(g, k, n, part):
        i = MOVED.index(g)
        other = lax.rem(b + k, B)
        rows, cols = ins[g].shape
        size = rows // f_parts(g)
        return remote(
            grad[g].at[rows_at((other - b0) * rows + part * size, size), rows_at(n * cols, cols)],
            r.fb[i].at[B - 1 - k, n, part * size : (part + 1) * size, :],
            r.f_send[i].at[k - 1, n, part],
            r.f_recv[i].at[B - 1 - k, n, part],
            (a * B + other, seq),
        )

    def wanted(k):
        shelf_of = lax.rem(b + k, B) - b0
        return (shelf_of >= 0) & (shelf_of < R)

    def f_start(g, ready=lambda part: True):
        for n in range(S):
            for k in range(1, B):
                for part in range(f_parts(g)):
                    @pl.when(wanted(k) & ready((lax.rem(b + k, B) - b0) * f_parts(g) + part))
                    def _():
                        f_copy(g, k, n, part).start()

    inward = jnp.where(a > a0, -1, 1)
    from_out = holds & (a != a0) & inside
    starts_line = holds & (a != a0) & jnp.logical_not(inside)

    def v_copy(g, n):
        i = MOVED.index(g)
        slot = jnp.where((a + 1 == a0), 1, 0)
        return remote(
            r.fb[i].at[0, n], r.vv[i].at[slot, n], r.v_send.at[i, n], r.v_recv.at[i, slot, n], (page + inward * B, seq)
        )

    def s_copy(g, n):
        i = MOVED.index(g)
        return remote(r.fb[i].at[0, n], r.back[i], r.s_send.at[i, n], r.s_recv.at[i], (page, n))

    def f_sum(g, n):
        i = MOVED.index(g)

        @pl.when(holds)
        def _():
            total = block(grad[g], g, mine, n)[...].astype(F32)
            for slot in range(B - 1):
                for part in range(f_parts(g)):
                    f_copy(g, B - 1 - slot, n, part).wait_recv()
                total = total + r.fb[i][slot, n].astype(F32)
            r.fb[i][0, n] = total.astype(BF16)

            @pl.when(starts_line)
            def _():
                v_copy(g, n).start()

    passed = jnp.where(a > a0, A - 1 - a, a)

    def v_sum(g, n, hop):
        i = MOVED.index(g)

        @pl.when(from_out & (passed == hop))
        def _():
            landed(r.vv[i].at[0, n], r.v_recv.at[i, 0, n])
            r.fb[i][0, n] = (r.fb[i][0, n].astype(F32) + r.vv[i][0, n].astype(F32)).astype(BF16)
            v_copy(g, n).start()

    def v_total(g, n):
        i = MOVED.index(g)

        @pl.when(collects)
        def _():
            @pl.when(a < A - 1)
            def _():
                landed(r.vv[i].at[0, n], r.v_recv.at[i, 0, n])

            @pl.when(a > 0)
            def _():
                landed(r.vv[i].at[1, n], r.v_recv.at[i, 1, n])

            total = r.fb[i][0, n].astype(F32)
            total = total + jnp.where(a < A - 1, r.vv[i][0, n].astype(F32), 0.0)
            total = total + jnp.where(a > 0, r.vv[i][1, n].astype(F32), 0.0)

            @pl.when(seq == n)
            def _():
                outs[g][...] = total

            @pl.when(seq != n)
            def _():
                r.fb[i][0, n] = total.astype(BF16)
                s_copy(g, n).start()

    def s_wait(g):
        i = MOVED.index(g)

        @pl.when(jnp.logical_not(collects))
        def _():
            landed(r.back[i], r.s_recv.at[i])
            outs[g][...] = r.back[i][...].astype(F32)

    def v_sent(g):
        for n in range(S):
            for k in range(1, B):
                for part in range(f_parts(g)):
                    @pl.when(wanted(k))
                    def _():
                        f_copy(g, k, n, part).wait_send()

            @pl.when(starts_line | from_out)
            def _():
                v_copy(g, n).wait_send()

            @pl.when(collects & (seq != n))
            def _():
                s_copy(g, n).wait_send()

    token_live = r.token_counts[0]
    patch_live = r.patch_counts[0]
    r.norm_terms[6:8, :] = jnp.zeros((2, D), F32)
    gains = lambda k: r.small[0, k : k + 1, :]
    biases = lambda k: r.small[0, 3 + k : 4 + k, :]
    QB = min(256, T)
    lane = lax.broadcasted_iota(jnp.int32, (1, LANES), 1)
    halves = [(lane // HEAD_DIM == h) for h in range(2)]
    half_of = [half.astype(F32).astype(BF16) for half in halves]
    scale = HEAD_DIM ** (-0.5)

    def project(dst, left, weight):
        for n, (out, index) in enumerate(dst):
            out[...] = nn(left[...], weight[index]).astype(BF16)

    def attend(q, k, v, o, probs, live, causal):
        @pl.loop(0, Dl // LANES)
        def _(pair):
            cols = rows_at(pair * LANES, LANES)
            for block in range(T // QB):
                extent = (block + 1) * QB if causal else T
                rows = slice(block * QB, (block + 1) * QB)
                q2 = q[rows, cols]
                k2, v2 = k[:extent, cols], v[:extent, cols]
                at = lax.broadcasted_iota(jnp.int32, (QB, extent), 1)
                allowed = at < live
                if causal:
                    row = block * QB + lax.broadcasted_iota(jnp.int32, (QB, extent), 0)
                    allowed = allowed & (at <= row)
                found = []
                for h in range(2):
                    scores = nt(q2 * half_of[h], k2) * scale
                    scores = jnp.where(allowed, scores, -1e30)
                    raised = jnp.exp(scores - jnp.max(scores, axis=-1, keepdims=True))
                    share = (raised / jnp.sum(raised, axis=-1, keepdims=True)).astype(BF16)
                    probs[2 * pair + h, rows, :extent] = share
                    found.append(nn(share, v2))
                o[rows, cols] = jnp.where(halves[0], found[0], found[1]).astype(BF16)

    def attend_back(q, k, v, do, probs, dq, dk, dv, causal):
        @pl.loop(0, Dl // LANES)
        def _(pair):
            cols = rows_at(pair * LANES, LANES)
            r.dk_sum[...] = jnp.zeros_like(r.dk_sum)
            r.dv_sum[...] = jnp.zeros_like(r.dv_sum)
            for block in range(T // QB):
                extent = (block + 1) * QB if causal else T
                rows = slice(block * QB, (block + 1) * QB)
                q2, do2 = q[rows, cols], do[rows, cols]
                k2, v2 = k[:extent, cols], v[:extent, cols]
                dqs, dks, dvs = [], [], []
                for h in range(2):
                    share = probs[2 * pair + h, rows, :extent]
                    wide = share.astype(F32)
                    dp = nt(do2 * half_of[h], v2)
                    delta = jnp.sum(wide * dp, axis=-1, keepdims=True)
                    ds = (wide * (dp - delta)).astype(BF16)
                    dqs.append(nn(ds, k2))
                    dks.append(tn(ds, q2))
                    dvs.append(tn(share, do2))
                dq[rows, cols] = (jnp.where(halves[0], dqs[0], dqs[1]) * scale).astype(BF16)
                r.dk_sum[:extent, :] += jnp.where(halves[0], dks[0], dks[1])
                r.dv_sum[:extent, :] += jnp.where(halves[0], dvs[0], dvs[1])
            dk[:, cols] = (r.dk_sum[...] * scale).astype(BF16)
            dv[:, cols] = r.dv_sum[...].astype(BF16)

    def norm_back(k, values, incoming, ch):
        unit, rate = normed(values)
        for row, term in ((k, incoming * unit), (3 + k, incoming)):
            so_far = jnp.sum(term, axis=0, keepdims=True)
            r.norm_terms[row : row + 1, :] = so_far if ch == 0 else r.norm_terms[row : row + 1, :] + so_far
        dn = incoming * gains(k)
        return rate * (
            dn - jnp.mean(dn, axis=-1, keepdims=True) - unit * jnp.mean(dn * unit, axis=-1, keepdims=True)
        )

    def norm_own(k, values, dst, ch):
        dst[part_of(seq, ch), :] = (normed(values)[0] * gains(k) + biases(k)).astype(BF16)

    few = r.norm_gains.shape[1]
    at_feature = lax.broadcasted_iota(jnp.int32, (few, D), 1)
    placed = at_feature == lax.broadcasted_iota(jnp.int32, (few, D), 0) + (page * S + seq) * few
    plan = []
    SLOW = 5

    def when(time, *steps):
        plan.extend((time, step) for step in steps)

    def each_row_part(step):
        def run():
            for ch in range(2):
                step(ch, slice(ch * half, (ch + 1) * half))

        return run

    results = [
        (r.own_mixed, r.mixed),
        (r.own_input_grad, r.input_grad),
        (r.own_memory_grad, r.memory_grad),
        *((r.sums[g], r.outs[g]) for g in MOVED),
        *((whole_of(r.sums, u), whole_of(r.outs, u)) for u in range(len(UNITS))),
    ]
    O_MIXED, O_INPUT, O_MEMORY, O_MOVED, O_UNITS = 0, 1, 2, 3, 6

    def leave(n):
        kept, out = results[n]
        return pltpu.make_async_copy(kept, out, r.o_sem.at[n])

    def w_moved(g, first, hop_time, gap, end_first, end_gap):
        ends = jnp.logical_not(inside)
        for n in range(S):
            when(first + n * gap, lambda n=n: m_first(g, n))
            for hop in range(1, A):
                time = first + n * gap + hop * hop_time
                if hop < A - 1:
                    when(time, lambda n=n, hop=hop: m_pass(g, n, hop, inside))
                if hop > 1:
                    time = end_first + n * end_gap + hop / 10
                when(time, lambda n=n, hop=hop: m_pass(g, n, hop, ends))

    def g_moved(g, first, hop_time, gap, late, last):
        for n in range(S):
            time = first + n * gap
            when(time, lambda n=n: f_sum(g, n))
            for hop in range(1, A - 1):
                when(time + late + hop * hop_time + (hop - 1) * SLOW, lambda n=n, hop=hop: v_sum(g, n, hop))
            when(last, lambda n=n: v_total(g, n))

    def g_units(units, first, hop_time, gap, late):
        for place, u in enumerate(units):
            time = first + gap * place / len(units)
            for m in range(A):
                when(time + gap * m, lambda m=m, u=u: y_sum(m, u))
            for m in range(A - 2):
                when(time + gap * m + late + hop_time, lambda m=m, u=u: z_sum(m, u))
            after = time + late + 2 * hop_time + SLOW
            when(max(after, time + gap * (A - 2)), lambda u=u: z_sum(A - 2, u))
            when(188, lambda u=u: z_total(u), lambda u=u: leave(O_UNITS + u).start())

    given = (
        (G_TOKENS, r.tokens, r.all_tokens), (G_MEMORY, r.memory, r.all_memory), (G_COT, r.cotangent, r.dyr)
    )
    loads = [pltpu.make_async_copy(piece, everyone.at[own], r.ld_sem.at[i]) for i, piece, everyone in given]

    def begin():
        r.small[0] = jnp.zeros((8, D), F32)
        r.small[0, 0:3, :] = nn(r.norm_gains[...], placed.astype(F32).astype(BF16))
        r.small[0, 3:6, :] = nn(r.norm_biases[...], placed.astype(F32).astype(BF16))
        small_start(0, 0)
        w_first(*SELF_UNITS)
        w_first(*turned, along=(2, 3))
        m_collect(SELF_OUT)
        ag_begin(*given[0])
        for load in loads:
            load.start()

    def small_next(i, level):
        small_wait(i, level)
        small_start(i, level + 1 if i == 0 else level - 1)

    def take_tokens():
        small_wait(0, 2)
        ag_wait(G_TOKENS, r.all_tokens)
        for load in loads:
            load.wait()

        @pl.loop(0, S)
        def _(n):
            at = rows_at(n * Tl, Tl)
            values = r.all_tokens[at, :].astype(F32)
            r.a1[at, :] = (normed(values)[0] * gains(0) + biases(0)).astype(BF16)

    def self_project():
        w_wait(*SELF_UNITS)
        project(((r.q, 0), (r.k, 1), (r.v, 2)), r.a1, w[SELF])

    def self_sum():
        m_wait(SELF_OUT)
        rs_start(R_CHAIN, lambda at: nn(r.o[at, :], w[SELF_OUT][...]))

    @each_row_part
    def self_add(ch, rows):
        r.x1[rows, :] = r.all_tokens[part_of(seq, ch), :].astype(F32) + rs_wait(R_CHAIN, ch)
        norm_own(1, r.x1[rows, :], r.a2, ch)
        ag_start(G_A2, r.a2.at[own], r.a2, ch)

    def memory_project():
        w_wait(*CROSS_UNITS)
        ag_wait(G_MEMORY, r.all_memory)
        project(((r.kc, 1), (r.vc, 2)), r.all_memory, w[CROSS])

    def cross_project():
        ag_wait(G_A2, r.a2)
        project(((r.qc, 0),), r.a2, w[CROSS])

    def cross_sum():
        m_wait(CROSS_OUT)
        rs_sent(R_CHAIN)
        rs_start(R_CHAIN, lambda at: nn(r.oc[at, :], w[CROSS_OUT][...]))

    def take_cotangent():
        ag_wait(G_COT, r.dyr)
        ag_sent(*given[2])

        @pl.loop(0, S)
        def _(n):
            at = rows_at(n * Tl, Tl)
            row = n * Tl + lax.broadcasted_iota(jnp.int32, (Tl, 1), 0)
            values = r.dyr[at, :].astype(F32)
            r.dyr[at, :] = jnp.where(row < token_live, values, 0.0).astype(BF16)

    @each_row_part
    def cross_add(ch, rows):
        r.x2[rows, :] = r.x1[rows, :] + rs_wait(R_CHAIN, ch)
        norm_own(2, r.x2[rows, :], r.a3, ch)
        ag_start(G_A3, r.a3.at[own], r.a3, ch)

    def hidden_units(lo, hi):
        @pl.loop(lo, hi)
        def _(n):
            cols = rows_at(n * Fq, Fq)
            out, slope = gelu_pair(nn(r.a3[...], w[UP][:, cols]))
            r.g[:, cols] = out.astype(BF16)
            r.slope[:, cols] = slope

    def down_grad(lo, hi):
        @pl.loop(lo, hi)
        def _(n):
            cols = rows_at(n * Fq, Fq)
            grad[DOWN][cols, :] = tn(r.g[:, cols], r.dyr[...]).astype(BF16)

    def hidden_grad(lo, hi):
        @pl.loop(lo, hi)
        def _(n):
            cols = rows_at(n * Fq, Fq)
            r.du[:, cols] = (nt(r.dyr[...], w[DOWN][cols, :]) * r.slope[:, cols]).astype(BF16)

    def up_grad(lo, hi):
        if lo < hi:
            @pl.loop(0, D // 256)
            def _(n):
                cols = rows_at(n * 256, 256)
                grad[UP][cols, lo * Fq : hi * Fq] = tn(r.a3[:, cols], r.du[:, lo * Fq : hi * Fq]).astype(BF16)

    ahead = QUARTERS - len(turned)

    def hidden():
        w_wait(*UP_UNITS[:ahead])
        ag_wait(G_A3, r.a3)
        hidden_units(0, ahead)
        down_grad(0, ahead)

    def hidden_rest():
        if turned:
            for d in range(1, A):
                w_step(d, *turned, on=jnp.logical_not(inside))
            w_wait(*turned)
            f_start(DOWN, lambda part: part < ahead)
            hidden_units(ahead, QUARTERS)
            down_grad(ahead, QUARTERS)
            f_start(DOWN, lambda part: part >= ahead)
        else:
            f_start(DOWN)

    straight = tuple(u for u in UP_UNITS if u not in turned)
    when(0, begin)
    when(6, lambda: w_step(1, *SELF_UNITS))
    when(8, lambda: small_next(0, 0), lambda: m_collect(CROSS_OUT), lambda: ag_begin(*given[1]), lambda: m_collect(DOWN))
    when(12, lambda: w_step(2, *SELF_UNITS))
    w_moved(SELF_OUT, 13, 4, 0.1, 25, 0.1)
    when(15, lambda: small_next(0, 1), lambda: ag_forward(G_TOKENS, r.all_tokens), lambda: ag_begin(*given[2]))
    when(16.5, lambda: w_step(3, *SELF_UNITS))
    when(17.5, lambda: w_first(*CROSS_UNITS, along=(2, 3)))
    when(17.5, lambda: w_first(*CROSS_UNITS, along=(0, 1)))
    when(22, lambda: w_first(*straight))
    when(23.5, lambda: w_step(1, *CROSS_UNITS))
    when(24.5, take_tokens)
    when(27, self_project)
    when(29, lambda: w_step(2, *CROSS_UNITS))
    w_moved(CROSS_OUT, 30, 5, 0.1, 46, 0.1)
    when(31, lambda: ag_forward(G_MEMORY, r.all_memory))
    when(32, lambda: attend(r.q, r.k, r.v, r.o, r.p, token_live, True))
    when(34.5, lambda: w_step(3, *CROSS_UNITS))
    when(36, self_sum)
    when(37, lambda: w_step(1, *straight))
    w_moved(DOWN, 37.5, 7.5, 3, 60, 5)
    when(42, lambda: ag_forward(G_COT, r.dyr))
    when(43, lambda: w_step(2, *straight))
    when(46, self_add)
    when(51, lambda: w_first(*turned, along=(0, 1)))
    when(48, memory_project)
    when(49, lambda: w_step(3, *straight))
    when(50, lambda: w_turn(*turned))
    when(52, lambda: ag_forward(G_A2, r.a2))
    when(53.2, cross_project)
    when(54, lambda: attend(r.qc, r.kc, r.vc, r.oc, r.pc, patch_live, False))
    when(57, cross_sum)
    when(62, lambda: w_step(1, *turned, on=inside))
    when(61, take_cotangent)
    when(67, cross_add)
    when(69, lambda: w_step(2, *turned, on=inside))
    when(75, lambda: ag_forward(G_A3, r.a3))
    when(76, hidden)
    when(84, hidden_rest)

    def hidden_back():
        m_wait(DOWN)
        hidden_grad(QUARTERS - len(turned_back), QUARTERS)
        up_grad(QUARTERS - len(turned_back), QUARTERS)
        for u in turned_back:
            c_first(u)
        hidden_grad(0, QUARTERS - len(turned_back))
        ag_sent(G_A3, r.a3.at[own], r.a3)
        rs_sent(R_CHAIN)
        rs_start(R_CHAIN, lambda at: nt(r.du[at, :], w[UP][...]))

    def up_grad_rest():
        up_grad(0, QUARTERS - len(turned_back))
        y_start(*UP_UNITS[: QUARTERS - len(turned_back)])

    @each_row_part
    def hidden_add(ch, rows):
        back_term = norm_back(2, r.x2[rows, :], rs_wait(R_CHAIN, ch), ch)
        r.dx2[rows, :] = r.dyr[part_of(seq, ch), :].astype(F32) + back_term
        r.dz2[part_of(seq, ch), :] = r.dx2[rows, :].astype(BF16)
        ag_start(G_DZ2, r.dz2.at[own], r.dz2, ch)

    def cross_back():
        ag_wait(G_DZ2, r.dz2)
        grad[CROSS_OUT][...] = tn(r.oc[...], r.dz2[...]).astype(BF16)
        f_start(CROSS_OUT)
        r.do[...] = nt(r.dz2[...], w[CROSS_OUT][...]).astype(BF16)
        attend_back(r.qc, r.kc, r.vc, r.do, r.pc, r.dq, r.dkc, r.dvc, False)

    def cross_back_sum():
        rs_sent(R_CHAIN)
        rs_start(R_CHAIN, lambda at: nt(r.dq[at, :], w[CROSS][0]))

    def cross_grad():
        for n, (left, right) in enumerate(((r.a2, r.dq), (r.all_memory, r.dkc), (r.all_memory, r.dvc))):
            grad[CROSS][n] = tn(left[...], right[...]).astype(BF16)
        y_start(*CROSS_UNITS)

    @each_row_part
    def cross_back_add(ch, rows):
        r.dx1[rows, :] = r.dx2[rows, :] + norm_back(1, r.x1[rows, :], rs_wait(R_CHAIN, ch), ch)
        r.dz1[part_of(seq, ch), :] = r.dx1[rows, :].astype(BF16)
        ag_start(G_DZ1, r.dz1.at[own], r.dz1, ch)

    def self_back():
        ag_wait(G_DZ1, r.dz1)
        grad[SELF_OUT][...] = tn(r.o[...], r.dz1[...]).astype(BF16)
        f_start(SELF_OUT)
        r.do[...] = nt(r.dz1[...], w[SELF_OUT][...]).astype(BF16)
        attend_back(r.q, r.k, r.v, r.do, r.p, r.dq, r.dk, r.dv, True)
        for n, right in enumerate((r.dq, r.dk, r.dv)):
            grad[SELF][n] = tn(r.a1[...], right[...]).astype(BF16)
        y_start(*SELF_UNITS)

    def self_back_sum():
        rs_sent(R_CHAIN)
        rs_start(
            R_CHAIN,
            lambda at: nt(r.dq[at, :], w[SELF][0]) + nt(r.dk[at, :], w[SELF][1]) + nt(r.dv[at, :], w[SELF][2]),
        )

    def memory_sum():
        ag_sent(G_A2, r.a2.at[own], r.a2)
        rs_start(R_MEMORY, lambda at: nt(r.dkc[at, :], w[CROSS][1]) + nt(r.dvc[at, :], w[CROSS][2]))

    @each_row_part
    def input_add(ch, rows):
        back_term = norm_back(0, r.all_tokens[part_of(seq, ch), :].astype(F32), rs_wait(R_CHAIN, ch), ch)
        r.own_input_grad[rows, :] = r.dx1[rows, :] + back_term

    def small_last():
        r.small[1] = r.norm_terms[...]
        small_start(1, 2)

    def mixed_sum():
        ag_sent(G_DZ2, r.dz2.at[own], r.dz2)
        rs_start(R_MIXED, lambda at: nn(r.g[at, :], w[DOWN][...]))

    @each_row_part
    def memory_add(ch, rows):
        r.own_memory_grad[rows, :] = rs_wait(R_MEMORY, ch)

    @each_row_part
    def mixed_add(ch, rows):
        live_row = (seq * Tl + ch * half + lax.broadcasted_iota(jnp.int32, (half, 1), 0)) < token_live
        r.own_mixed[rows, :] = jnp.where(live_row, r.x2[rows, :] + rs_wait(R_MIXED, ch), 0.0).astype(BF16)

    def norms_out():
        small_wait(1, 0)
        picked = lax.dot_general(
            r.small[1],
            placed.astype(F32),
            (((1,), (1,)), ((), ())),
            precision=lax.Precision.HIGHEST,
            preferred_element_type=F32,
        )
        r.gains_grad[...] = picked[0:3]
        r.biases_grad[...] = picked[3:6]

    when(87, hidden_back)
    when(95, up_grad_rest)
    if turned_back:
        when(99, lambda: c_sum(0, UP_UNITS[3]))
        when(102, lambda: c_sum(1, UP_UNITS[3]))
        when(105, lambda: c_sum(2, UP_UNITS[3]))
        when(112, lambda: c_total(UP_UNITS[3]))
        when(142, lambda: c_end(UP_UNITS[3]), lambda: leave(O_UNITS + UP_UNITS[3]).start())
        g_moved(DOWN, 98, 7.2, 5.6, 4, 155)
        g_units(UP_UNITS[:3], 121, 4.5, 4.2, 7)
    else:
        g_moved(DOWN, 97, 7.2, 5.6, 0, 155)
        g_units(UP_UNITS, 121, 4.5, 5.6, 0)
    when(103, hidden_add)
    when(109, lambda: ag_forward(G_DZ2, r.dz2))
    when(111, cross_back)
    when(117, cross_back_sum)
    when(119, cross_grad)
    when(126.5, cross_back_add)
    when(132.5, lambda: ag_forward(G_DZ1, r.dz1))
    when(134.5, self_back)
    when(140.5, self_back_sum)
    g_moved(CROSS_OUT, 138, 3.2, 1.4, 4, 172)
    when(145, memory_sum)
    g_units(CROSS_UNITS, 144, 6, 4.2, 4)
    when(149, input_add, lambda: leave(O_INPUT).start())
    when(150, small_last)
    when(153, mixed_sum)
    when(160, lambda: small_next(1, 2))
    when(179, memory_add, lambda: leave(O_MEMORY).start())
    g_moved(SELF_OUT, 159, 3.2, 1.4, 2, 182)
    when(177, lambda: small_next(1, 1))
    when(179, mixed_add, lambda: leave(O_MIXED).start())
    g_units(SELF_UNITS, 166, 6, 4.2, 0)
    for time, g in ((179, DOWN), (179, CROSS_OUT), (190, SELF_OUT)):
        when(time, lambda g=g: s_wait(g), lambda g=g: leave(O_MOVED + MOVED.index(g)).start())
    when(190, norms_out)

    for _, step in sorted(plan, key=lambda entry: entry[0]):
        step()

    for n in range(len(results)):
        leave(n).wait()
    for i in (R_CHAIN, R_MIXED, R_MEMORY):
        rs_sent(i)
    for i, piece, everyone in given[:2]:
        ag_sent(i, piece, everyone)
    ag_sent(G_DZ1, r.dz1.at[own], r.dz1)
    for u in range(len(UNITS)):
        w_sent(u)
        z_sent(u)
    for g in MOVED:
        m_sent(g)
        v_sent(g)


def layer_call(A, B, S, rows, weights, norms, counts):
    V = pltpu.VMEM
    Tl, D = rows[0].shape
    T = Tl * S
    Dl = weights[SELF].shape[2]
    Fl = weights[UP].shape[1]
    pages = A * B
    R = pages // S
    heads = Dl // HEAD_DIM
    shards = [x.shape for x in weights]
    full = []
    for g, s in enumerate(shards):
        if g in (SELF, CROSS):
            full.append((s[0], s[1] * pages, s[2]))
        elif g == UP:
            full.append((s[0] * pages, s[1]))
        else:
            full.append((s[0] * R, s[1] * S))
    hbm, vmem, smem = (pl.BlockSpec(memory_space=m) for m in (pl.ANY, V, pltpu.SMEM))
    shape = jax.ShapeDtypeStruct
    dma = pltpu.SemaphoreType.DMA
    small_slots = S + A + B - 3
    units = len(UNITS)
    pieces = [
        (shards[g][0], Fl // QUARTERS) if g == UP else shards[g] if n is None else shards[g][1:] for g, n in UNITS
    ]
    turn = pieces[-1]
    if B == 2:
        pieces[-1] = (16, LANES)
    else:
        turn = (16, LANES)
    row_ref, wide_ref = V((T, D), BF16), V((T, Dl), BF16)
    own_ref, hidden_ref = V((Tl, D), F32), V((T, Fl), BF16)
    operands = dict(
        tokens=rows[0],
        memory=rows[1],
        cotangent=rows[2],
        ins=list(weights),
        norm_gains=norms[0],
        norm_biases=norms[1],
        token_counts=counts[0],
        patch_counts=counts[1],
    )
    specs = dict(
        tokens=hbm, memory=hbm, cotangent=hbm, ins=[hbm] * 6, norm_gains=vmem, norm_biases=vmem, token_counts=smem, patch_counts=smem
    )
    results = dict(
        mixed=shape((Tl, D), BF16),
        input_grad=shape((Tl, D), F32),
        memory_grad=shape((Tl, D), F32),
        outs=[shape(s, F32) for s in shards],
        gains_grad=shape(norms[0].shape, F32),
        biases_grad=shape(norms[1].shape, F32),
    )
    scratch = dict(
        w=[V(s, BF16) for s in full],
        grad=[V(s, BF16) for s in full],
        rb=[V((B - 1, A, *piece), BF16) for piece in pieces],
        zz=[V((A + 1, *piece), BF16) for piece in pieces],
        ta=V((2, A, *turn), BF16),
        tz=V((2, A + 1, *turn), BF16),
        tb=V(turn, BF16),
        fb=[V((B - 1, S, *shards[g]), BF16) for g in MOVED],
        vv=[V((2, S, *shards[g]), BF16) for g in MOVED],
        back=[V(shards[g], BF16) for g in MOVED],
        all_tokens=row_ref,
        all_memory=row_ref,
        dyr=row_ref,
        a1=row_ref,
        a2=row_ref,
        a3=row_ref,
        dz2=row_ref,
        q=wide_ref,
        k=wide_ref,
        v=wide_ref,
        o=wide_ref,
        qc=wide_ref,
        kc=wide_ref,
        vc=wide_ref,
        oc=wide_ref,
        do=wide_ref,
        dq=wide_ref,
        dk=wide_ref,
        dv=wide_ref,
        dkc=wide_ref,
        dvc=wide_ref,
        p=V((heads, T, T), BF16),
        pc=V((heads, T, T), BF16),
        g=hidden_ref,
        du=hidden_ref,
        slope=V((T, Fl), F32),
        x1=own_ref,
        x2=own_ref,
        dx1=own_ref,
        dx2=own_ref,
        dk_sum=V((T, LANES), F32),
        dv_sum=V((T, LANES), F32),
        chain_part=row_ref,
        got=[V((S - 1, Tl, D), BF16)] * 3,
        own_mixed=V((Tl, D), BF16),
        own_input_grad=own_ref,
        own_memory_grad=own_ref,
        sums=[V(s, F32) for s in shards],
        small=V((2, 8, D), F32),
        small_got=V((2, small_slots, 8, D), F32),
        norm_terms=V((8, D), F32),
        ag_send=dma((7, 2, S - 1)),
        ag_recv=dma((7, 2, S)),
        rs_send=dma((3, 2, S - 1)),
        rs_recv=dma((3, 2, S - 1)),
        sm_send=dma((small_slots,)),
        sm_recv=dma((small_slots,)),
        ld_sem=dma((3,)),
        o_sem=dma((units + 6,)),
        w_send=dma((units, 2 * (A + 1) + (A if B == 2 else pages + A))),
        w_recv=dma((units, pages)),
        w_local=dma((units,)),
        y_send=dma((units, B - 1, A)),
        y_recv=dma((units, B - 1, A)),
        z_send=dma((units, A)),
        z_recv=dma((units, A + 1)),
        tz_send=dma((2, A)),
        tz_recv=dma((2, A + 1)),
        m_gave=dma((3,)),
        m_got=dma((3, S)),
        m_send=dma((3, S, B + 1)),
        m_recv=dma((3, R, S)),
        f_send=[dma((B - 1, S, max(QUARTERS // R, 1) if g == DOWN else 1)) for g in MOVED],
        f_recv=[dma((B - 1, S, max(QUARTERS // R, 1) if g == DOWN else 1)) for g in MOVED],
        v_send=dma((3, S)),
        v_recv=dma((3, 2, S)),
        s_send=dma((3, S)),
        s_recv=dma((3,)),
    )
    parts = [jax.tree.flatten(part) for part in (operands, specs, results, scratch)]
    values, in_specs, out_shape, scratch_shapes = (leaves for leaves, _ in parts)
    ends = [len(values), len(values) + len(out_shape)]

    def kernel(*refs):
        held = (refs[: ends[0]], refs[ends[0] : ends[1]], refs[ends[1] :])
        r = types.SimpleNamespace()
        for (_, tree), some in zip((parts[0], parts[2], parts[3]), held):
            vars(r).update(jax.tree.unflatten(tree, some))
        layer_kernel(A, B, S, r)

    found = pl.pallas_call(
        kernel,
        out_shape=out_shape,
        in_specs=in_specs,
        out_specs=[vmem if s.shape == norms[0].shape else hbm for s in out_shape],
        scratch_shapes=scratch_shapes,
        compiler_params=pltpu.CompilerParams(
            collective_id=0, has_side_effects=True, vmem_limit_bytes=62 * 2**20
        ),
        name="layer",
    )(*values)
    return jax.tree.unflatten(parts[2][1], found)


def keep_kernel(*refs):
    *arrays, sems = refs
    count = len(arrays) // 3
    given, kept, held = (arrays[n * count : (n + 1) * count] for n in range(3))
    loads = [pltpu.make_async_copy(given[n], held[n], sems.at[0, n]) for n in range(count)]
    stores = [pltpu.make_async_copy(held[n], kept[n], sems.at[1, n]) for n in range(count)]
    for load in loads:
        load.start()
    for load, store in zip(loads, stores):
        load.wait()
        store.start()
    for store in stores:
        store.wait()


def keep(*arrays):
    hbm = pl.BlockSpec(memory_space=pl.ANY)
    return pl.pallas_call(
        keep_kernel,
        out_shape=[jax.ShapeDtypeStruct(x.shape, x.dtype) for x in arrays],
        in_specs=[hbm] * len(arrays),
        out_specs=[hbm] * len(arrays),
        scratch_shapes=[pltpu.VMEM(x.shape, x.dtype) for x in arrays]
        + [pltpu.SemaphoreType.DMA((2, len(arrays)))],
        name="keep",
    )(*arrays)


def per_device(
    tokens,
    memory,
    cotangent,
    self_qkv,
    self_out,
    cross_qkv,
    cross_out,
    up_weight,
    down_weight,
    norm_gains,
    norm_biases,
    token_counts,
    patch_counts,
):
    pages = lax.axis_size("page")
    parts = lax.axis_size("seq")
    wide = 2 if pages == 8 else 8
    found = layer_call(
        pages // wide,
        wide,
        parts,
        (tokens[0], memory[0], cotangent[0]),
        (self_qkv, self_out, cross_qkv, cross_out, up_weight, down_weight),
        (norm_gains, norm_biases),
        (token_counts, patch_counts),
    )
    return keep(
        found["mixed"][None],
        found["input_grad"][None],
        found["memory_grad"][None],
        *found["outs"],
        found["gains_grad"],
        found["biases_grad"],
    )


def solution(mesh):
    rows = P("page", "seq", None)
    stack = P(None, "page", "seq")
    flat = P("page", "seq")
    norm = P(None, ("page", "seq"))
    counts = P("page")
    return jax.shard_map(
        per_device,
        mesh=mesh,
        in_specs=(rows, rows, rows, stack, flat, stack, flat, flat, flat, norm, norm, counts, counts),
        out_specs=(rows, rows, rows, stack, flat, stack, flat, flat, flat, norm, norm),
        check_vma=False,
    )
```

```python
import types

import jax
import jax.numpy as jnp
from jax import lax
from jax.experimental import pallas as pl
from jax.experimental.pallas import tpu as pltpu
from jax.sharding import PartitionSpec as P

HEAD_DIM = 64
F32 = jnp.float32
BF16 = jnp.bfloat16
MESH = pl.DeviceIdType.MESH
SELF, SELF_OUT, CROSS, CROSS_OUT, UP, DOWN = range(6)
MOVED = (SELF_OUT, CROSS_OUT, DOWN)
QUARTERS = 4
UNITS = ((SELF, 0), (SELF, 1), (SELF, 2), (CROSS, None), (UP, (0, 2)), (UP, (2, 4)))
BACK_UNITS = ((SELF, 0), (SELF, 1), (SELF, 2), (CROSS, None), (UP, (0, 3)), (UP, (3, 4)))
SELF_UNITS, CROSS_UNITS, UP_UNITS = (0, 1, 2), (3,), (4, 5)
G_TOKENS, G_MEMORY, G_COT, G_A2, G_A3, G_DZ2, G_DZ1 = range(7)
R_CHAIN, R_MIXED, R_MEMORY = range(3)
LANES = 128


def nn(left, right):
    return lax.dot_general(left, right, (((1,), (0,)), ((), ())), preferred_element_type=F32)


def nt(left, right):
    return lax.dot_general(left, right, (((1,), (1,)), ((), ())), preferred_element_type=F32)


def tn(left, right):
    return lax.dot_general(left, right, (((0,), (0,)), ((), ())), preferred_element_type=F32)


def rows_at(start, size):
    return pl.ds(pl.multiple_of(start, size), size)


def normed(values):
    center = values - jnp.mean(values, axis=-1, keepdims=True)
    rate = lax.rsqrt(jnp.mean(center * center, axis=-1, keepdims=True) + 1e-05)
    return center * rate, rate


def gelu_pair(values):
    chance = 0.5 + 0.5 * lax.erf(values * 0.7071067811865476)
    density = jnp.exp(-0.5 * values * values) * 0.3989422804014327
    return values * chance, chance + values * density


def layer_kernel(A, B, S, r):
    r.dz1 = r.a3
    r.part = [r.chain_part, r.dz2, r.a2]
    ins, w, grad, outs = r.ins, r.w, r.grad, r.sums
    page, seq = lax.axis_index("page"), lax.axis_index("seq")
    a, b = lax.div(page, B), lax.rem(page, B)
    R = A * B // S
    Tl, D = r.tokens.shape
    T = Tl * S
    Dl = ins[SELF].shape[2]
    Fl = ins[UP].shape[1]
    Fq = Fl // QUARTERS
    own = rows_at(seq * Tl, Tl)
    shelf, collector = lax.rem(page, R), lax.div(page, R)
    collects = seq == collector
    a0, b0 = lax.div(seq * R, B), lax.rem(seq * R, B)
    mine = b - b0
    holds = (mine >= 0) & (mine < R)

    def remote(src, dst, send, recv, device):
        return pltpu.make_async_remote_copy(
            src_ref=src, dst_ref=dst, send_sem=send, recv_sem=recv, device_id=device, device_id_type=MESH
        )

    def landed(dst, recv):
        remote(dst, dst, recv, recv, (page, seq)).wait_recv()

    barrier = pltpu.get_barrier_semaphore()

    def greet(device):
        pl.semaphore_signal(barrier, inc=1, device_id=device, device_id_type=MESH)

    for k in range(1, S):
        greet((page, lax.rem(seq + k, S)))
    for k in range(1, B):
        greet((a * B + lax.rem(b + k, B), seq))
    for k in range(1, A):
        greet((lax.rem(a + k, A) * B + b, seq))

    pl.semaphore_wait(barrier, S + A + B - 3)

    X = S // 2
    chip, core = lax.div(seq, 2), lax.rem(seq, 2)
    sibling = chip * 2 + 1 - core
    half = Tl // 2

    def part_of(source, ch, parts=2):
        size = Tl // parts
        return rows_at(source * Tl + ch * size, size)

    def parts_of(i):
        return 1 if i <= G_COT else 2

    def chip_at(dx):
        return lax.rem(chip + dx, X)

    def ag_copy(i, src, dst, ch, n):
        source = chip_at(2 * X - 1 - n) * 2 + core if n >= X else seq
        parts = parts_of(i)
        mine = dst.at[part_of(source, ch, parts)] if n >= X else src.at[rows_at(ch * (Tl // parts), Tl // parts)]
        to = chip_at(n) * 2 + core if 0 < n < X else sibling
        place = dst.at[part_of(source, ch, parts)]
        return remote(mine, place, r.ag_send[i].at[ch, n], r.ag_recv[i].at[ch, source], (page, to))

    def ag_start(i, src, dst, ch):
        for n in (*range(1, X), 0):
            ag_copy(i, src, dst, ch, n).start()

    def ag_begin(i, src, dst):
        for ch in range(parts_of(i)):
            ag_start(i, src, dst, ch)

    def ag_forward(i, dst):
        for ch in range(parts_of(i)):
            for n in range(X, 2 * X - 1):
                source = chip_at(2 * X - 1 - n) * 2 + core
                landed(dst.at[part_of(source, ch, parts_of(i))], r.ag_recv[i].at[ch, source])
                ag_copy(i, None, dst, ch, n).start()

    def ag_wait(i, dst):
        for ch in range(parts_of(i)):
            for x in range(X):
                source = 2 * x + 1 - core
                landed(dst.at[part_of(source, ch, parts_of(i))], r.ag_recv[i].at[ch, source])

    def ag_sent(i, src, dst):
        for ch in range(parts_of(i)):
            for n in range(2 * X - 1):
                ag_copy(i, src, dst, ch, n).wait_send()

    def rs_copy(i, x, ch):
        return remote(
            r.part[i].at[part_of(x * 2 + 1 - core, ch)],
            r.got[i].at[x, rows_at(ch * half, half)],
            r.rs_send.at[i, ch, x],
            r.rs_recv.at[i, ch, x],
            (page, sibling),
        )

    def rs_far(i, dx, ch):
        to = chip_at(dx) * 2 + core
        slot = X + dx - 1
        return remote(
            r.part[i].at[part_of(to, ch)],
            r.got[i].at[slot, rows_at(ch * half, half)],
            r.rs_send.at[i, ch, slot],
            r.rs_recv.at[i, ch, slot],
            (page, to),
        )

    def rs_start(i, term):
        part, got = r.part[i], r.got[i]
        for n in range(1, X + 1):
            x = chip_at(n)
            at = rows_at((x * 2 + 1 - core) * Tl, Tl)
            part[at, :] = term(at).astype(BF16)
            for ch in range(2):
                rs_copy(i, x, ch).start()
        for dx in range(1, X):
            x = chip_at(dx)
            at = rows_at((x * 2 + core) * Tl, Tl)
            mine = term(at)
            for ch in range(2):
                rs_copy(i, x, ch).wait_recv()
                other = got[x, ch * half : (ch + 1) * half, :].astype(F32)
                part[part_of(x * 2 + core, ch), :] = (mine[ch * half : (ch + 1) * half] + other).astype(BF16)
                rs_far(i, dx, ch).start()
        part[own, :] = term(own).astype(BF16)

    def rs_wait(i, ch):
        rows = slice(ch * half, (ch + 1) * half)
        rs_copy(i, chip, ch).wait_recv()
        total = r.part[i][part_of(seq, ch), :].astype(F32) + r.got[i][chip, rows, :].astype(F32)
        for dx in range(1, X):
            rs_far(i, dx, ch).wait_recv()
            total = total + r.got[i][X + dx - 1, rows, :].astype(F32)
        return total

    def rs_sent(i):
        for ch in range(2):
            for x in range(X):
                rs_copy(i, x, ch).wait_send()
            for dx in range(1, X):
                rs_far(i, dx, ch).wait_send()

    def small_copies(i, level):
        count, base, device = (
            (B, 0, lambda k: (a * B + lax.rem(b + k, B), seq)),
            (A, B - 1, lambda k: (lax.rem(a + k, A) * B + b, seq)),
            (S, A + B - 2, lambda k: (page, lax.rem(seq + k, S))),
        )[level]
        return [
            remote(
                r.small.at[i],
                r.small_got.at[i, base + k - 1],
                r.sm_send.at[base + k - 1],
                r.sm_recv.at[base + k - 1],
                device(k),
            )
            for k in range(1, count)
        ], base

    def small_start(i, level):
        for copy in small_copies(i, level)[0]:
            copy.start()

    def small_wait(i, level):
        copies, base = small_copies(i, level)
        for copy in copies:
            copy.wait()
        total = r.small[i]
        for k in range(len(copies)):
            total = total + r.small_got[i, base + k]
        r.small[i] = total

    def unit_of(arrays, u):
        g, n = (UNITS if arrays is w or arrays is ins else BACK_UNITS)[u]
        return g, slice(n[0] * Fq, n[1] * Fq) if g == UP else n

    def rows_of(arrays, u, j):
        g, n = unit_of(arrays, u)
        size = ins[g].shape[-2]
        at = rows_at(j * size, size)
        if g == UP:
            return arrays[g].at[at, n]
        return arrays[g].at[:, at, :] if n is None else arrays[g].at[n, at, :]

    def whole_of(arrays, u):
        g, n = unit_of(arrays, u)
        if g == UP:
            return arrays[g].at[:, n]
        return arrays[g] if n is None else arrays[g].at[n]

    turned = turned_back = UP_UNITS[1:] if B == 2 else ()
    beside = a * B + 1 - b
    inside = (a > 0) & (a < A - 1)

    def w_slot(u, j, way):
        t, e = lax.div(j, B), lax.rem(j, B)
        over = A if B == 2 else A * B + A
        base = u * (A + 1 + over)
        if way < 2:
            if u in turned:
                base = jnp.where(e == b, base, len(UNITS) * (A + 1 + over))
            return r.w_send.at[base + jnp.where((t == a) & (way == 1), A, t)]
        return r.w_send.at[base + A + 1 + (t if B == 2 else jnp.where((e == b) & (way == 3), A * B + t, j))]

    def w_copy(u, j, way, src=None):
        place = rows_of(w, u, j)
        device = (page + (-B, B, -1, 1)[way], seq)
        return remote(place if src is None else src, place, w_slot(u, j, way), r.w_recv.at[u, j], device)

    ways = (a > 0, a < A - 1, b > 0, b < B - 1)

    def w_forward(u, j, along, src=None):
        for way in along:
            @pl.when(ways[way])
            def _():
                w_copy(u, j, way, src).start()

    def w_local(u):
        return pltpu.make_async_copy(whole_of(ins, u), rows_of(w, u, page), r.w_local.at[u])

    def w_first(*units, along=(0, 1, 2, 3)):
        for u in units:
            w_forward(u, page, along, whole_of(ins, u))
            if 2 in along:
                w_local(u).start()

    def w_turn(*units):
        for u in units:
            landed(rows_of(w, u, beside), r.w_recv.at[u, beside])
            w_forward(u, beside, (0, 1))

    def w_step(d, *units, on=True):
        for u in units:
            for sign, way in ((-1, 1), (1, 0)):
                @pl.when((a + sign * d >= 0) & (a + sign * d < A) & on)
                def _():
                    for column in (page, beside) if u in turned else (page,):
                        j = column + sign * d * B
                        landed(rows_of(w, u, j), r.w_recv.at[u, j])
                        w_forward(u, j, (way,) if u in turned else (way, 2, 3))

    def w_wait(*units):
        for u in units:
            w_local(u).wait()
            for e in range(1, 1 if u in turned else B):
                for t in range(A):
                    @pl.when(b - e >= 0)
                    def _():
                        j = t * B + b - e
                        landed(rows_of(w, u, j), r.w_recv.at[u, j])
                        w_forward(u, j, (3,))

                    @pl.when(b + e < B)
                    def _():
                        j = t * B + b + e
                        landed(rows_of(w, u, j), r.w_recv.at[u, j])
                        w_forward(u, j, (2,))

    def w_sent(u):
        for t in range(A):
            for e in range(B):
                j = t * B + e
                along = ((b == e) & (t >= a), (b == e) & (t <= a), e >= b, e <= b)
                if u in turned:
                    along = (t >= a, t <= a, (b == e) & (t == a), (b == e) & (t == a))
                for way, when in enumerate(along):
                    @pl.when(when & ways[way])
                    def _():
                        w_copy(u, j, way).wait_send()

    def block(array, g, e, n):
        rows, cols = ins[g].shape
        return array.at[rows_at(e * rows, rows), rows_at(n * cols, cols)]

    def m_local(g):
        return pltpu.make_async_copy(ins[g], block(w[g], g, shelf, seq), r.m_got.at[MOVED.index(g), seq])

    def m_collect_copy(g):
        i = MOVED.index(g)
        return remote(
            ins[g], block(w[g], g, shelf, seq), r.m_gave.at[i], r.m_got.at[i, seq], (page, collector)
        )

    def m_collect(g):
        @pl.when(collects)
        def _():
            m_local(g).start()

        @pl.when(jnp.logical_not(collects))
        def _():
            m_collect_copy(g).start()

    def m_copy(g, n, way):
        i = MOVED.index(g)
        place = block(w[g], g, mine, n)
        device = (page + B, page - B)[way] if way < 2 else a * B + lax.rem(b + way - 1, B)
        return remote(place, place, r.m_send.at[i, n, way], r.m_recv.at[i, mine, n], (device, seq))

    m_ways = [holds & (a >= a0) & (a < A - 1), holds & (a <= a0) & (a > 0)] + [holds] * (B - 1)

    def m_forward(g, n):
        for way in range(B + 1):
            @pl.when(m_ways[way])
            def _():
                m_copy(g, n, way).start()

    def m_first(g, n):
        @pl.when(collects)
        def _():
            @pl.when(seq == n)
            def _():
                m_local(g).wait()

            @pl.when(seq != n)
            def _():
                landed(block(w[g], g, shelf, n), r.m_got.at[MOVED.index(g), n])

            m_forward(g, n)

    hops = jnp.abs(a - a0)

    def m_pass(g, n, hop, where):
        @pl.when(holds & (hops == hop) & where)
        def _():
            landed(block(w[g], g, mine, n), r.m_recv.at[MOVED.index(g), mine, n])
            m_forward(g, n)

    def m_wait(g):
        for e in range(R):
            @pl.when(jnp.logical_not(holds) | (mine != e))
            def _():
                for n in range(S):
                    landed(block(w[g], g, e, n), r.m_recv.at[MOVED.index(g), e, n])

    def m_sent(g):
        @pl.when(jnp.logical_not(collects))
        def _():
            m_collect_copy(g).wait_send()

        for n in range(S):
            for way in range(B + 1):
                @pl.when(m_ways[way])
                def _():
                    m_copy(g, n, way).wait_send()

    low = 2 * a < A
    near = jnp.where(low, a, A - 1 - a)

    def order(m):
        if m == A - 1:
            return a
        t = jnp.where(m < A - 1 - near, A - 1 - m, m - (A - 1 - near))
        return jnp.where(low, t, A - 1 - t)

    def y_copy(u, k, t):
        other = lax.rem(b + k, B)
        return remote(
            rows_of(grad, u, t * B + other),
            r.rb[u].at[B - 1 - k, t],
            r.y_send.at[u, k - 1, t],
            r.y_recv.at[u, B - 1 - k, t],
            (a * B + other, seq),
        )

    def y_start(*units):
        for m in range(A):
            for u in units:
                for k in range(1, B):
                    y_copy(u, k, order(m)).start()

    def z_copy(u, t, sign):
        slot = jnp.where((t == a + sign) & (sign < 0), A, t)
        return remote(
            r.rb[u].at[0, t],
            r.zz[u].at[slot],
            r.z_send.at[u, t],
            r.z_recv.at[u, slot],
            (page + sign * B, seq),
        )

    def z_way(t):
        sign = jnp.where(t > a, 1, -1)
        before = a - sign
        return sign, (before >= 0) & (before < A)

    def y_sum(m, u):
        t = order(m)
        total = rows_of(grad, u, t * B + b)[...].astype(F32)
        for slot in range(B - 1):
            landed(r.rb[u].at[slot, t], r.y_recv.at[u, slot, t])
            total = total + r.rb[u][slot, t].astype(F32)
        r.rb[u][0, t] = total.astype(BF16)
        if m < A - 1:
            sign, has = z_way(t)

            @pl.when(jnp.logical_not(has))
            def _():
                z_copy(u, t, sign).start()

    def z_sum(m, u):
        t = order(m)
        sign, has = z_way(t)

        @pl.when(has)
        def _():
            landed(r.zz[u].at[t], r.z_recv.at[u, t])
            r.rb[u][0, t] = (r.rb[u][0, t].astype(F32) + r.zz[u][t].astype(F32)).astype(BF16)
            z_copy(u, t, sign).start()

    def z_total(u):
        @pl.when(a > 0)
        def _():
            landed(r.zz[u].at[a], r.z_recv.at[u, a])

        @pl.when(a < A - 1)
        def _():
            landed(r.zz[u].at[A], r.z_recv.at[u, A])

        total = r.rb[u][0, a].astype(F32)
        total = total + jnp.where(a > 0, r.zz[u][a].astype(F32), 0.0)
        total = total + jnp.where(a < A - 1, r.zz[u][A].astype(F32), 0.0)
        whole_of(outs, u)[...] = total

    def c_copy(u, t, sign, side, src):
        slot = jnp.where((t == a + sign) & (sign < 0), A, t)
        return remote(
            src,
            r.tz.at[side, slot],
            r.tz_send.at[side, t],
            r.tz_recv.at[side, slot],
            (page + sign * B, seq),
        )

    def c_own(u, t, side):
        return rows_of(grad, u, t * B + (b, 1 - b)[side])

    def c_first(u):
        for m in range(A - 1):
            t = order(m)
            sign, has = z_way(t)
            for side in range(2):
                @pl.when(jnp.logical_not(has))
                def _():
                    c_copy(u, t, sign, side, c_own(u, t, side)).start()

    def c_sum(m, u):
        t = order(m)
        sign, has = z_way(t)

        @pl.when(has)
        def _():
            for side in range(2):
                landed(r.tz.at[side, t], r.tz_recv.at[side, t])
                total = c_own(u, t, side)[...].astype(F32) + r.tz[side, t].astype(F32)
                r.ta[side, t] = total.astype(BF16)
                c_copy(u, t, sign, side, r.ta.at[side, t]).start()

    def c_turn(u):
        return remote(r.ta.at[1, a], r.tb, r.y_send.at[u, 0, 0], r.y_recv.at[u, 0, 0], (beside, seq))

    def c_total(u):
        for side in (1, 0):
            total = c_own(u, a, side)[...].astype(F32)
            for has, slot in ((a > 0, a), (a < A - 1, A)):
                @pl.when(has)
                def _():
                    landed(r.tz.at[side, slot], r.tz_recv.at[side, slot])

                total = total + jnp.where(has, r.tz[side, slot].astype(F32), 0.0)
            if side:
                r.ta[1, a] = total.astype(BF16)
                c_turn(u).start()
            else:
                whole_of(outs, u)[...] = total

    def c_end(u):
        landed(r.tb, r.y_recv.at[u, 0, 0])
        whole_of(outs, u)[...] = whole_of(outs, u)[...] + r.tb[...].astype(F32)

    def z_sent(u):
        if u in turned_back:
            c_turn(u).wait_send()
            for m in range(A - 1):
                t = order(m)
                for side in range(2):
                    c_copy(u, t, z_way(t)[0], side, c_own(u, t, side)).wait_send()
            return
        for t in range(A):
            for k in range(1, B):
                y_copy(u, k, t).wait_send()

            @pl.when(t != a)
            def _():
                z_copy(u, t, jnp.where(t > a, 1, -1)).wait_send()

    def f_parts(g):
        return max(QUARTERS // R, 1) if g == DOWN else 1

    def f_copy(g, k, n, part):
        i = MOVED.index(g)
        other = lax.rem(b + k, B)
        rows, cols = ins[g].shape
        size = rows // f_parts(g)
        return remote(
            grad[g].at[rows_at((other - b0) * rows + part * size, size), rows_at(n * cols, cols)],
            r.fb[i].at[B - 1 - k, n, part * size : (part + 1) * size, :],
            r.f_send[i].at[k - 1, n, part],
            r.f_recv[i].at[B - 1 - k, n, part],
            (a * B + other, seq),
        )

    def wanted(k):
        shelf_of = lax.rem(b + k, B) - b0
        return (shelf_of >= 0) & (shelf_of < R)

    def f_start(g, ready=lambda part: True):
        for n in range(S):
            for k in range(1, B):
                for part in range(f_parts(g)):
                    @pl.when(wanted(k) & ready((lax.rem(b + k, B) - b0) * f_parts(g) + part))
                    def _():
                        f_copy(g, k, n, part).start()

    inward = jnp.where(a > a0, -1, 1)
    from_out = holds & (a != a0) & inside
    starts_line = holds & (a != a0) & jnp.logical_not(inside)

    def v_copy(g, n):
        i = MOVED.index(g)
        slot = jnp.where((a + 1 == a0), 1, 0)
        return remote(
            r.fb[i].at[0, n], r.vv[i].at[slot, n], r.v_send.at[i, n], r.v_recv.at[i, slot, n], (page + inward * B, seq)
        )

    def s_copy(g, n):
        i = MOVED.index(g)
        return remote(r.fb[i].at[0, n], r.back[i], r.s_send.at[i, n], r.s_recv.at[i], (page, n))

    def f_sum(g, n):
        i = MOVED.index(g)

        @pl.when(holds)
        def _():
            total = block(grad[g], g, mine, n)[...].astype(F32)
            for slot in range(B - 1):
                for part in range(f_parts(g)):
                    f_copy(g, B - 1 - slot, n, part).wait_recv()
                total = total + r.fb[i][slot, n].astype(F32)
            r.fb[i][0, n] = total.astype(BF16)

            @pl.when(starts_line)
            def _():
                v_copy(g, n).start()

    passed = jnp.where(a > a0, A - 1 - a, a)

    def v_sum(g, n, hop):
        i = MOVED.index(g)

        @pl.when(from_out & (passed == hop))
        def _():
            landed(r.vv[i].at[0, n], r.v_recv.at[i, 0, n])
            r.fb[i][0, n] = (r.fb[i][0, n].astype(F32) + r.vv[i][0, n].astype(F32)).astype(BF16)
            v_copy(g, n).start()

    def v_total(g, n):
        i = MOVED.index(g)

        @pl.when(collects)
        def _():
            @pl.when(a < A - 1)
            def _():
                landed(r.vv[i].at[0, n], r.v_recv.at[i, 0, n])

            @pl.when(a > 0)
            def _():
                landed(r.vv[i].at[1, n], r.v_recv.at[i, 1, n])

            total = r.fb[i][0, n].astype(F32)
            total = total + jnp.where(a < A - 1, r.vv[i][0, n].astype(F32), 0.0)
            total = total + jnp.where(a > 0, r.vv[i][1, n].astype(F32), 0.0)

            @pl.when(seq == n)
            def _():
                outs[g][...] = total

            @pl.when(seq != n)
            def _():
                r.fb[i][0, n] = total.astype(BF16)
                s_copy(g, n).start()

    def s_wait(g):
        i = MOVED.index(g)

        @pl.when(jnp.logical_not(collects))
        def _():
            landed(r.back[i], r.s_recv.at[i])
            outs[g][...] = r.back[i][...].astype(F32)

    def v_sent(g):
        for n in range(S):
            for k in range(1, B):
                for part in range(f_parts(g)):
                    @pl.when(wanted(k))
                    def _():
                        f_copy(g, k, n, part).wait_send()

            @pl.when(starts_line | from_out)
            def _():
                v_copy(g, n).wait_send()

            @pl.when(collects & (seq != n))
            def _():
                s_copy(g, n).wait_send()

    token_live = r.token_counts[0]
    patch_live = r.patch_counts[0]
    r.norm_terms[6:8, :] = jnp.zeros((2, D), F32)
    gains = lambda k: r.small[0, k : k + 1, :]
    biases = lambda k: r.small[0, 3 + k : 4 + k, :]
    QB = min(256, T)
    lane = lax.broadcasted_iota(jnp.int32, (1, LANES), 1)
    halves = [(lane // HEAD_DIM == h) for h in range(2)]
    half_of = [half.astype(F32).astype(BF16) for half in halves]
    scale = HEAD_DIM ** (-0.5)

    def project(dst, left, weight):
        for n, (out, index) in enumerate(dst):
            out[...] = nn(left[...], weight[index]).astype(BF16)

    def attend(q, k, v, o, probs, live, causal):
        @pl.loop(0, Dl // LANES)
        def _(pair):
            cols = rows_at(pair * LANES, LANES)
            for block in range(T // QB):
                extent = (block + 1) * QB if causal else T
                rows = slice(block * QB, (block + 1) * QB)
                q2 = q[rows, cols]
                k2, v2 = k[:extent, cols], v[:extent, cols]
                at = lax.broadcasted_iota(jnp.int32, (QB, extent), 1)
                allowed = at < live
                if causal:
                    row = block * QB + lax.broadcasted_iota(jnp.int32, (QB, extent), 0)
                    allowed = allowed & (at <= row)
                found = []
                for h in range(2):
                    scores = nt(q2 * half_of[h], k2) * scale
                    scores = jnp.where(allowed, scores, -1e30)
                    raised = jnp.exp(scores - jnp.max(scores, axis=-1, keepdims=True))
                    share = (raised / jnp.sum(raised, axis=-1, keepdims=True)).astype(BF16)
                    probs[2 * pair + h, rows, :extent] = share
                    found.append(nn(share, v2))
                o[rows, cols] = jnp.where(halves[0], found[0], found[1]).astype(BF16)

    def attend_back(q, k, v, do, probs, dq, dk, dv, causal):
        @pl.loop(0, Dl // LANES)
        def _(pair):
            cols = rows_at(pair * LANES, LANES)
            r.dk_sum[...] = jnp.zeros_like(r.dk_sum)
            r.dv_sum[...] = jnp.zeros_like(r.dv_sum)
            for block in range(T // QB):
                extent = (block + 1) * QB if causal else T
                rows = slice(block * QB, (block + 1) * QB)
                q2, do2 = q[rows, cols], do[rows, cols]
                k2, v2 = k[:extent, cols], v[:extent, cols]
                dqs, dks, dvs = [], [], []
                for h in range(2):
                    share = probs[2 * pair + h, rows, :extent]
                    wide = share.astype(F32)
                    dp = nt(do2 * half_of[h], v2)
                    delta = jnp.sum(wide * dp, axis=-1, keepdims=True)
                    ds = (wide * (dp - delta)).astype(BF16)
                    dqs.append(nn(ds, k2))
                    dks.append(tn(ds, q2))
                    dvs.append(tn(share, do2))
                dq[rows, cols] = (jnp.where(halves[0], dqs[0], dqs[1]) * scale).astype(BF16)
                r.dk_sum[:extent, :] += jnp.where(halves[0], dks[0], dks[1])
                r.dv_sum[:extent, :] += jnp.where(halves[0], dvs[0], dvs[1])
            dk[:, cols] = (r.dk_sum[...] * scale).astype(BF16)
            dv[:, cols] = r.dv_sum[...].astype(BF16)

    def norm_back(k, values, incoming, ch):
        unit, rate = normed(values)
        for row, term in ((k, incoming * unit), (3 + k, incoming)):
            so_far = jnp.sum(term, axis=0, keepdims=True)
            r.norm_terms[row : row + 1, :] = so_far if ch == 0 else r.norm_terms[row : row + 1, :] + so_far
        dn = incoming * gains(k)
        return rate * (
            dn - jnp.mean(dn, axis=-1, keepdims=True) - unit * jnp.mean(dn * unit, axis=-1, keepdims=True)
        )

    def norm_own(k, values, dst, ch):
        dst[part_of(seq, ch), :] = (normed(values)[0] * gains(k) + biases(k)).astype(BF16)

    few = r.norm_gains.shape[1]
    at_feature = lax.broadcasted_iota(jnp.int32, (few, D), 1)
    placed = at_feature == lax.broadcasted_iota(jnp.int32, (few, D), 0) + (page * S + seq) * few
    plan = []
    SLOW = 5

    def when(time, *steps):
        plan.extend((time, step) for step in steps)

    def each_row_part(step):
        def run():
            for ch in range(2):
                step(ch, slice(ch * half, (ch + 1) * half))

        return run

    results = [
        (r.own_mixed, r.mixed),
        (r.own_input_grad, r.input_grad),
        (r.own_memory_grad, r.memory_grad),
        *((r.sums[g], r.outs[g]) for g in MOVED),
        *((whole_of(r.sums, u), whole_of(r.outs, u)) for u in range(len(UNITS))),
    ]
    O_MIXED, O_INPUT, O_MEMORY, O_MOVED, O_UNITS = 0, 1, 2, 3, 6

    def leave(n):
        kept, out = results[n]
        return pltpu.make_async_copy(kept, out, r.o_sem.at[n])

    def w_moved(g, first, hop_time, gap, end_first, end_gap):
        ends = jnp.logical_not(inside)
        for n in range(S):
            when(first + n * gap, lambda n=n: m_first(g, n))
            for hop in range(1, A):
                time = first + n * gap + hop * hop_time
                if hop < A - 1:
                    when(time, lambda n=n, hop=hop: m_pass(g, n, hop, inside))
                if hop > 1:
                    time = end_first + n * end_gap + hop / 10
                when(time, lambda n=n, hop=hop: m_pass(g, n, hop, ends))

    def g_moved(g, first, hop_time, gap, late, last):
        for n in range(S):
            time = first + n * gap
            when(time, lambda n=n: f_sum(g, n))
            for hop in range(1, A - 1):
                when(time + late + hop * hop_time + (hop - 1) * SLOW, lambda n=n, hop=hop: v_sum(g, n, hop))
            when(last, lambda n=n: v_total(g, n))

    def g_units(units, first, hop_time, gap, late):
        for place, u in enumerate(units):
            time = first + gap * place / len(units)
            for m in range(A):
                when(time + gap * m, lambda m=m, u=u: y_sum(m, u))
            for m in range(A - 2):
                when(time + gap * m + late + hop_time, lambda m=m, u=u: z_sum(m, u))
            after = time + late + 2 * hop_time + SLOW
            when(max(after, time + gap * (A - 2)), lambda u=u: z_sum(A - 2, u))
            when(188, lambda u=u: z_total(u), lambda u=u: leave(O_UNITS + u).start())

    given = (
        (G_TOKENS, r.tokens, r.all_tokens), (G_MEMORY, r.memory, r.all_memory), (G_COT, r.cotangent, r.dyr)
    )
    loads = [pltpu.make_async_copy(piece, everyone.at[own], r.ld_sem.at[i]) for i, piece, everyone in given]

    def begin():
        r.small[0] = jnp.zeros((8, D), F32)
        r.small[0, 0:3, :] = nn(r.norm_gains[...], placed.astype(F32).astype(BF16))
        r.small[0, 3:6, :] = nn(r.norm_biases[...], placed.astype(F32).astype(BF16))
        small_start(0, 0)
        w_first(*SELF_UNITS)
        w_first(*turned, along=(2, 3))
        m_collect(SELF_OUT)
        ag_begin(*given[0])
        for load in loads:
            load.start()

    def small_next(i, level):
        small_wait(i, level)
        small_start(i, level + 1 if i == 0 else level - 1)

    def take_tokens():
        small_wait(0, 2)
        ag_wait(G_TOKENS, r.all_tokens)
        for load in loads:
            load.wait()

        @pl.loop(0, S)
        def _(n):
            at = rows_at(n * Tl, Tl)
            values = r.all_tokens[at, :].astype(F32)
            r.a1[at, :] = (normed(values)[0] * gains(0) + biases(0)).astype(BF16)

    def self_project():
        w_wait(*SELF_UNITS)
        project(((r.q, 0), (r.k, 1), (r.v, 2)), r.a1, w[SELF])

    def self_sum():
        m_wait(SELF_OUT)
        rs_start(R_CHAIN, lambda at: nn(r.o[at, :], w[SELF_OUT][...]))

    @each_row_part
    def self_add(ch, rows):
        r.x1[rows, :] = r.all_tokens[part_of(seq, ch), :].astype(F32) + rs_wait(R_CHAIN, ch)
        norm_own(1, r.x1[rows, :], r.a2, ch)
        ag_start(G_A2, r.a2.at[own], r.a2, ch)

    def memory_project():
        w_wait(*CROSS_UNITS)
        ag_wait(G_MEMORY, r.all_memory)
        project(((r.kc, 1), (r.vc, 2)), r.all_memory, w[CROSS])

    def cross_project():
        ag_wait(G_A2, r.a2)
        project(((r.qc, 0),), r.a2, w[CROSS])

    def cross_sum():
        m_wait(CROSS_OUT)
        rs_sent(R_CHAIN)
        rs_start(R_CHAIN, lambda at: nn(r.oc[at, :], w[CROSS_OUT][...]))

    def take_cotangent():
        ag_wait(G_COT, r.dyr)
        ag_sent(*given[2])

        @pl.loop(0, S)
        def _(n):
            at = rows_at(n * Tl, Tl)
            row = n * Tl + lax.broadcasted_iota(jnp.int32, (Tl, 1), 0)
            values = r.dyr[at, :].astype(F32)
            r.dyr[at, :] = jnp.where(row < token_live, values, 0.0).astype(BF16)

    @each_row_part
    def cross_add(ch, rows):
        r.x2[rows, :] = r.x1[rows, :] + rs_wait(R_CHAIN, ch)
        norm_own(2, r.x2[rows, :], r.a3, ch)
        ag_start(G_A3, r.a3.at[own], r.a3, ch)

    def hidden_units(lo, hi):
        @pl.loop(lo, hi)
        def _(n):
            cols = rows_at(n * Fq, Fq)
            out, slope = gelu_pair(nn(r.a3[...], w[UP][:, cols]))
            r.g[:, cols] = out.astype(BF16)
            r.slope[:, cols] = slope

    def down_grad(lo, hi):
        @pl.loop(lo, hi)
        def _(n):
            cols = rows_at(n * Fq, Fq)
            grad[DOWN][cols, :] = tn(r.g[:, cols], r.dyr[...]).astype(BF16)

    def hidden_grad(lo, hi):
        @pl.loop(lo, hi)
        def _(n):
            cols = rows_at(n * Fq, Fq)
            r.du[:, cols] = (nt(r.dyr[...], w[DOWN][cols, :]) * r.slope[:, cols]).astype(BF16)

    def up_grad(lo, hi):
        if lo < hi:
            @pl.loop(0, D // 256)
            def _(n):
                cols = rows_at(n * 256, 256)
                grad[UP][cols, lo * Fq : hi * Fq] = tn(r.a3[:, cols], r.du[:, lo * Fq : hi * Fq]).astype(BF16)

    straight = tuple(u for u in UP_UNITS if u not in turned)
    ahead = UNITS[UP_UNITS[1]][1][0] if turned else QUARTERS
    back_from = BACK_UNITS[UP_UNITS[1]][1][0] if turned_back else QUARTERS

    def hidden():
        w_wait(*straight)
        ag_wait(G_A3, r.a3)
        hidden_units(0, ahead)
        down_grad(0, ahead)

    def hidden_rest():
        if turned:
            for d in range(1, A):
                w_step(d, *turned, on=jnp.logical_not(inside))
            w_wait(*turned)
            f_start(DOWN, lambda part: part < ahead)
            hidden_units(ahead, QUARTERS)
            down_grad(ahead, QUARTERS)
            f_start(DOWN, lambda part: part >= ahead)
        else:
            f_start(DOWN)

    when(0, begin)
    when(6, lambda: w_step(1, *SELF_UNITS))
    when(8, lambda: small_next(0, 0), lambda: m_collect(CROSS_OUT), lambda: ag_begin(*given[1]), lambda: m_collect(DOWN))
    when(12, lambda: w_step(2, *SELF_UNITS))
    w_moved(SELF_OUT, 13, 4, 0.1, 25, 0.1)
    when(15, lambda: small_next(0, 1), lambda: ag_forward(G_TOKENS, r.all_tokens), lambda: ag_begin(*given[2]))
    when(16.5, lambda: w_step(3, *SELF_UNITS))
    when(17.5, lambda: w_first(*CROSS_UNITS, along=(2, 3)))
    when(17.5, lambda: w_first(*CROSS_UNITS, along=(0, 1)))
    when(22, lambda: w_first(*straight))
    when(23.5, lambda: w_step(1, *CROSS_UNITS))
    when(24.5, take_tokens)
    when(27, self_project)
    when(29, lambda: w_step(2, *CROSS_UNITS))
    w_moved(CROSS_OUT, 30, 5, 0.1, 46, 0.1)
    when(31, lambda: ag_forward(G_MEMORY, r.all_memory))
    when(32, lambda: attend(r.q, r.k, r.v, r.o, r.p, token_live, True))
    when(34.5, lambda: w_step(3, *CROSS_UNITS))
    when(36, self_sum)
    when(37, lambda: w_step(1, *straight))
    w_moved(DOWN, 37.5, 7.5, 3, 60, 5)
    when(42, lambda: ag_forward(G_COT, r.dyr))
    when(43, lambda: w_step(2, *straight))
    when(46, self_add)
    when(51, lambda: w_first(*turned, along=(0, 1)))
    when(48, memory_project)
    when(49, lambda: w_step(3, *straight))
    when(50, lambda: w_turn(*turned))
    when(52, lambda: ag_forward(G_A2, r.a2))
    when(53.2, cross_project)
    when(54, lambda: attend(r.qc, r.kc, r.vc, r.oc, r.pc, patch_live, False))
    when(57, cross_sum)
    when(62, lambda: w_step(1, *turned, on=inside))
    when(61, take_cotangent)
    when(67, cross_add)
    when(69, lambda: w_step(2, *turned, on=inside))
    when(75, lambda: ag_forward(G_A3, r.a3))
    when(76, hidden)
    when(84, hidden_rest)

    def hidden_back():
        m_wait(DOWN)
        hidden_grad(back_from, QUARTERS)
        up_grad(back_from, QUARTERS)
        for u in turned_back:
            c_first(u)
        hidden_grad(0, back_from)
        ag_sent(G_A3, r.a3.at[own], r.a3)
        rs_sent(R_CHAIN)
        rs_start(R_CHAIN, lambda at: nt(r.du[at, :], w[UP][...]))

    def up_grad_rest():
        up_grad(0, back_from)
        y_start(*(u for u in UP_UNITS if u not in turned_back))

    @each_row_part
    def hidden_add(ch, rows):
        back_term = norm_back(2, r.x2[rows, :], rs_wait(R_CHAIN, ch), ch)
        r.dx2[rows, :] = r.dyr[part_of(seq, ch), :].astype(F32) + back_term
        r.dz2[part_of(seq, ch), :] = r.dx2[rows, :].astype(BF16)
        ag_start(G_DZ2, r.dz2.at[own], r.dz2, ch)

    def cross_back():
        ag_wait(G_DZ2, r.dz2)
        grad[CROSS_OUT][...] = tn(r.oc[...], r.dz2[...]).astype(BF16)
        f_start(CROSS_OUT)
        r.do[...] = nt(r.dz2[...], w[CROSS_OUT][...]).astype(BF16)
        attend_back(r.qc, r.kc, r.vc, r.do, r.pc, r.dq, r.dkc, r.dvc, False)

    def cross_back_sum():
        rs_sent(R_CHAIN)
        rs_start(R_CHAIN, lambda at: nt(r.dq[at, :], w[CROSS][0]))

    def cross_grad():
        for n, (left, right) in enumerate(((r.a2, r.dq), (r.all_memory, r.dkc), (r.all_memory, r.dvc))):
            grad[CROSS][n] = tn(left[...], right[...]).astype(BF16)
        y_start(*CROSS_UNITS)

    @each_row_part
    def cross_back_add(ch, rows):
        r.dx1[rows, :] = r.dx2[rows, :] + norm_back(1, r.x1[rows, :], rs_wait(R_CHAIN, ch), ch)
        r.dz1[part_of(seq, ch), :] = r.dx1[rows, :].astype(BF16)
        ag_start(G_DZ1, r.dz1.at[own], r.dz1, ch)

    def self_back():
        ag_wait(G_DZ1, r.dz1)
        grad[SELF_OUT][...] = tn(r.o[...], r.dz1[...]).astype(BF16)
        f_start(SELF_OUT)
        r.do[...] = nt(r.dz1[...], w[SELF_OUT][...]).astype(BF16)
        attend_back(r.q, r.k, r.v, r.do, r.p, r.dq, r.dk, r.dv, True)
        for n, right in enumerate((r.dq, r.dk, r.dv)):
            grad[SELF][n] = tn(r.a1[...], right[...]).astype(BF16)
        y_start(*SELF_UNITS)

    def self_back_sum():
        rs_sent(R_CHAIN)
        rs_start(
            R_CHAIN,
            lambda at: nt(r.dq[at, :], w[SELF][0]) + nt(r.dk[at, :], w[SELF][1]) + nt(r.dv[at, :], w[SELF][2]),
        )

    def memory_sum():
        ag_sent(G_A2, r.a2.at[own], r.a2)
        rs_start(R_MEMORY, lambda at: nt(r.dkc[at, :], w[CROSS][1]) + nt(r.dvc[at, :], w[CROSS][2]))

    @each_row_part
    def input_add(ch, rows):
        back_term = norm_back(0, r.all_tokens[part_of(seq, ch), :].astype(F32), rs_wait(R_CHAIN, ch), ch)
        r.own_input_grad[rows, :] = r.dx1[rows, :] + back_term

    def small_last():
        r.small[1] = r.norm_terms[...]
        small_start(1, 2)

    def mixed_sum():
        ag_sent(G_DZ2, r.dz2.at[own], r.dz2)
        rs_start(R_MIXED, lambda at: nn(r.g[at, :], w[DOWN][...]))

    @each_row_part
    def memory_add(ch, rows):
        r.own_memory_grad[rows, :] = rs_wait(R_MEMORY, ch)

    @each_row_part
    def mixed_add(ch, rows):
        live_row = (seq * Tl + ch * half + lax.broadcasted_iota(jnp.int32, (half, 1), 0)) < token_live
        r.own_mixed[rows, :] = jnp.where(live_row, r.x2[rows, :] + rs_wait(R_MIXED, ch), 0.0).astype(BF16)

    def norms_out():
        small_wait(1, 0)
        picked = lax.dot_general(
            r.small[1],
            placed.astype(F32),
            (((1,), (1,)), ((), ())),
            precision=lax.Precision.HIGHEST,
            preferred_element_type=F32,
        )
        r.gains_grad[...] = picked[0:3]
        r.biases_grad[...] = picked[3:6]

    when(87, hidden_back)
    when(95, up_grad_rest)
    if turned_back:
        when(99, lambda: c_sum(0, UP_UNITS[1]))
        when(102, lambda: c_sum(1, UP_UNITS[1]))
        when(105, lambda: c_sum(2, UP_UNITS[1]))
        when(112, lambda: c_total(UP_UNITS[1]))
        when(142, lambda: c_end(UP_UNITS[1]), lambda: leave(O_UNITS + UP_UNITS[1]).start())
        g_moved(DOWN, 98, 7.2, 5.6, 4, 155)
        g_units(UP_UNITS[:1], 122, 6, 4.2, 5)
    else:
        g_moved(DOWN, 97, 7.2, 5.6, 0, 155)
        g_units(UP_UNITS, 121, 4.5, 5.6, 0)
    when(103, hidden_add)
    when(109, lambda: ag_forward(G_DZ2, r.dz2))
    when(111, cross_back)
    when(117, cross_back_sum)
    when(119, cross_grad)
    when(126.5, cross_back_add)
    when(132.5, lambda: ag_forward(G_DZ1, r.dz1))
    when(134.5, self_back)
    when(140.5, self_back_sum)
    g_moved(CROSS_OUT, 138, 3.2, 1.4, 4, 172)
    when(145, memory_sum)
    g_units(CROSS_UNITS, 144, 6, 4.2, 4)
    when(149, input_add, lambda: leave(O_INPUT).start())
    when(150, small_last)
    when(153, mixed_sum)
    when(160, lambda: small_next(1, 2))
    when(179, memory_add, lambda: leave(O_MEMORY).start())
    g_moved(SELF_OUT, 159, 3.2, 1.4, 4, 183)
    when(177, lambda: small_next(1, 1))
    when(179, mixed_add, lambda: leave(O_MIXED).start())
    g_units(SELF_UNITS, 166, 6, 4.2, 0)
    for time, g in ((179, DOWN), (179, CROSS_OUT), (190, SELF_OUT)):
        when(time, lambda g=g: s_wait(g), lambda g=g: leave(O_MOVED + MOVED.index(g)).start())
    when(190, norms_out)

    for _, step in sorted(plan, key=lambda entry: entry[0]):
        step()

    for n in range(len(results)):
        leave(n).wait()
    for i in (R_CHAIN, R_MIXED, R_MEMORY):
        rs_sent(i)
    for i, piece, everyone in given[:2]:
        ag_sent(i, piece, everyone)
    ag_sent(G_DZ1, r.dz1.at[own], r.dz1)
    for u in range(len(UNITS)):
        w_sent(u)
        z_sent(u)
    for g in MOVED:
        m_sent(g)
        v_sent(g)


def layer_call(A, B, S, rows, weights, norms, counts):
    V = pltpu.VMEM
    Tl, D = rows[0].shape
    T = Tl * S
    Dl = weights[SELF].shape[2]
    Fl = weights[UP].shape[1]
    pages = A * B
    R = pages // S
    heads = Dl // HEAD_DIM
    shards = [x.shape for x in weights]
    full = []
    for g, s in enumerate(shards):
        if g in (SELF, CROSS):
            full.append((s[0], s[1] * pages, s[2]))
        elif g == UP:
            full.append((s[0] * pages, s[1]))
        else:
            full.append((s[0] * R, s[1] * S))
    hbm, vmem, smem = (pl.BlockSpec(memory_space=m) for m in (pl.ANY, V, pltpu.SMEM))
    shape = jax.ShapeDtypeStruct
    dma = pltpu.SemaphoreType.DMA
    small_slots = S + A + B - 3
    units = len(UNITS)
    pieces = [
        (shards[g][0], (n[1] - n[0]) * Fl // QUARTERS) if g == UP else shards[g] if n is None else shards[g][1:]
        for g, n in BACK_UNITS
    ]
    turn = pieces[-1]
    if B == 2:
        pieces[-1] = (16, LANES)
    else:
        turn = (16, LANES)
    row_ref, wide_ref = V((T, D), BF16), V((T, Dl), BF16)
    own_ref, hidden_ref = V((Tl, D), F32), V((T, Fl), BF16)
    operands = dict(
        tokens=rows[0],
        memory=rows[1],
        cotangent=rows[2],
        ins=list(weights),
        norm_gains=norms[0],
        norm_biases=norms[1],
        token_counts=counts[0],
        patch_counts=counts[1],
    )
    specs = dict(
        tokens=hbm, memory=hbm, cotangent=hbm, ins=[hbm] * 6, norm_gains=vmem, norm_biases=vmem, token_counts=smem, patch_counts=smem
    )
    results = dict(
        mixed=shape((Tl, D), BF16),
        input_grad=shape((Tl, D), F32),
        memory_grad=shape((Tl, D), F32),
        outs=[shape(s, F32) for s in shards],
        gains_grad=shape(norms[0].shape, F32),
        biases_grad=shape(norms[1].shape, F32),
    )
    scratch = dict(
        w=[V(s, BF16) for s in full],
        grad=[V(s, BF16) for s in full],
        rb=[V((B - 1, A, *piece), BF16) for piece in pieces],
        zz=[V((A + 1, *piece), BF16) for piece in pieces],
        ta=V((2, A, *turn), BF16),
        tz=V((2, A + 1, *turn), BF16),
        tb=V(turn, BF16),
        fb=[V((B - 1, S, *shards[g]), BF16) for g in MOVED],
        vv=[V((2, S, *shards[g]), BF16) for g in MOVED],
        back=[V(shards[g], BF16) for g in MOVED],
        all_tokens=row_ref,
        all_memory=row_ref,
        dyr=row_ref,
        a1=row_ref,
        a2=row_ref,
        a3=row_ref,
        dz2=row_ref,
        q=wide_ref,
        k=wide_ref,
        v=wide_ref,
        o=wide_ref,
        qc=wide_ref,
        kc=wide_ref,
        vc=wide_ref,
        oc=wide_ref,
        do=wide_ref,
        dq=wide_ref,
        dk=wide_ref,
        dv=wide_ref,
        dkc=wide_ref,
        dvc=wide_ref,
        p=V((heads, T, T), BF16),
        pc=V((heads, T, T), BF16),
        g=hidden_ref,
        du=hidden_ref,
        slope=V((T, Fl), F32),
        x1=own_ref,
        x2=own_ref,
        dx1=own_ref,
        dx2=own_ref,
        dk_sum=V((T, LANES), F32),
        dv_sum=V((T, LANES), F32),
        chain_part=row_ref,
        got=[V((S - 1, Tl, D), BF16)] * 3,
        own_mixed=V((Tl, D), BF16),
        own_input_grad=own_ref,
        own_memory_grad=own_ref,
        sums=[V(s, F32) for s in shards],
        small=V((2, 8, D), F32),
        small_got=V((2, small_slots, 8, D), F32),
        norm_terms=V((8, D), F32),
        ag_send=[dma((1 if i <= G_COT else 2, S - 1)) for i in range(7)],
        ag_recv=[dma((1 if i <= G_COT else 2, S)) for i in range(7)],
        rs_send=dma((3, 2, S - 1)),
        rs_recv=dma((3, 2, S - 1)),
        sm_send=dma((small_slots,)),
        sm_recv=dma((small_slots,)),
        ld_sem=dma((3,)),
        o_sem=dma((units + 6,)),
        w_send=dma((units * (A + 1 + (A if B == 2 else pages + A)) + A + 1,)),
        w_recv=dma((units, pages)),
        w_local=dma((units,)),
        y_send=dma((units, B - 1, A)),
        y_recv=dma((units, B - 1, A)),
        z_send=dma((units, A)),
        z_recv=dma((units, A + 1)),
        tz_send=dma((2, A)),
        tz_recv=dma((2, A + 1)),
        m_gave=dma((3,)),
        m_got=dma((3, S)),
        m_send=dma((3, S, B + 1)),
        m_recv=dma((3, R, S)),
        f_send=[dma((B - 1, S, max(QUARTERS // R, 1) if g == DOWN else 1)) for g in MOVED],
        f_recv=[dma((B - 1, S, max(QUARTERS // R, 1) if g == DOWN else 1)) for g in MOVED],
        v_send=dma((3, S)),
        v_recv=dma((3, 2, S)),
        s_send=dma((3, S)),
        s_recv=dma((3,)),
    )
    parts = [jax.tree.flatten(part) for part in (operands, specs, results, scratch)]
    values, in_specs, out_shape, scratch_shapes = (leaves for leaves, _ in parts)
    ends = [len(values), len(values) + len(out_shape)]

    def kernel(*refs):
        held = (refs[: ends[0]], refs[ends[0] : ends[1]], refs[ends[1] :])
        r = types.SimpleNamespace()
        for (_, tree), some in zip((parts[0], parts[2], parts[3]), held):
            vars(r).update(jax.tree.unflatten(tree, some))
        layer_kernel(A, B, S, r)

    found = pl.pallas_call(
        kernel,
        out_shape=out_shape,
        in_specs=in_specs,
        out_specs=[vmem if s.shape == norms[0].shape else hbm for s in out_shape],
        scratch_shapes=scratch_shapes,
        compiler_params=pltpu.CompilerParams(
            collective_id=0, has_side_effects=True, vmem_limit_bytes=62 * 2**20
        ),
        name="layer",
    )(*values)
    return jax.tree.unflatten(parts[2][1], found)


def keep_kernel(*refs):
    *arrays, sems = refs
    count = len(arrays) // 3
    given, kept, held = (arrays[n * count : (n + 1) * count] for n in range(3))
    loads = [pltpu.make_async_copy(given[n], held[n], sems.at[0, n]) for n in range(count)]
    stores = [pltpu.make_async_copy(held[n], kept[n], sems.at[1, n]) for n in range(count)]
    for load in loads:
        load.start()
    for load, store in zip(loads, stores):
        load.wait()
        store.start()
    for store in stores:
        store.wait()


def keep(*arrays):
    hbm = pl.BlockSpec(memory_space=pl.ANY)
    return pl.pallas_call(
        keep_kernel,
        out_shape=[jax.ShapeDtypeStruct(x.shape, x.dtype) for x in arrays],
        in_specs=[hbm] * len(arrays),
        out_specs=[hbm] * len(arrays),
        scratch_shapes=[pltpu.VMEM(x.shape, x.dtype) for x in arrays]
        + [pltpu.SemaphoreType.DMA((2, len(arrays)))],
        name="keep",
    )(*arrays)


def per_device(
    tokens,
    memory,
    cotangent,
    self_qkv,
    self_out,
    cross_qkv,
    cross_out,
    up_weight,
    down_weight,
    norm_gains,
    norm_biases,
    token_counts,
    patch_counts,
):
    pages = lax.axis_size("page")
    parts = lax.axis_size("seq")
    wide = 2 if pages == 8 else 8
    found = layer_call(
        pages // wide,
        wide,
        parts,
        (tokens[0], memory[0], cotangent[0]),
        (self_qkv, self_out, cross_qkv, cross_out, up_weight, down_weight),
        (norm_gains, norm_biases),
        (token_counts, patch_counts),
    )
    return keep(
        found["mixed"][None],
        found["input_grad"][None],
        found["memory_grad"][None],
        *found["outs"],
        found["gains_grad"],
        found["biases_grad"],
    )


def solution(mesh):
    rows = P("page", "seq", None)
    stack = P(None, "page", "seq")
    flat = P("page", "seq")
    norm = P(None, ("page", "seq"))
    counts = P("page")
    return jax.shard_map(
        per_device,
        mesh=mesh,
        in_specs=(rows, rows, rows, stack, flat, stack, flat, flat, flat, norm, norm, counts, counts),
        out_specs=(rows, rows, rows, stack, flat, stack, flat, flat, flat, norm, norm),
        check_vma=False,
    )
```

```python
import types

import jax
import jax.numpy as jnp
from jax import lax
from jax.experimental import pallas as pl
from jax.experimental.pallas import tpu as pltpu
from jax.sharding import PartitionSpec as P

HEAD_DIM = 64
F32 = jnp.float32
BF16 = jnp.bfloat16
MESH = pl.DeviceIdType.MESH
SELF, SELF_OUT, CROSS, CROSS_OUT, UP, DOWN = range(6)
MOVED = (SELF_OUT, CROSS_OUT, DOWN)
QUARTERS = 4
UNITS = ((SELF, 0), (SELF, 1), (SELF, 2), (CROSS, None), (UP, (0, 2)), (UP, (2, 4)))
BACK_UNITS = ((SELF, 0), (SELF, 1), (SELF, 2), (CROSS, None), (UP, (0, 3)), (UP, (3, 4)))
SELF_UNITS, CROSS_UNITS, UP_UNITS = (0, 1, 2), (3,), (4, 5)
G_TOKENS, G_MEMORY, G_COT, G_A2, G_A3, G_DZ2, G_DZ1 = range(7)
R_CHAIN, R_MIXED, R_MEMORY = range(3)
LANES = 128


def nn(left, right):
    return lax.dot_general(left, right, (((1,), (0,)), ((), ())), preferred_element_type=F32)


def nt(left, right):
    return lax.dot_general(left, right, (((1,), (1,)), ((), ())), preferred_element_type=F32)


def tn(left, right):
    return lax.dot_general(left, right, (((0,), (0,)), ((), ())), preferred_element_type=F32)


def rows_at(start, size):
    return pl.ds(pl.multiple_of(start, size), size)


def normed(values):
    center = values - jnp.mean(values, axis=-1, keepdims=True)
    rate = lax.rsqrt(jnp.mean(center * center, axis=-1, keepdims=True) + 1e-05)
    return center * rate, rate


def gelu_pair(values):
    chance = 0.5 + 0.5 * lax.erf(values * 0.7071067811865476)
    density = jnp.exp(-0.5 * values * values) * 0.3989422804014327
    return values * chance, chance + values * density


def layer_kernel(A, B, S, r):
    r.dz1 = r.a3
    r.part = [r.chain_part, r.dz2, r.a2]
    ins, w, grad, outs = r.ins, r.w, r.grad, r.sums
    page, seq = lax.axis_index("page"), lax.axis_index("seq")
    a, b = lax.div(page, B), lax.rem(page, B)
    R = A * B // S
    Tl, D = r.tokens.shape
    T = Tl * S
    Dl = ins[SELF].shape[2]
    Fl = ins[UP].shape[1]
    Fq = Fl // QUARTERS
    own = rows_at(seq * Tl, Tl)
    shelf, collector = lax.rem(page, R), lax.div(page, R)
    collects = seq == collector
    a0, b0 = lax.div(seq * R, B), lax.rem(seq * R, B)
    mine = b - b0
    holds = (mine >= 0) & (mine < R)

    def remote(src, dst, send, recv, device):
        return pltpu.make_async_remote_copy(
            src_ref=src, dst_ref=dst, send_sem=send, recv_sem=recv, device_id=device, device_id_type=MESH
        )

    def landed(dst, recv):
        remote(dst, dst, recv, recv, (page, seq)).wait_recv()

    barrier = pltpu.get_barrier_semaphore()

    def greet(device):
        pl.semaphore_signal(barrier, inc=1, device_id=device, device_id_type=MESH)

    for k in range(1, S):
        greet((page, lax.rem(seq + k, S)))
    for k in range(1, B):
        greet((a * B + lax.rem(b + k, B), seq))
    for k in range(1, A):
        greet((lax.rem(a + k, A) * B + b, seq))

    pl.semaphore_wait(barrier, S + A + B - 3)

    X = S // 2
    chip, core = lax.div(seq, 2), lax.rem(seq, 2)
    sibling = chip * 2 + 1 - core
    half = Tl // 2

    def part_of(source, ch, parts=2):
        size = Tl // parts
        return rows_at(source * Tl + ch * size, size)

    def parts_of(i):
        return 1 if i <= G_COT else 2

    def chip_at(dx):
        return lax.rem(chip + dx, X)

    def ag_copy(i, src, dst, ch, n):
        source = chip_at(2 * X - 1 - n) * 2 + core if n >= X else seq
        parts = parts_of(i)
        mine = dst.at[part_of(source, ch, parts)] if n >= X else src.at[rows_at(ch * (Tl // parts), Tl // parts)]
        to = chip_at(n) * 2 + core if 0 < n < X else sibling
        place = dst.at[part_of(source, ch, parts)]
        return remote(mine, place, r.ag_send[i].at[ch, n], r.ag_recv[i].at[ch, source], (page, to))

    def ag_start(i, src, dst, ch):
        for n in (*range(1, X), 0):
            ag_copy(i, src, dst, ch, n).start()

    def ag_begin(i, src, dst):
        for ch in range(parts_of(i)):
            ag_start(i, src, dst, ch)

    def ag_forward(i, dst):
        for ch in range(parts_of(i)):
            for n in range(X, 2 * X - 1):
                source = chip_at(2 * X - 1 - n) * 2 + core
                landed(dst.at[part_of(source, ch, parts_of(i))], r.ag_recv[i].at[ch, source])
                ag_copy(i, None, dst, ch, n).start()

    def ag_wait(i, dst):
        for ch in range(parts_of(i)):
            for x in range(X):
                source = 2 * x + 1 - core
                landed(dst.at[part_of(source, ch, parts_of(i))], r.ag_recv[i].at[ch, source])

    def ag_sent(i, src, dst):
        for ch in range(parts_of(i)):
            for n in range(2 * X - 1):
                ag_copy(i, src, dst, ch, n).wait_send()

    def rs_parts(i):
        return 2 if i == R_CHAIN else 1

    def rs_copy(i, x, ch):
        return remote(
            r.part[i].at[part_of(x * 2 + 1 - core, ch, rs_parts(i))],
            r.got[i].at[x, rows_at(ch * (Tl // rs_parts(i)), Tl // rs_parts(i))],
            r.rs_send[i].at[ch, x],
            r.rs_recv[i].at[ch, x],
            (page, sibling),
        )

    def rs_far(i, dx, ch):
        to = chip_at(dx) * 2 + core
        slot = X + dx - 1
        return remote(
            r.part[i].at[part_of(to, ch, rs_parts(i))],
            r.got[i].at[slot, rows_at(ch * (Tl // rs_parts(i)), Tl // rs_parts(i))],
            r.rs_send[i].at[ch, slot],
            r.rs_recv[i].at[ch, slot],
            (page, to),
        )

    def rs_start(i, term):
        part, got = r.part[i], r.got[i]
        for n in range(1, X + 1):
            x = chip_at(n)
            at = rows_at((x * 2 + 1 - core) * Tl, Tl)
            part[at, :] = term(at).astype(BF16)
            for ch in range(rs_parts(i)):
                rs_copy(i, x, ch).start()
        for dx in range(1, X):
            x = chip_at(dx)
            at = rows_at((x * 2 + core) * Tl, Tl)
            mine = term(at)
            for ch in range(rs_parts(i)):
                rs_copy(i, x, ch).wait_recv()
                rows = slice(ch * (Tl // rs_parts(i)), (ch + 1) * (Tl // rs_parts(i)))
                other = got[x, rows, :].astype(F32)
                part[part_of(x * 2 + core, ch, rs_parts(i)), :] = (mine[rows] + other).astype(BF16)
                rs_far(i, dx, ch).start()
        part[own, :] = term(own).astype(BF16)

    def rs_wait(i, ch):
        rows = slice(ch * half, (ch + 1) * half)
        if ch < rs_parts(i):
            rs_copy(i, chip, ch).wait_recv()
        total = r.part[i][part_of(seq, ch), :].astype(F32) + r.got[i][chip, rows, :].astype(F32)
        for dx in range(1, X):
            if ch < rs_parts(i):
                rs_far(i, dx, ch).wait_recv()
            total = total + r.got[i][X + dx - 1, rows, :].astype(F32)
        return total

    def rs_sent(i):
        for ch in range(rs_parts(i)):
            for x in range(X):
                rs_copy(i, x, ch).wait_send()
            for dx in range(1, X):
                rs_far(i, dx, ch).wait_send()

    def small_copies(i, level):
        count, base, device = (
            (B, 0, lambda k: (a * B + lax.rem(b + k, B), seq)),
            (A, B - 1, lambda k: (lax.rem(a + k, A) * B + b, seq)),
            (S, A + B - 2, lambda k: (page, lax.rem(seq + k, S))),
        )[level]
        return [
            remote(
                r.small.at[i],
                r.small_got.at[i, base + k - 1],
                r.sm_send.at[base + k - 1],
                r.sm_recv.at[base + k - 1],
                device(k),
            )
            for k in range(1, count)
        ], base

    def small_start(i, level):
        for copy in small_copies(i, level)[0]:
            copy.start()

    def small_wait(i, level):
        copies, base = small_copies(i, level)
        for copy in copies:
            copy.wait()
        total = r.small[i]
        for k in range(len(copies)):
            total = total + r.small_got[i, base + k]
        r.small[i] = total

    def unit_of(arrays, u):
        g, n = (UNITS if arrays is w or arrays is ins else BACK_UNITS)[u]
        return g, slice(n[0] * Fq, n[1] * Fq) if g == UP else n

    def rows_of(arrays, u, j):
        g, n = unit_of(arrays, u)
        size = ins[g].shape[-2]
        at = rows_at(j * size, size)
        if g == UP:
            return arrays[g].at[at, n]
        return arrays[g].at[:, at, :] if n is None else arrays[g].at[n, at, :]

    def whole_of(arrays, u):
        g, n = unit_of(arrays, u)
        if g == UP:
            return arrays[g].at[:, n]
        return arrays[g] if n is None else arrays[g].at[n]

    turned = turned_back = UP_UNITS[1:] if B == 2 else ()
    beside = a * B + 1 - b
    inside = (a > 0) & (a < A - 1)

    def w_slot(u, j, way):
        t, e = lax.div(j, B), lax.rem(j, B)
        over = A if B == 2 else A * B + A
        base = u * (A + 1 + over)
        if way < 2:
            if u in turned:
                base = jnp.where(e == b, base, len(UNITS) * (A + 1 + over))
            return r.w_send.at[base + jnp.where((t == a) & (way == 1), A, t)]
        return r.w_send.at[base + A + 1 + (t if B == 2 else jnp.where((e == b) & (way == 3), A * B + t, j))]

    def w_copy(u, j, way, src=None):
        place = rows_of(w, u, j)
        device = (page + (-B, B, -1, 1)[way], seq)
        return remote(place if src is None else src, place, w_slot(u, j, way), r.w_recv.at[u, j], device)

    ways = (a > 0, a < A - 1, b > 0, b < B - 1)

    def w_forward(u, j, along, src=None):
        for way in along:
            @pl.when(ways[way])
            def _():
                w_copy(u, j, way, src).start()

    def w_local(u):
        return pltpu.make_async_copy(whole_of(ins, u), rows_of(w, u, page), r.w_local.at[u])

    def w_first(*units, along=(0, 1, 2, 3)):
        for u in units:
            w_forward(u, page, along, whole_of(ins, u))
            if 2 in along:
                w_local(u).start()

    def w_turn(*units):
        for u in units:
            landed(rows_of(w, u, beside), r.w_recv.at[u, beside])
            w_forward(u, beside, (0, 1))

    def w_step(d, *units, on=True):
        for u in units:
            for sign, way in ((-1, 1), (1, 0)):
                @pl.when((a + sign * d >= 0) & (a + sign * d < A) & on)
                def _():
                    for column in (page, beside) if u in turned else (page,):
                        j = column + sign * d * B
                        landed(rows_of(w, u, j), r.w_recv.at[u, j])
                        w_forward(u, j, (way,) if u in turned else (way, 2, 3))

    def w_wait(*units):
        for u in units:
            w_local(u).wait()
            for e in range(1, 1 if u in turned else B):
                for t in range(A):
                    @pl.when(b - e >= 0)
                    def _():
                        j = t * B + b - e
                        landed(rows_of(w, u, j), r.w_recv.at[u, j])
                        w_forward(u, j, (3,))

                    @pl.when(b + e < B)
                    def _():
                        j = t * B + b + e
                        landed(rows_of(w, u, j), r.w_recv.at[u, j])
                        w_forward(u, j, (2,))

    def w_sent(u):
        for t in range(A):
            for e in range(B):
                j = t * B + e
                along = ((b == e) & (t >= a), (b == e) & (t <= a), e >= b, e <= b)
                if u in turned:
                    along = (t >= a, t <= a, (b == e) & (t == a), (b == e) & (t == a))
                for way, when in enumerate(along):
                    @pl.when(when & ways[way])
                    def _():
                        w_copy(u, j, way).wait_send()

    def block(array, g, e, n):
        rows, cols = ins[g].shape
        return array.at[rows_at(e * rows, rows), rows_at(n * cols, cols)]

    def m_local(g):
        return pltpu.make_async_copy(ins[g], block(w[g], g, shelf, seq), r.m_got.at[MOVED.index(g), seq])

    def m_collect_copy(g):
        i = MOVED.index(g)
        return remote(
            ins[g], block(w[g], g, shelf, seq), r.m_gave.at[i], r.m_got.at[i, seq], (page, collector)
        )

    def m_collect(g):
        @pl.when(collects)
        def _():
            m_local(g).start()

        @pl.when(jnp.logical_not(collects))
        def _():
            m_collect_copy(g).start()

    def m_copy(g, n, way):
        i = MOVED.index(g)
        place = block(w[g], g, mine, n)
        device = (page + B, page - B)[way] if way < 2 else a * B + lax.rem(b + way - 1, B)
        return remote(place, place, r.m_send.at[i, n, way], r.m_recv.at[i, mine, n], (device, seq))

    m_ways = [holds & (a >= a0) & (a < A - 1), holds & (a <= a0) & (a > 0)] + [holds] * (B - 1)

    def m_forward(g, n):
        for way in range(B + 1):
            @pl.when(m_ways[way])
            def _():
                m_copy(g, n, way).start()

    def m_first(g, n):
        @pl.when(collects)
        def _():
            @pl.when(seq == n)
            def _():
                m_local(g).wait()

            @pl.when(seq != n)
            def _():
                landed(block(w[g], g, shelf, n), r.m_got.at[MOVED.index(g), n])

            m_forward(g, n)

    hops = jnp.abs(a - a0)

    def m_pass(g, n, hop, where):
        @pl.when(holds & (hops == hop) & where)
        def _():
            landed(block(w[g], g, mine, n), r.m_recv.at[MOVED.index(g), mine, n])
            m_forward(g, n)

    def m_wait(g):
        for e in range(R):
            @pl.when(jnp.logical_not(holds) | (mine != e))
            def _():
                for n in range(S):
                    landed(block(w[g], g, e, n), r.m_recv.at[MOVED.index(g), e, n])

    def m_sent(g):
        @pl.when(jnp.logical_not(collects))
        def _():
            m_collect_copy(g).wait_send()

        for n in range(S):
            for way in range(B + 1):
                @pl.when(m_ways[way])
                def _():
                    m_copy(g, n, way).wait_send()

    low = 2 * a < A
    near = jnp.where(low, a, A - 1 - a)

    def order(m):
        if m == A - 1:
            return a
        t = jnp.where(m < A - 1 - near, A - 1 - m, m - (A - 1 - near))
        return jnp.where(low, t, A - 1 - t)

    def y_copy(u, k, t):
        other = lax.rem(b + k, B)
        return remote(
            rows_of(grad, u, t * B + other),
            r.rb[u].at[B - 1 - k, t],
            r.y_send.at[u, k - 1, t],
            r.y_recv.at[u, B - 1 - k, t],
            (a * B + other, seq),
        )

    def y_start(*units):
        for m in range(A):
            for u in units:
                for k in range(1, B):
                    y_copy(u, k, order(m)).start()

    def z_copy(u, t, sign):
        slot = jnp.where((t == a + sign) & (sign < 0), A, t)
        return remote(
            r.rb[u].at[0, t],
            r.zz[u].at[slot],
            r.z_send.at[u, t],
            r.z_recv.at[u, slot],
            (page + sign * B, seq),
        )

    def z_way(t):
        sign = jnp.where(t > a, 1, -1)
        before = a - sign
        return sign, (before >= 0) & (before < A)

    def y_sum(m, u):
        t = order(m)
        total = rows_of(grad, u, t * B + b)[...].astype(F32)
        for slot in range(B - 1):
            landed(r.rb[u].at[slot, t], r.y_recv.at[u, slot, t])
            total = total + r.rb[u][slot, t].astype(F32)
        r.rb[u][0, t] = total.astype(BF16)
        if m < A - 1:
            sign, has = z_way(t)

            @pl.when(jnp.logical_not(has))
            def _():
                z_copy(u, t, sign).start()

    def z_sum(m, u):
        t = order(m)
        sign, has = z_way(t)

        @pl.when(has)
        def _():
            landed(r.zz[u].at[t], r.z_recv.at[u, t])
            r.rb[u][0, t] = (r.rb[u][0, t].astype(F32) + r.zz[u][t].astype(F32)).astype(BF16)
            z_copy(u, t, sign).start()

    def z_total(u):
        @pl.when(a > 0)
        def _():
            landed(r.zz[u].at[a], r.z_recv.at[u, a])

        @pl.when(a < A - 1)
        def _():
            landed(r.zz[u].at[A], r.z_recv.at[u, A])

        total = r.rb[u][0, a].astype(F32)
        total = total + jnp.where(a > 0, r.zz[u][a].astype(F32), 0.0)
        total = total + jnp.where(a < A - 1, r.zz[u][A].astype(F32), 0.0)
        whole_of(outs, u)[...] = total

    def c_copy(u, t, sign, side, src):
        slot = jnp.where((t == a + sign) & (sign < 0), A, t)
        return remote(
            src,
            r.tz.at[side, slot],
            r.tz_send.at[side, t],
            r.tz_recv.at[side, slot],
            (page + sign * B, seq),
        )

    def c_own(u, t, side):
        return rows_of(grad, u, t * B + (b, 1 - b)[side])

    def c_first(u):
        for m in range(A - 1):
            t = order(m)
            sign, has = z_way(t)
            for side in range(2):
                @pl.when(jnp.logical_not(has))
                def _():
                    c_copy(u, t, sign, side, c_own(u, t, side)).start()

    def c_sum(m, u):
        t = order(m)
        sign, has = z_way(t)

        @pl.when(has)
        def _():
            for side in range(2):
                landed(r.tz.at[side, t], r.tz_recv.at[side, t])
                total = c_own(u, t, side)[...].astype(F32) + r.tz[side, t].astype(F32)
                r.ta[side, t] = total.astype(BF16)
                c_copy(u, t, sign, side, r.ta.at[side, t]).start()

    def c_turn(u):
        return remote(r.ta.at[1, a], r.tb, r.y_send.at[u, 0, 0], r.y_recv.at[u, 0, 0], (beside, seq))

    def c_total(u):
        for side in (1, 0):
            total = c_own(u, a, side)[...].astype(F32)
            for has, slot in ((a > 0, a), (a < A - 1, A)):
                @pl.when(has)
                def _():
                    landed(r.tz.at[side, slot], r.tz_recv.at[side, slot])

                total = total + jnp.where(has, r.tz[side, slot].astype(F32), 0.0)
            if side:
                r.ta[1, a] = total.astype(BF16)
                c_turn(u).start()
            else:
                whole_of(outs, u)[...] = total

    def c_end(u):
        landed(r.tb, r.y_recv.at[u, 0, 0])
        whole_of(outs, u)[...] = whole_of(outs, u)[...] + r.tb[...].astype(F32)

    def z_sent(u):
        if u in turned_back:
            c_turn(u).wait_send()
            for m in range(A - 1):
                t = order(m)
                for side in range(2):
                    c_copy(u, t, z_way(t)[0], side, c_own(u, t, side)).wait_send()
            return
        for t in range(A):
            for k in range(1, B):
                y_copy(u, k, t).wait_send()

            @pl.when(t != a)
            def _():
                z_copy(u, t, jnp.where(t > a, 1, -1)).wait_send()

    def f_parts(g):
        return max(QUARTERS // R, 1) if g == DOWN else 1

    def f_copy(g, k, n, part):
        i = MOVED.index(g)
        other = lax.rem(b + k, B)
        rows, cols = ins[g].shape
        size = rows // f_parts(g)
        return remote(
            grad[g].at[rows_at((other - b0) * rows + part * size, size), rows_at(n * cols, cols)],
            r.fb[i].at[B - 1 - k, n, part * size : (part + 1) * size, :],
            r.f_send[i].at[k - 1, n, part],
            r.f_recv[i].at[B - 1 - k, n, part],
            (a * B + other, seq),
        )

    def wanted(k):
        shelf_of = lax.rem(b + k, B) - b0
        return (shelf_of >= 0) & (shelf_of < R)

    def f_start(g, ready=lambda part: True):
        for n in range(S):
            for k in range(1, B):
                for part in range(f_parts(g)):
                    @pl.when(wanted(k) & ready((lax.rem(b + k, B) - b0) * f_parts(g) + part))
                    def _():
                        f_copy(g, k, n, part).start()

    inward = jnp.where(a > a0, -1, 1)
    from_out = holds & (a != a0) & inside
    starts_line = holds & (a != a0) & jnp.logical_not(inside)

    def v_copy(g, n):
        i = MOVED.index(g)
        slot = jnp.where((a + 1 == a0), 1, 0)
        return remote(
            r.fb[i].at[0, n], r.vv[i].at[slot, n], r.v_send.at[i, n], r.v_recv.at[i, slot, n], (page + inward * B, seq)
        )

    def s_copy(g, n):
        i = MOVED.index(g)
        return remote(r.fb[i].at[0, n], r.back[i], r.s_send.at[i, n], r.s_recv.at[i], (page, n))

    def f_sum(g, n):
        i = MOVED.index(g)

        @pl.when(holds)
        def _():
            total = block(grad[g], g, mine, n)[...].astype(F32)
            for slot in range(B - 1):
                for part in range(f_parts(g)):
                    f_copy(g, B - 1 - slot, n, part).wait_recv()
                total = total + r.fb[i][slot, n].astype(F32)
            r.fb[i][0, n] = total.astype(BF16)

            @pl.when(starts_line)
            def _():
                v_copy(g, n).start()

    passed = jnp.where(a > a0, A - 1 - a, a)

    def v_sum(g, n, hop):
        i = MOVED.index(g)

        @pl.when(from_out & (passed == hop))
        def _():
            landed(r.vv[i].at[0, n], r.v_recv.at[i, 0, n])
            r.fb[i][0, n] = (r.fb[i][0, n].astype(F32) + r.vv[i][0, n].astype(F32)).astype(BF16)
            v_copy(g, n).start()

    def v_total(g, n):
        i = MOVED.index(g)

        @pl.when(collects)
        def _():
            @pl.when(a < A - 1)
            def _():
                landed(r.vv[i].at[0, n], r.v_recv.at[i, 0, n])

            @pl.when(a > 0)
            def _():
                landed(r.vv[i].at[1, n], r.v_recv.at[i, 1, n])

            total = r.fb[i][0, n].astype(F32)
            total = total + jnp.where(a < A - 1, r.vv[i][0, n].astype(F32), 0.0)
            total = total + jnp.where(a > 0, r.vv[i][1, n].astype(F32), 0.0)

            @pl.when(seq == n)
            def _():
                outs[g][...] = total

            @pl.when(seq != n)
            def _():
                r.fb[i][0, n] = total.astype(BF16)
                s_copy(g, n).start()

    def s_wait(g):
        i = MOVED.index(g)

        @pl.when(jnp.logical_not(collects))
        def _():
            landed(r.back[i], r.s_recv.at[i])
            outs[g][...] = r.back[i][...].astype(F32)

    def v_sent(g):
        for n in range(S):
            for k in range(1, B):
                for part in range(f_parts(g)):
                    @pl.when(wanted(k))
                    def _():
                        f_copy(g, k, n, part).wait_send()

            @pl.when(starts_line | from_out)
            def _():
                v_copy(g, n).wait_send()

            @pl.when(collects & (seq != n))
            def _():
                s_copy(g, n).wait_send()

    token_live = r.token_counts[0]
    patch_live = r.patch_counts[0]
    r.norm_terms[6:8, :] = jnp.zeros((2, D), F32)
    gains = lambda k: r.small[0, k : k + 1, :]
    biases = lambda k: r.small[0, 3 + k : 4 + k, :]
    QB = min(256, T)
    lane = lax.broadcasted_iota(jnp.int32, (1, LANES), 1)
    halves = [(lane // HEAD_DIM == h) for h in range(2)]
    half_of = [half.astype(F32).astype(BF16) for half in halves]
    scale = HEAD_DIM ** (-0.5)

    def project(dst, left, weight):
        for n, (out, index) in enumerate(dst):
            out[...] = nn(left[...], weight[index]).astype(BF16)

    def attend(q, k, v, o, probs, live, causal):
        @pl.loop(0, Dl // LANES)
        def _(pair):
            cols = rows_at(pair * LANES, LANES)
            for block in range(T // QB):
                extent = (block + 1) * QB if causal else T
                rows = slice(block * QB, (block + 1) * QB)
                q2 = q[rows, cols]
                k2, v2 = k[:extent, cols], v[:extent, cols]
                at = lax.broadcasted_iota(jnp.int32, (QB, extent), 1)
                allowed = at < live
                if causal:
                    row = block * QB + lax.broadcasted_iota(jnp.int32, (QB, extent), 0)
                    allowed = allowed & (at <= row)
                found = []
                for h in range(2):
                    scores = nt(q2 * half_of[h], k2) * scale
                    scores = jnp.where(allowed, scores, -1e30)
                    raised = jnp.exp(scores - jnp.max(scores, axis=-1, keepdims=True))
                    share = (raised / jnp.sum(raised, axis=-1, keepdims=True)).astype(BF16)
                    probs[2 * pair + h, rows, :extent] = share
                    found.append(nn(share, v2))
                o[rows, cols] = jnp.where(halves[0], found[0], found[1]).astype(BF16)

    def attend_back(q, k, v, do, probs, dq, dk, dv, causal):
        @pl.loop(0, Dl // LANES)
        def _(pair):
            cols = rows_at(pair * LANES, LANES)
            r.dk_sum[...] = jnp.zeros_like(r.dk_sum)
            r.dv_sum[...] = jnp.zeros_like(r.dv_sum)
            for block in range(T // QB):
                extent = (block + 1) * QB if causal else T
                rows = slice(block * QB, (block + 1) * QB)
                q2, do2 = q[rows, cols], do[rows, cols]
                k2, v2 = k[:extent, cols], v[:extent, cols]
                dqs, dks, dvs = [], [], []
                for h in range(2):
                    share = probs[2 * pair + h, rows, :extent]
                    wide = share.astype(F32)
                    dp = nt(do2 * half_of[h], v2)
                    delta = jnp.sum(wide * dp, axis=-1, keepdims=True)
                    ds = (wide * (dp - delta)).astype(BF16)
                    dqs.append(nn(ds, k2))
                    dks.append(tn(ds, q2))
                    dvs.append(tn(share, do2))
                dq[rows, cols] = (jnp.where(halves[0], dqs[0], dqs[1]) * scale).astype(BF16)
                r.dk_sum[:extent, :] += jnp.where(halves[0], dks[0], dks[1])
                r.dv_sum[:extent, :] += jnp.where(halves[0], dvs[0], dvs[1])
            dk[:, cols] = (r.dk_sum[...] * scale).astype(BF16)
            dv[:, cols] = r.dv_sum[...].astype(BF16)

    def norm_back(k, values, incoming, ch):
        unit, rate = normed(values)
        for row, term in ((k, incoming * unit), (3 + k, incoming)):
            so_far = jnp.sum(term, axis=0, keepdims=True)
            r.norm_terms[row : row + 1, :] = so_far if ch == 0 else r.norm_terms[row : row + 1, :] + so_far
        dn = incoming * gains(k)
        return rate * (
            dn - jnp.mean(dn, axis=-1, keepdims=True) - unit * jnp.mean(dn * unit, axis=-1, keepdims=True)
        )

    def norm_own(k, values, dst, ch):
        dst[part_of(seq, ch), :] = (normed(values)[0] * gains(k) + biases(k)).astype(BF16)

    few = r.norm_gains.shape[1]
    at_feature = lax.broadcasted_iota(jnp.int32, (few, D), 1)
    placed = at_feature == lax.broadcasted_iota(jnp.int32, (few, D), 0) + (page * S + seq) * few
    plan = []
    SLOW = 5

    def when(time, *steps):
        plan.extend((time, step) for step in steps)

    def each_row_part(step):
        def run():
            for ch in range(2):
                step(ch, slice(ch * half, (ch + 1) * half))

        return run

    results = [
        (r.own_mixed, r.mixed),
        (r.own_input_grad, r.input_grad),
        (r.own_memory_grad, r.memory_grad),
        *((r.sums[g], r.outs[g]) for g in MOVED),
        *((whole_of(r.sums, u), whole_of(r.outs, u)) for u in range(len(UNITS))),
    ]
    O_MIXED, O_INPUT, O_MEMORY, O_MOVED, O_UNITS = 0, 1, 2, 3, 6

    def leave(n):
        kept, out = results[n]
        return pltpu.make_async_copy(kept, out, r.o_sem.at[n])

    def w_moved(g, first, hop_time, gap, end_first, end_gap):
        ends = jnp.logical_not(inside)
        for n in range(S):
            when(first + n * gap, lambda n=n: m_first(g, n))
            for hop in range(1, A):
                time = first + n * gap + hop * hop_time
                if hop < A - 1:
                    when(time, lambda n=n, hop=hop: m_pass(g, n, hop, inside))
                if hop > 1:
                    time = end_first + n * end_gap + hop / 10
                when(time, lambda n=n, hop=hop: m_pass(g, n, hop, ends))

    def g_moved(g, first, hop_time, gap, late, last):
        for n in range(S):
            time = first + n * gap
            when(time, lambda n=n: f_sum(g, n))
            for hop in range(1, A - 1):
                when(time + late + hop * hop_time + (hop - 1) * SLOW, lambda n=n, hop=hop: v_sum(g, n, hop))
            when(last, lambda n=n: v_total(g, n))

    def g_units(units, first, hop_time, gap, late):
        for place, u in enumerate(units):
            time = first + gap * place / len(units)
            for m in range(A):
                when(time + gap * m, lambda m=m, u=u: y_sum(m, u))
            for m in range(A - 2):
                when(time + gap * m + late + hop_time, lambda m=m, u=u: z_sum(m, u))
            after = time + late + 2 * hop_time + SLOW
            when(max(after, time + gap * (A - 2)), lambda u=u: z_sum(A - 2, u))
            when(188, lambda u=u: z_total(u), lambda u=u: leave(O_UNITS + u).start())

    given = (
        (G_TOKENS, r.tokens, r.all_tokens), (G_MEMORY, r.memory, r.all_memory), (G_COT, r.cotangent, r.dyr)
    )
    loads = [pltpu.make_async_copy(piece, everyone.at[own], r.ld_sem.at[i]) for i, piece, everyone in given]

    def begin():
        r.small[0] = jnp.zeros((8, D), F32)
        r.small[0, 0:3, :] = nn(r.norm_gains[...], placed.astype(F32).astype(BF16))
        r.small[0, 3:6, :] = nn(r.norm_biases[...], placed.astype(F32).astype(BF16))
        small_start(0, 0)
        w_first(*SELF_UNITS)
        w_first(*turned, along=(2, 3))
        m_collect(SELF_OUT)
        ag_begin(*given[0])
        for load in loads:
            load.start()

    def small_next(i, level):
        small_wait(i, level)
        small_start(i, level + 1 if i == 0 else level - 1)

    def take_tokens():
        small_wait(0, 2)
        ag_wait(G_TOKENS, r.all_tokens)
        for load in loads:
            load.wait()

        @pl.loop(0, S)
        def _(n):
            at = rows_at(n * Tl, Tl)
            values = r.all_tokens[at, :].astype(F32)
            r.a1[at, :] = (normed(values)[0] * gains(0) + biases(0)).astype(BF16)

    def self_project():
        w_wait(*SELF_UNITS)
        project(((r.q, 0), (r.k, 1), (r.v, 2)), r.a1, w[SELF])

    def self_sum():
        m_wait(SELF_OUT)
        rs_start(R_CHAIN, lambda at: nn(r.o[at, :], w[SELF_OUT][...]))

    @each_row_part
    def self_add(ch, rows):
        r.x1[rows, :] = r.all_tokens[part_of(seq, ch), :].astype(F32) + rs_wait(R_CHAIN, ch)
        norm_own(1, r.x1[rows, :], r.a2, ch)
        ag_start(G_A2, r.a2.at[own], r.a2, ch)

    def memory_project():
        w_wait(*CROSS_UNITS)
        ag_wait(G_MEMORY, r.all_memory)
        project(((r.kc, 1), (r.vc, 2)), r.all_memory, w[CROSS])

    def cross_project():
        ag_wait(G_A2, r.a2)
        project(((r.qc, 0),), r.a2, w[CROSS])

    def cross_sum():
        m_wait(CROSS_OUT)
        rs_sent(R_CHAIN)
        rs_start(R_CHAIN, lambda at: nn(r.oc[at, :], w[CROSS_OUT][...]))

    def take_cotangent():
        ag_wait(G_COT, r.dyr)
        ag_sent(*given[2])

        @pl.loop(0, S)
        def _(n):
            at = rows_at(n * Tl, Tl)
            row = n * Tl + lax.broadcasted_iota(jnp.int32, (Tl, 1), 0)
            values = r.dyr[at, :].astype(F32)
            r.dyr[at, :] = jnp.where(row < token_live, values, 0.0).astype(BF16)

    @each_row_part
    def cross_add(ch, rows):
        r.x2[rows, :] = r.x1[rows, :] + rs_wait(R_CHAIN, ch)
        norm_own(2, r.x2[rows, :], r.a3, ch)
        ag_start(G_A3, r.a3.at[own], r.a3, ch)

    def hidden_units(lo, hi):
        @pl.loop(lo, hi)
        def _(n):
            cols = rows_at(n * Fq, Fq)
            out, slope = gelu_pair(nn(r.a3[...], w[UP][:, cols]))
            r.g[:, cols] = out.astype(BF16)
            r.slope[:, cols] = slope

    def down_grad(lo, hi):
        @pl.loop(lo, hi)
        def _(n):
            cols = rows_at(n * Fq, Fq)
            grad[DOWN][cols, :] = tn(r.g[:, cols], r.dyr[...]).astype(BF16)

    def hidden_grad(lo, hi):
        @pl.loop(lo, hi)
        def _(n):
            cols = rows_at(n * Fq, Fq)
            r.du[:, cols] = (nt(r.dyr[...], w[DOWN][cols, :]) * r.slope[:, cols]).astype(BF16)

    def up_grad(lo, hi):
        if lo < hi:
            @pl.loop(0, D // 256)
            def _(n):
                cols = rows_at(n * 256, 256)
                grad[UP][cols, lo * Fq : hi * Fq] = tn(r.a3[:, cols], r.du[:, lo * Fq : hi * Fq]).astype(BF16)

    straight = tuple(u for u in UP_UNITS if u not in turned)
    ahead = UNITS[UP_UNITS[1]][1][0] if turned else QUARTERS
    back_from = BACK_UNITS[UP_UNITS[1]][1][0] if turned_back else QUARTERS

    def hidden():
        w_wait(*straight)
        ag_wait(G_A3, r.a3)
        hidden_units(0, ahead)
        down_grad(0, ahead)

    def hidden_rest():
        if turned:
            for d in range(1, A):
                w_step(d, *turned, on=jnp.logical_not(inside))
            w_wait(*turned)
            f_start(DOWN, lambda part: part < ahead)
            hidden_units(ahead, QUARTERS)
            down_grad(ahead, QUARTERS)
            f_start(DOWN, lambda part: part >= ahead)
        else:
            f_start(DOWN)

    when(0, begin)
    when(6, lambda: w_step(1, *SELF_UNITS))
    when(8, lambda: small_next(0, 0), lambda: m_collect(CROSS_OUT), lambda: ag_begin(*given[1]), lambda: m_collect(DOWN))
    when(12, lambda: w_step(2, *SELF_UNITS))
    w_moved(SELF_OUT, 13, 4, 0.1, 25, 0.1)
    when(15, lambda: small_next(0, 1), lambda: ag_forward(G_TOKENS, r.all_tokens), lambda: ag_begin(*given[2]))
    when(16.5, lambda: w_step(3, *SELF_UNITS))
    when(17.5, lambda: w_first(*CROSS_UNITS, along=(2, 3)))
    when(17.5, lambda: w_first(*CROSS_UNITS, along=(0, 1)))
    when(22, lambda: w_first(*straight))
    when(23.5, lambda: w_step(1, *CROSS_UNITS))
    when(24.5, take_tokens)
    when(27, self_project)
    when(29, lambda: w_step(2, *CROSS_UNITS))
    w_moved(CROSS_OUT, 30, 5, 0.1, 46, 0.1)
    when(31, lambda: ag_forward(G_MEMORY, r.all_memory))
    when(32, lambda: attend(r.q, r.k, r.v, r.o, r.p, token_live, True))
    when(34.5, lambda: w_step(3, *CROSS_UNITS))
    when(36, self_sum)
    when(37, lambda: w_step(1, *straight))
    w_moved(DOWN, 37.5, 7.5, 3, 60, 5)
    when(42, lambda: ag_forward(G_COT, r.dyr))
    when(43, lambda: w_step(2, *straight))
    when(46, self_add)
    when(51, lambda: w_first(*turned, along=(0, 1)))
    when(48, memory_project)
    when(49, lambda: w_step(3, *straight))
    when(50, lambda: w_turn(*turned))
    when(52, lambda: ag_forward(G_A2, r.a2))
    when(53.2, cross_project)
    when(54, lambda: attend(r.qc, r.kc, r.vc, r.oc, r.pc, patch_live, False))
    when(57, cross_sum)
    when(62, lambda: w_step(1, *turned, on=inside))
    when(61, take_cotangent)
    when(67, cross_add)
    when(69, lambda: w_step(2, *turned, on=inside))
    when(75, lambda: ag_forward(G_A3, r.a3))
    when(76, hidden)
    when(84, hidden_rest)

    def hidden_back():
        m_wait(DOWN)
        hidden_grad(back_from, QUARTERS)
        up_grad(back_from, QUARTERS)
        for u in turned_back:
            c_first(u)
        hidden_grad(0, back_from)
        ag_sent(G_A3, r.a3.at[own], r.a3)
        rs_sent(R_CHAIN)
        rs_start(R_CHAIN, lambda at: nt(r.du[at, :], w[UP][...]))

    def up_grad_rest():
        up_grad(0, back_from)
        y_start(*(u for u in UP_UNITS if u not in turned_back))

    @each_row_part
    def hidden_add(ch, rows):
        back_term = norm_back(2, r.x2[rows, :], rs_wait(R_CHAIN, ch), ch)
        r.dx2[rows, :] = r.dyr[part_of(seq, ch), :].astype(F32) + back_term
        r.dz2[part_of(seq, ch), :] = r.dx2[rows, :].astype(BF16)
        ag_start(G_DZ2, r.dz2.at[own], r.dz2, ch)

    def cross_back():
        ag_wait(G_DZ2, r.dz2)
        grad[CROSS_OUT][...] = tn(r.oc[...], r.dz2[...]).astype(BF16)
        f_start(CROSS_OUT)
        r.do[...] = nt(r.dz2[...], w[CROSS_OUT][...]).astype(BF16)
        attend_back(r.qc, r.kc, r.vc, r.do, r.pc, r.dq, r.dkc, r.dvc, False)

    def cross_back_sum():
        rs_sent(R_CHAIN)
        rs_start(R_CHAIN, lambda at: nt(r.dq[at, :], w[CROSS][0]))

    def cross_grad():
        for n, (left, right) in enumerate(((r.a2, r.dq), (r.all_memory, r.dkc), (r.all_memory, r.dvc))):
            grad[CROSS][n] = tn(left[...], right[...]).astype(BF16)
        y_start(*CROSS_UNITS)

    @each_row_part
    def cross_back_add(ch, rows):
        r.dx1[rows, :] = r.dx2[rows, :] + norm_back(1, r.x1[rows, :], rs_wait(R_CHAIN, ch), ch)
        r.dz1[part_of(seq, ch), :] = r.dx1[rows, :].astype(BF16)
        ag_start(G_DZ1, r.dz1.at[own], r.dz1, ch)

    def self_back():
        ag_wait(G_DZ1, r.dz1)
        grad[SELF_OUT][...] = tn(r.o[...], r.dz1[...]).astype(BF16)
        f_start(SELF_OUT)
        r.do[...] = nt(r.dz1[...], w[SELF_OUT][...]).astype(BF16)
        attend_back(r.q, r.k, r.v, r.do, r.p, r.dq, r.dk, r.dv, True)
        for n, right in enumerate((r.dq, r.dk, r.dv)):
            grad[SELF][n] = tn(r.a1[...], right[...]).astype(BF16)
        y_start(*SELF_UNITS)

    def self_back_sum():
        rs_sent(R_CHAIN)
        rs_start(
            R_CHAIN,
            lambda at: nt(r.dq[at, :], w[SELF][0]) + nt(r.dk[at, :], w[SELF][1]) + nt(r.dv[at, :], w[SELF][2]),
        )

    def memory_sum():
        ag_sent(G_A2, r.a2.at[own], r.a2)
        rs_start(R_MEMORY, lambda at: nt(r.dkc[at, :], w[CROSS][1]) + nt(r.dvc[at, :], w[CROSS][2]))

    @each_row_part
    def input_add(ch, rows):
        back_term = norm_back(0, r.all_tokens[part_of(seq, ch), :].astype(F32), rs_wait(R_CHAIN, ch), ch)
        r.own_input_grad[rows, :] = r.dx1[rows, :] + back_term

    def small_last():
        r.small[1] = r.norm_terms[...]
        small_start(1, 2)

    def mixed_sum():
        ag_sent(G_DZ2, r.dz2.at[own], r.dz2)
        rs_start(R_MIXED, lambda at: nn(r.g[at, :], w[DOWN][...]))

    @each_row_part
    def memory_add(ch, rows):
        r.own_memory_grad[rows, :] = rs_wait(R_MEMORY, ch)

    @each_row_part
    def mixed_add(ch, rows):
        live_row = (seq * Tl + ch * half + lax.broadcasted_iota(jnp.int32, (half, 1), 0)) < token_live
        r.own_mixed[rows, :] = jnp.where(live_row, r.x2[rows, :] + rs_wait(R_MIXED, ch), 0.0).astype(BF16)

    def norms_out():
        small_wait(1, 0)
        picked = lax.dot_general(
            r.small[1],
            placed.astype(F32),
            (((1,), (1,)), ((), ())),
            precision=lax.Precision.HIGHEST,
            preferred_element_type=F32,
        )
        r.gains_grad[...] = picked[0:3]
        r.biases_grad[...] = picked[3:6]

    when(87, hidden_back)
    when(95, up_grad_rest)
    if turned_back:
        when(99, lambda: c_sum(0, UP_UNITS[1]))
        when(102, lambda: c_sum(1, UP_UNITS[1]))
        when(105, lambda: c_sum(2, UP_UNITS[1]))
        when(112, lambda: c_total(UP_UNITS[1]))
        when(142, lambda: c_end(UP_UNITS[1]), lambda: leave(O_UNITS + UP_UNITS[1]).start())
        g_moved(DOWN, 98, 7.2, 5.6, 4, 155)
        g_units(UP_UNITS[:1], 122, 6, 4.2, 5)
    else:
        g_moved(DOWN, 97, 7.2, 5.6, 0, 155)
        g_units(UP_UNITS, 121, 4.5, 5.6, 0)
    when(103, hidden_add)
    when(109, lambda: ag_forward(G_DZ2, r.dz2))
    when(111, cross_back)
    when(117, cross_back_sum)
    when(119, cross_grad)
    when(126.5, cross_back_add)
    when(132.5, lambda: ag_forward(G_DZ1, r.dz1))
    when(134.5, self_back)
    when(140.5, self_back_sum)
    g_moved(CROSS_OUT, 138, 3.2, 1.4, 4, 172)
    when(145, memory_sum)
    g_units(CROSS_UNITS, 144, 6, 4.2, 4)
    when(149, input_add, lambda: leave(O_INPUT).start())
    when(150, small_last)
    when(153, mixed_sum)
    when(160, lambda: small_next(1, 2))
    when(179, memory_add, lambda: leave(O_MEMORY).start())
    g_moved(SELF_OUT, 159, 3.2, 1.4, 6, 184)
    when(177, lambda: small_next(1, 1))
    when(179, mixed_add, lambda: leave(O_MIXED).start())
    g_units(SELF_UNITS, 166, 6, 4.2, 0)
    for time, g in ((179, DOWN), (179, CROSS_OUT), (190, SELF_OUT)):
        when(time, lambda g=g: s_wait(g), lambda g=g: leave(O_MOVED + MOVED.index(g)).start())
    when(190, norms_out)

    for _, step in sorted(plan, key=lambda entry: entry[0]):
        step()

    for n in range(len(results)):
        leave(n).wait()
    for i in (R_CHAIN, R_MIXED, R_MEMORY):
        rs_sent(i)
    for i, piece, everyone in given[:2]:
        ag_sent(i, piece, everyone)
    ag_sent(G_DZ1, r.dz1.at[own], r.dz1)
    for u in range(len(UNITS)):
        w_sent(u)
        z_sent(u)
    for g in MOVED:
        m_sent(g)
        v_sent(g)


def layer_call(A, B, S, rows, weights, norms, counts):
    V = pltpu.VMEM
    Tl, D = rows[0].shape
    T = Tl * S
    Dl = weights[SELF].shape[2]
    Fl = weights[UP].shape[1]
    pages = A * B
    R = pages // S
    heads = Dl // HEAD_DIM
    shards = [x.shape for x in weights]
    full = []
    for g, s in enumerate(shards):
        if g in (SELF, CROSS):
            full.append((s[0], s[1] * pages, s[2]))
        elif g == UP:
            full.append((s[0] * pages, s[1]))
        else:
            full.append((s[0] * R, s[1] * S))
    hbm, vmem, smem = (pl.BlockSpec(memory_space=m) for m in (pl.ANY, V, pltpu.SMEM))
    shape = jax.ShapeDtypeStruct
    dma = pltpu.SemaphoreType.DMA
    small_slots = S + A + B - 3
    units = len(UNITS)
    pieces = [
        (shards[g][0], (n[1] - n[0]) * Fl // QUARTERS) if g == UP else shards[g] if n is None else shards[g][1:]
        for g, n in BACK_UNITS
    ]
    turn = pieces[-1]
    if B == 2:
        pieces[-1] = (16, LANES)
    else:
        turn = (16, LANES)
    row_ref, wide_ref = V((T, D), BF16), V((T, Dl), BF16)
    own_ref, hidden_ref = V((Tl, D), F32), V((T, Fl), BF16)
    operands = dict(
        tokens=rows[0],
        memory=rows[1],
        cotangent=rows[2],
        ins=list(weights),
        norm_gains=norms[0],
        norm_biases=norms[1],
        token_counts=counts[0],
        patch_counts=counts[1],
    )
    specs = dict(
        tokens=hbm, memory=hbm, cotangent=hbm, ins=[hbm] * 6, norm_gains=vmem, norm_biases=vmem, token_counts=smem, patch_counts=smem
    )
    results = dict(
        mixed=shape((Tl, D), BF16),
        input_grad=shape((Tl, D), F32),
        memory_grad=shape((Tl, D), F32),
        outs=[shape(s, F32) for s in shards],
        gains_grad=shape(norms[0].shape, F32),
        biases_grad=shape(norms[1].shape, F32),
    )
    scratch = dict(
        w=[V(s, BF16) for s in full],
        grad=[V(s, BF16) for s in full],
        rb=[V((B - 1, A, *piece), BF16) for piece in pieces],
        zz=[V((A + 1, *piece), BF16) for piece in pieces],
        ta=V((2, A, *turn), BF16),
        tz=V((2, A + 1, *turn), BF16),
        tb=V(turn, BF16),
        fb=[V((B - 1, S, *shards[g]), BF16) for g in MOVED],
        vv=[V((2, S, *shards[g]), BF16) for g in MOVED],
        back=[V(shards[g], BF16) for g in MOVED],
        all_tokens=row_ref,
        all_memory=row_ref,
        dyr=row_ref,
        a1=row_ref,
        a2=row_ref,
        a3=row_ref,
        dz2=row_ref,
        q=wide_ref,
        k=wide_ref,
        v=wide_ref,
        o=wide_ref,
        qc=wide_ref,
        kc=wide_ref,
        vc=wide_ref,
        oc=wide_ref,
        do=wide_ref,
        dq=wide_ref,
        dk=wide_ref,
        dv=wide_ref,
        dkc=wide_ref,
        dvc=wide_ref,
        p=V((heads, T, T), BF16),
        pc=V((heads, T, T), BF16),
        g=hidden_ref,
        du=hidden_ref,
        slope=V((T, Fl), F32),
        x1=own_ref,
        x2=own_ref,
        dx1=own_ref,
        dx2=own_ref,
        dk_sum=V((T, LANES), F32),
        dv_sum=V((T, LANES), F32),
        chain_part=row_ref,
        got=[V((S - 1, Tl, D), BF16)] * 3,
        own_mixed=V((Tl, D), BF16),
        own_input_grad=own_ref,
        own_memory_grad=own_ref,
        sums=[V(s, F32) for s in shards],
        small=V((2, 8, D), F32),
        small_got=V((2, small_slots, 8, D), F32),
        norm_terms=V((8, D), F32),
        ag_send=[dma((1 if i <= G_COT else 2, S - 1)) for i in range(7)],
        ag_recv=[dma((1 if i <= G_COT else 2, S)) for i in range(7)],
        rs_send=[dma((2 if i == R_CHAIN else 1, S - 1)) for i in range(3)],
        rs_recv=[dma((2 if i == R_CHAIN else 1, S - 1)) for i in range(3)],
        sm_send=dma((small_slots,)),
        sm_recv=dma((small_slots,)),
        ld_sem=dma((3,)),
        o_sem=dma((units + 6,)),
        w_send=dma((units * (A + 1 + (A if B == 2 else pages + A)) + A + 1,)),
        w_recv=dma((units, pages)),
        w_local=dma((units,)),
        y_send=dma((units, B - 1, A)),
        y_recv=dma((units, B - 1, A)),
        z_send=dma((units, A)),
        z_recv=dma((units, A + 1)),
        tz_send=dma((2, A)),
        tz_recv=dma((2, A + 1)),
        m_gave=dma((3,)),
        m_got=dma((3, S)),
        m_send=dma((3, S, B + 1)),
        m_recv=dma((3, R, S)),
        f_send=[dma((B - 1, S, max(QUARTERS // R, 1) if g == DOWN else 1)) for g in MOVED],
        f_recv=[dma((B - 1, S, max(QUARTERS // R, 1) if g == DOWN else 1)) for g in MOVED],
        v_send=dma((3, S)),
        v_recv=dma((3, 2, S)),
        s_send=dma((3, S)),
        s_recv=dma((3,)),
    )
    parts = [jax.tree.flatten(part) for part in (operands, specs, results, scratch)]
    values, in_specs, out_shape, scratch_shapes = (leaves for leaves, _ in parts)
    ends = [len(values), len(values) + len(out_shape)]

    def kernel(*refs):
        held = (refs[: ends[0]], refs[ends[0] : ends[1]], refs[ends[1] :])
        r = types.SimpleNamespace()
        for (_, tree), some in zip((parts[0], parts[2], parts[3]), held):
            vars(r).update(jax.tree.unflatten(tree, some))
        layer_kernel(A, B, S, r)

    found = pl.pallas_call(
        kernel,
        out_shape=out_shape,
        in_specs=in_specs,
        out_specs=[vmem if s.shape == norms[0].shape else hbm for s in out_shape],
        scratch_shapes=scratch_shapes,
        compiler_params=pltpu.CompilerParams(
            collective_id=0, has_side_effects=True, vmem_limit_bytes=62 * 2**20
        ),
        name="layer",
    )(*values)
    return jax.tree.unflatten(parts[2][1], found)


def keep_kernel(*refs):
    *arrays, sems = refs
    count = len(arrays) // 3
    given, kept, held = (arrays[n * count : (n + 1) * count] for n in range(3))
    loads = [pltpu.make_async_copy(given[n], held[n], sems.at[0, n]) for n in range(count)]
    stores = [pltpu.make_async_copy(held[n], kept[n], sems.at[1, n]) for n in range(count)]
    for load in loads:
        load.start()
    for load, store in zip(loads, stores):
        load.wait()
        store.start()
    for store in stores:
        store.wait()


def keep(*arrays):
    hbm = pl.BlockSpec(memory_space=pl.ANY)
    return pl.pallas_call(
        keep_kernel,
        out_shape=[jax.ShapeDtypeStruct(x.shape, x.dtype) for x in arrays],
        in_specs=[hbm] * len(arrays),
        out_specs=[hbm] * len(arrays),
        scratch_shapes=[pltpu.VMEM(x.shape, x.dtype) for x in arrays]
        + [pltpu.SemaphoreType.DMA((2, len(arrays)))],
        name="keep",
    )(*arrays)


def per_device(
    tokens,
    memory,
    cotangent,
    self_qkv,
    self_out,
    cross_qkv,
    cross_out,
    up_weight,
    down_weight,
    norm_gains,
    norm_biases,
    token_counts,
    patch_counts,
):
    pages = lax.axis_size("page")
    parts = lax.axis_size("seq")
    wide = 2 if pages == 8 else 8
    found = layer_call(
        pages // wide,
        wide,
        parts,
        (tokens[0], memory[0], cotangent[0]),
        (self_qkv, self_out, cross_qkv, cross_out, up_weight, down_weight),
        (norm_gains, norm_biases),
        (token_counts, patch_counts),
    )
    return keep(
        found["mixed"][None],
        found["input_grad"][None],
        found["memory_grad"][None],
        *found["outs"],
        found["gains_grad"],
        found["biases_grad"],
    )


def solution(mesh):
    rows = P("page", "seq", None)
    stack = P(None, "page", "seq")
    flat = P("page", "seq")
    norm = P(None, ("page", "seq"))
    counts = P("page")
    return jax.shard_map(
        per_device,
        mesh=mesh,
        in_specs=(rows, rows, rows, stack, flat, stack, flat, flat, flat, norm, norm, counts, counts),
        out_specs=(rows, rows, rows, stack, flat, stack, flat, flat, flat, norm, norm),
        check_vma=False,
    )
```
